32 devices in a mesh: dp: 8 (over z, y), expert: 4 (over x, core).
Axes of the slice: x: 2, y: 2, z: 4, core: 2. Of those that a mesh axis runs over, the one named last changes fastest.
Arguments:
- tokens: bfloat16 [3, 32, 197, 384], P(None, ('dp', 'expert')), may hold values from -6 to 6
- expert_index: int32 [3, 32, 197, 2], P(None, ('dp', 'expert')), may hold values from 0 to 3, as said below
- expert_slot: int32 [3, 32, 197, 2], P(None, ('dp', 'expert')), may hold values from 0 to 127, as said below
- route_kept: int32 [3, 32, 197, 2], P(None, ('dp', 'expert')), may hold values from 0 to 1, as said below
- ln1_gain: bfloat16 [384], P('dp'), may hold values from 0.5 to 1.5
- w_qkv: bfloat16 [384, 1152], P('dp'), may hold values from -0.3125 to 0.3125
- w_out: bfloat16 [384, 384], P('dp'), may hold values from -1.5 to 1.5
- ln2_gain: bfloat16 [384], P('dp'), may hold values from 0.5 to 1.5
- w_router: bfloat16 [384, 4], P('dp'), may hold values from -0.21875 to 0.21875
- expert_in: bfloat16 [4, 384, 1536], P('expert', 'dp'), may hold values from -0.3125 to 0.3125
- expert_bias: bfloat16 [4, 1536], P('expert', 'dp'), may hold values from -3 to 3
- expert_out: bfloat16 [4, 1536, 384], P('expert', 'dp'), may hold values from -3.5 to 3.5
- cotangent: bfloat16 [3, 32, 197, 384], P(None, ('dp', 'expert')), may hold values from -6 to 6
Outputs:
- output: bfloat16 [3, 32, 197, 384], P(None, ('dp', 'expert'))
- d_tokens: float32 [3, 32, 197, 384], P(None, ('dp', 'expert'))
- d_ln1_gain: float32 [384], P('dp')
- d_w_qkv: float32 [384, 1152], P('dp')
- d_w_out: float32 [384, 384], P('dp')
- d_ln2_gain: float32 [384], P('dp')
- d_w_router: float32 [384, 4], P('dp')
- d_expert_in: float32 [4, 384, 1536], P('expert', 'dp')
- d_expert_bias: float32 [4, 1536], P('expert', 'dp')
- d_expert_out: float32 [4, 1536, 384], P('expert', 'dp')
The draws below stay inside these ranges and needn't reach their ends.
Inputs may be any that keep to these rules, and one draw needn't show every extreme that they name: `expert_index`: each token names two different experts. `expert_slot`: in each micro-batch and each aligned block of 1 images, the kept routes to one expert take the slots 0, 1, 2 and so on in token order, a token's first expert before its second, without gaps or repeats; a dropped route has slot 0. In every micro-batch one expert has all 128 slots taken in every block. `route_kept`: in each micro-batch and each aligned block of 1 images, a route is kept exactly when fewer than 128 earlier routes of the block, in that order, go to the same expert; every block drops some routes.
All inputs are finite; a program needn't handle non-finite values.
Results may differ from the reference program's by a relative error of at most 0.024.
Values may be sent and summed in bfloat16 or wider, within the bound.
No kernel may reach another device: no remote copies, remote signals or barrier semaphores. Data moves between devices by JAX's collectives and lax.ppermute only.
A program may use at most 128 MiB of HBM per device.

```python
import jax
import jax.numpy as jnp
from jax import lax

HEADS = 6
HEAD_DIM = 64
D = 384
FF = 1536
SEQ = 197
IMG_DEV = 1
MB = 3
EXPERTS = 4
IMAGES = 32
CAP = 128


def routing_table(key):
    block_count = IMAGES // IMG_DEV
    token_rows = IMG_DEV * SEQ
    subkeys = jax.random.split(key, 5)
    orders = jax.vmap(lambda single: jax.random.permutation(single, EXPERTS))(jax.random.split(subkeys[0], MB))
    shape = (MB, block_count, token_rows)
    skewed = jnp.minimum(jax.random.randint(subkeys[1], shape, 0, EXPERTS), jax.random.randint(subkeys[2], shape, 0, EXPERTS))
    first = jax.vmap(lambda order, choose: order[choose])(orders, skewed)
    forced = jax.random.randint(subkeys[3], (MB,), 0, EXPERTS)
    position = jnp.arange(token_rows, dtype=jnp.int32)
    first = jnp.where(position[None, None, :] < CAP + 2, forced[:, None, None], first)
    second = (first + jax.random.randint(subkeys[4], shape, 1, EXPERTS)) % EXPERTS
    routes = jnp.stack([first, second], axis=-1).reshape(MB, block_count, 2 * token_rows)
    one_hot = (routes[..., None] == jnp.arange(EXPERTS, dtype=jnp.int32)).astype(jnp.int32)
    before = jnp.cumsum(one_hot, axis=2) - one_hot
    rank = jnp.sum(before * one_hot, axis=-1)
    kept = (rank < CAP).astype(jnp.int32)
    slot = jnp.where(kept > 0, rank, 0).astype(jnp.int32)
    final_shape = (MB, IMAGES, SEQ, 2)
    return (routes.reshape(final_shape).astype(jnp.int32), slot.reshape(final_shape), kept.reshape(final_shape))


def draw_expert_index(key, part):
    return routing_table(key)[0]


def draw_expert_slot(key, part):
    return routing_table(key)[1]


def draw_route_kept(key, part):
    return routing_table(key)[2]


def steps_of(key, extent, cuts, low, high):
    def one(axis_at, blocks):
        heights = jax.random.uniform(jax.random.fold_in(jax.random.fold_in(key, 6), axis_at), (blocks,), jnp.float32, low / len(cuts), high / len(cuts))
        return jnp.repeat(jnp.exp(heights), extent[axis_at] // blocks).reshape((-1,) + (1,) * (len(extent) - axis_at - 1))

    factor_of = one(*cuts[0])
    for cut in cuts[1:]:
        factor_of = factor_of * one(*cut)
    return factor_of


def scatter_about(stream_key, shape, scale, most, pieces=(), kind=jnp.bfloat16):
    loudness = steps_of(stream_key, shape, pieces, -0.22, 0.18) if pieces else 1.0
    array = jax.random.normal(stream_key, shape, jnp.float32) * scale * loudness
    return jnp.minimum(jnp.maximum(array, -most), most).astype(kind)


def setup_inputs(seed: int = 0) -> dict:
    seeds = jax.random.split(jax.random.key(seed), 14)
    return {
        "tokens": scatter_about(seeds[0], (MB, IMAGES, SEQ, D), 1.0, 6.0, ((1, 32),)),
        "expert_index": draw_expert_index(jax.random.fold_in(seeds[13], 71), 0),
        "expert_slot": draw_expert_slot(jax.random.fold_in(seeds[13], 71), 0),
        "route_kept": draw_route_kept(jax.random.fold_in(seeds[13], 71), 0),
        "ln1_gain": jnp.clip(1.0 + 0.1 * jax.random.normal(seeds[4], (D,), jnp.float32), 0.5, 1.5).astype(jnp.bfloat16),
        "w_qkv": scatter_about(seeds[5], (D, 3 * D), D ** -0.5, 0.3125, ((0, 8),)),
        "w_out": scatter_about(seeds[6], (D, D), (max(D // 25, 1)) ** -0.5, 1.5, ((0, 8),)),
        "ln2_gain": jnp.clip(1.0 + 0.1 * jax.random.normal(seeds[7], (D,), jnp.float32), 0.5, 1.5).astype(jnp.bfloat16),
        "w_router": scatter_about(seeds[8], (D, EXPERTS), (2 * D) ** -0.5, 0.21875, ((0, 8),)),
        "expert_in": scatter_about(seeds[9], (EXPERTS, D, FF), D ** -0.5, 0.3125, ((0, 4), (1, 8))),
        "expert_bias": scatter_about(seeds[10], (EXPERTS, FF), 0.5, 3.0, ((0, 4), (1, 8))),
        "expert_out": scatter_about(seeds[11], (EXPERTS, FF, D), (max(FF // 512, 1)) ** -0.5, 3.5, ((0, 4), (1, 8))),
        "cotangent": scatter_about(seeds[12], (MB, IMAGES, SEQ, D), 1.0, 6.0, ((1, 32),)),
    }


@jax.custom_vjp
def low(v):
    return lax.optimization_barrier(v.astype(jnp.bfloat16)).astype(jnp.float32)

@jax.custom_vjp
def low_back(v):
    return v

def low_keep(v):
    return (low(v), None)

def low_pass(kept, grad):
    return (grad,)

def back_keep(v):
    return (v, None)

def back_low(kept, grad):
    return (low(grad),)
low.defvjp(low_keep, low_pass)
low_back.defvjp(back_keep, back_low)
EPSILON = 1e-06

def layer_norm(values, gain):
    centre = lax.optimization_barrier(jnp.mean(values, axis=-1, keepdims=True))
    centered = values - centre
    spread = lax.optimization_barrier(jnp.mean(centered * centered, axis=-1, keepdims=True))
    return centered * lax.rsqrt(spread + EPSILON) * gain

def block_forward(inputs, route_expert, route_slot, route_live, gain_one, packed_w, out_w, gain_two, router_w, first_w, first_bias, second_w):
    token_rows = IMG_DEV * SEQ
    scale = HEAD_DIM ** (-0.5)
    highest = lax.Precision.HIGHEST
    normed = layer_norm(inputs, gain_one)
    packed = low(low_back(jnp.dot(low(normed), packed_w, precision=highest)))
    head_split = packed.reshape(IMG_DEV, SEQ, 3, HEADS, HEAD_DIM)
    query = head_split[:, :, 0]
    keyed = head_split[:, :, 1]
    valued = head_split[:, :, 2]
    scores = low_back(jnp.einsum('iqhd,ikhd->ihqk', query, keyed, precision=highest) * scale)
    attn = jax.nn.softmax(scores, axis=-1)
    attended = jnp.einsum('ihqk,ikhd->iqhd', low(attn), valued, precision=highest).reshape(token_rows, D)
    attended = low(low_back(attended))
    middle = inputs + low_back(jnp.dot(attended, out_w, precision=highest))
    normed_two = layer_norm(middle, gain_two)
    router = jax.nn.softmax(jnp.dot(normed_two, router_w, precision=highest), axis=-1)
    live_float = route_live.astype(jnp.float32)
    one_hot = (route_expert[:, :, None] == jnp.arange(EXPERTS, dtype=jnp.int32)[None, None, :]).astype(jnp.float32)
    gates = lax.optimization_barrier(jnp.sum(one_hot * router[:, None, :], axis=-1)) * live_float
    route_target = (route_expert * CAP + route_slot).reshape(-1).astype(jnp.int32)
    routed = jnp.repeat(low(normed_two), 2, axis=0) * live_float.reshape(-1, 1)
    inbox = jnp.zeros((EXPERTS * CAP, D), jnp.float32).at[route_target].add(routed)
    inbox = low_back(inbox).reshape(EXPERTS, CAP, D)
    hidden = jnp.einsum('ecd,edf->ecf', inbox, first_w, precision=highest) + first_bias[:, None, :]
    hidden = low_back(hidden)
    active = low(jax.nn.gelu(hidden, approximate=False))
    outbox = jnp.einsum('ecf,efd->ecd', active, second_w, precision=highest)
    outbox = low(low_back(outbox)).reshape(EXPERTS * CAP, D)
    picked = outbox[route_target].reshape(token_rows, 2, D)
    return middle + lax.optimization_barrier(jnp.sum(gates[:, :, None] * picked, axis=1))

def reference(tokens, expert_index, expert_slot, route_kept, ln1_gain, w_qkv, w_out, ln2_gain, w_router, expert_in, expert_bias, expert_out, cotangent):
    block_count = MB * (IMAGES // IMG_DEV)
    token_rows = IMG_DEV * SEQ
    route_expert = expert_index.reshape(block_count, token_rows, 2)
    route_slot = expert_slot.reshape(block_count, token_rows, 2)
    route_live = route_kept.reshape(block_count, token_rows, 2)

    def forward(inputs, gain_one, packed_w, out_w, gain_two, router_w, first_w, first_bias, second_w):

        def block_step(block_item):
            return block_forward(block_item[0], block_item[1], block_item[2], block_item[3], gain_one, packed_w, out_w, gain_two, router_w, first_w, first_bias, second_w)
        mapped = lax.map(jax.checkpoint(block_step), (inputs.reshape(block_count, token_rows, D), route_expert, route_slot, route_live))
        return mapped.reshape(MB, IMAGES, SEQ, D)
    output, pullback = jax.vjp(forward, tokens.astype(jnp.float32), ln1_gain.astype(jnp.float32), w_qkv.astype(jnp.float32), w_out.astype(jnp.float32), ln2_gain.astype(jnp.float32), w_router.astype(jnp.float32), expert_in.astype(jnp.float32), expert_bias.astype(jnp.float32), expert_out.astype(jnp.float32))
    grads = pullback(cotangent.astype(jnp.float32))
    return (output.astype(jnp.bfloat16), grads[0], grads[1], grads[2], grads[3], grads[4], grads[5], grads[6], grads[7], grads[8])
```

```python
import functools

import jax
import jax.numpy as jnp
from jax import lax
from jax.experimental import pallas as pl
from jax.experimental.pallas import tpu as pltpu
from jax.sharding import PartitionSpec as P

HEADS = 6
HEAD_DIM = 64
D = 384
SEQ = 197
MB = 3
LANES = 128
EPSILON = 1e-06
HIGHEST = lax.Precision.HIGHEST
VMEM_BYTES = 48 * 1024 * 1024
bf16 = jnp.bfloat16
f32 = jnp.float32


def dot(a, b, ca=1, cb=0, precision=None):
    return lax.dot_general(
        a, b, (((ca,), (cb,)), ((), ())), precision=precision, preferred_element_type=f32
    )


def xor_pairs(n, k):
    return [(i, i ^ k) for i in range(n)]


def spread_of(values):
    centre = jnp.mean(values, axis=-1, keepdims=True)
    centered = values - centre
    spread = jnp.mean(centered * centered, axis=-1, keepdims=True)
    rate = lax.rsqrt(spread + EPSILON)
    return centered * rate, rate


def norm_back(grad_hat, hat, rate):
    mean_one = jnp.mean(grad_hat, axis=-1, keepdims=True)
    mean_two = jnp.mean(grad_hat * hat, axis=-1, keepdims=True)
    return rate * (grad_hat - mean_one - hat * mean_two)


def side_rows(dense_ref):
    return jnp.transpose(dense_ref[:, 4 * D :].astype(f32))


def route_masks(index_ref, slot_ref, kept_ref, me, groups, capacity):
    index = index_ref[0, 0]
    target = jnp.where(kept_ref[0, 0] > 0, (index ^ me) * capacity + slot_ref[0, 0], -1)
    lanes = lax.broadcasted_iota(jnp.int32, (SEQ, groups * capacity), 1)
    places = [(lanes == target[:, k : k + 1]).astype(f32).astype(bf16) for k in range(2)]
    experts = lax.broadcasted_iota(jnp.int32, (SEQ, groups), 1)
    chosen = [(experts == index[:, k : k + 1]).astype(f32) for k in range(2)]
    return places, chosen


def half_mask(which):
    lanes = lax.broadcasted_iota(jnp.int32, (SEQ, LANES), 1)
    return (lanes < HEAD_DIM) if which == 0 else (lanes >= HEAD_DIM)


def forward_kernel(groups, capacity, me_ref, tokens_ref, index_ref, slot_ref, kept_ref, cot_ref, dense_ref, packed_ref, attn_ref, attended_ref, middle_ref, router_ref, *sends):
    me = me_ref[0]
    side = side_rows(dense_ref)
    gain_one = side[groups : groups + 1]
    gain_two = side[groups + 1 : groups + 2]
    inputs = tokens_ref[0, 0].astype(f32)
    hat, _ = spread_of(inputs)
    normed_low = (hat * gain_one).astype(bf16)
    packed = dot(normed_low, dense_ref[:, : 3 * D]).astype(bf16)
    packed_ref[...] = packed
    scale = HEAD_DIM ** (-0.5)
    parts = []
    for pair in range(HEADS // 2):
        lo = pair * LANES
        query = packed[:, lo : lo + LANES]
        keyed = packed[:, D + lo : D + lo + LANES]
        valued = packed[:, 2 * D + lo : 2 * D + lo + LANES]
        outs = []
        for which in range(2):
            masked = jnp.where(half_mask(which), query, jnp.zeros_like(query))
            scores = dot(masked, keyed, 1, 1) * scale
            top = jnp.max(scores, axis=-1, keepdims=True)
            raised = jnp.exp(scores - top)
            total = jnp.sum(raised, axis=-1, keepdims=True)
            attn_low = (raised * (1.0 / total)).astype(bf16)
            attn_ref[2 * pair + which] = attn_low
            outs.append(dot(attn_low, valued))
        parts.append(jnp.where(half_mask(0), outs[0], outs[1]))
    attended = jnp.concatenate(parts, axis=1).astype(bf16)
    attended_ref[...] = attended
    middle = inputs + dot(attended, dense_ref[:, 3 * D : 4 * D])
    middle_ref[...] = middle
    hat_two, _ = spread_of(middle)
    normed_two = hat_two * gain_two
    router_w = dense_ref[:, 4 * D :].astype(f32)[:, :groups]
    logits = dot(normed_two, router_w, precision=HIGHEST)
    raised = jnp.exp(logits - jnp.max(logits, axis=-1, keepdims=True))
    router = raised / jnp.sum(raised, axis=-1, keepdims=True)
    router_ref[...] = router
    places, chosen = route_masks(index_ref, slot_ref, kept_ref, me, groups, capacity)
    cot = cot_ref[0, 0].astype(f32)
    inbox = dot(places[0] + places[1], normed_two.astype(bf16), 0, 0).astype(bf16)
    grad_outbox = jnp.zeros((groups * capacity, D), f32)
    for k in range(2):
        gate = jnp.sum(chosen[k] * router, axis=-1, keepdims=True)
        grad_outbox += dot(places[k], (gate * cot).astype(bf16), 0, 0)
    grad_outbox = grad_outbox.astype(bf16)
    for g in range(groups):
        sends[g][:capacity] = inbox[g * capacity : (g + 1) * capacity]
        sends[g][capacity:] = grad_outbox[g * capacity : (g + 1) * capacity]


def expert_kernel(groups, capacity, *refs):
    boxes = refs[:groups]
    first_ref, bias_ref, second_ref = refs[groups : groups + 3]
    backs = refs[groups + 3 : 2 * groups + 3]
    active_ref, grad_hidden_ref = refs[2 * groups + 3 :]
    inbox = jnp.concatenate([box[:capacity] for box in boxes], axis=0)
    grad_outbox = jnp.concatenate([box[capacity:] for box in boxes], axis=0)
    wide = first_ref.shape[1]
    step = wide // 3
    outbox = jnp.zeros((groups * capacity, D), f32)
    grad_inbox = jnp.zeros((groups * capacity, D), f32)
    for at in range(0, wide, step):
        first = first_ref[:, at : at + step]
        second = second_ref[at : at + step, :]
        hidden = dot(inbox, first) + bias_ref[:, at : at + step].astype(f32)
        cdf = 0.5 + 0.5 * lax.erf(hidden * (0.5**0.5))
        density = jnp.exp(hidden * hidden * (-0.5)) * 0.3989422804014327
        active = (hidden * cdf).astype(bf16)
        grad_active = dot(grad_outbox, second, 1, 1)
        grad_hidden = ((cdf + hidden * density) * grad_active).astype(bf16)
        active_ref[:, at : at + step] = active
        grad_hidden_ref[:, at : at + step] = grad_hidden
        outbox += dot(active, second)
        grad_inbox += dot(grad_hidden, first, 1, 1)
    outbox = outbox.astype(bf16)
    grad_inbox = grad_inbox.astype(bf16)
    for g in range(groups):
        backs[g][:capacity] = outbox[g * capacity : (g + 1) * capacity]
        backs[g][capacity:] = grad_inbox[g * capacity : (g + 1) * capacity]


def second_grad_kernel(groups, capacity, owners, *refs):
    boxes = [refs[m * groups : (m + 1) * groups] for m in range(MB)]
    actives = refs[MB * groups : MB * groups + MB]
    out_ref = refs[-1]
    rows = out_ref.shape[1]
    grads = [
        jnp.concatenate([box[capacity:] for box in boxes[m]], axis=0) for m in range(MB)
    ]
    wide = owners * rows
    step = wide // 3 if (wide // 3) % rows == 0 else wide // 2
    for at in range(0, wide, step):
        total = dot(actives[0][:, at : at + step], grads[0], 0, 0)
        for m in range(1, MB):
            total += dot(actives[m][:, at : at + step], grads[m], 0, 0)
        total = total.astype(bf16)
        for j in range(step // rows):
            out_ref[at // rows + j] = total[j * rows : (j + 1) * rows]


def first_grad_kernel(groups, capacity, owners, *refs):
    boxes = [refs[m * groups : (m + 1) * groups] for m in range(MB)]
    hiddens = refs[MB * groups : MB * groups + MB]
    out_ref = refs[-1]
    rows = D // owners
    extra = out_ref.shape[1] - rows
    inboxes = [
        jnp.concatenate([box[:capacity] for box in boxes[m]], axis=0) for m in range(MB)
    ]
    wide = out_ref.shape[2]
    step = wide // 3
    for at in range(0, wide, step):
        total = dot(inboxes[0], hiddens[0][:, at : at + step], 0, 0)
        bias = jnp.sum(hiddens[0][:, at : at + step].astype(f32), axis=0, keepdims=True)
        for m in range(1, MB):
            total += dot(inboxes[m], hiddens[m][:, at : at + step], 0, 0)
            bias += jnp.sum(hiddens[m][:, at : at + step].astype(f32), axis=0, keepdims=True)
        total = total.astype(bf16)
        bias = jnp.broadcast_to(bias, (extra, step)).astype(bf16)
        for j in range(owners):
            out_ref[j, :rows, at : at + step] = total[j * rows : (j + 1) * rows]
            out_ref[j, rows:, at : at + step] = bias


def backward_kernel(groups, capacity, has_total, me_ref, tokens_ref, index_ref, slot_ref, kept_ref, cot_ref, dense_ref, packed_ref, attn_ref, attended_ref, middle_ref, router_ref, *refs):
    backs = refs[:groups]
    total_ref = refs[groups] if has_total else None
    output_ref, d_tokens_ref, grads_ref = refs[-3:]
    me = me_ref[0]
    side = side_rows(dense_ref)
    gain_one = side[groups : groups + 1]
    gain_two = side[groups + 1 : groups + 2]
    middle = middle_ref[...]
    router = router_ref[...]
    cot = cot_ref[0, 0].astype(f32)
    places, chosen = route_masks(index_ref, slot_ref, kept_ref, me, groups, capacity)
    outbox = jnp.concatenate([box[:capacity] for box in backs], axis=0)
    grad_inbox = jnp.concatenate([box[capacity:] for box in backs], axis=0)
    mixed = middle
    grad_router = jnp.zeros((SEQ, groups), f32)
    for k in range(2):
        picked = dot(places[k], outbox)
        gate = jnp.sum(chosen[k] * router, axis=-1, keepdims=True)
        mixed = mixed + gate * picked
        grad_router += chosen[k] * jnp.sum(cot * picked, axis=-1, keepdims=True)
    output_ref[0] = mixed.astype(bf16)
    grad_logits = router * (grad_router - jnp.sum(router * grad_router, axis=-1, keepdims=True))
    router_w = dense_ref[:, 4 * D :].astype(f32)[:, :groups]
    grad_normed_two = dot(grad_logits, router_w, 1, 1, precision=HIGHEST) + dot(
        places[0] + places[1], grad_inbox
    )
    hat_two, rate_two = spread_of(middle)
    grad_middle = norm_back(grad_normed_two * gain_two, hat_two, rate_two) + cot
    lanes = lax.broadcasted_iota(jnp.int32, (SEQ, LANES), 1)
    column_one = (lanes == groups).astype(f32)
    column_two = (lanes == groups + 1).astype(f32)
    logits_wide = sum(
        jnp.where(lanes == e, grad_logits[:, e : e + 1], 0.0) for e in range(groups)
    )
    side_grad = dot(hat_two * gain_two, logits_wide, 0, 0, precision=HIGHEST)
    side_grad += dot(grad_normed_two * hat_two, column_two, 0, 0, precision=HIGHEST)
    grad_branch = grad_middle.astype(bf16)
    out_grad = dot(attended_ref[...], grad_branch, 0, 0)
    grad_attended = dot(grad_branch, dense_ref[:, 3 * D : 4 * D], 1, 1).astype(bf16)
    scale = HEAD_DIM ** (-0.5)
    first_half = half_mask(0)
    queries, keys, values = [], [], []
    for pair in range(HEADS // 2):
        lo = pair * LANES
        query = packed_ref[:, lo : lo + LANES]
        keyed = packed_ref[:, D + lo : D + lo + LANES]
        valued = packed_ref[:, 2 * D + lo : 2 * D + lo + LANES]
        pulled = grad_attended[:, lo : lo + LANES]
        q_outs, k_outs, v_outs = [], [], []
        for which in range(2):
            attn_low = attn_ref[2 * pair + which]
            attn = attn_low.astype(f32)
            masked = jnp.where(half_mask(which), pulled, jnp.zeros_like(pulled))
            weighted = dot(masked, valued, 1, 1)
            inner = jnp.sum(attn * weighted, axis=-1, keepdims=True)
            grad_scores = (attn * (weighted - inner)).astype(bf16)
            v_outs.append(dot(attn_low, pulled, 0, 0))
            q_outs.append(dot(grad_scores, keyed))
            k_outs.append(dot(grad_scores, query, 0, 0))
        queries.append(jnp.where(first_half, q_outs[0], q_outs[1]) * scale)
        keys.append(jnp.where(first_half, k_outs[0], k_outs[1]) * scale)
        values.append(jnp.where(first_half, v_outs[0], v_outs[1]))
    grad_packed = jnp.concatenate(queries + keys + values, axis=1).astype(bf16)
    grad_normed = dot(grad_packed, dense_ref[:, : 3 * D], 1, 1)
    hat, rate = spread_of(tokens_ref[0, 0].astype(f32))
    packed_grad = dot((hat * gain_one).astype(bf16), grad_packed, 0, 0)
    side_grad += dot(grad_normed * hat, column_one, 0, 0, precision=HIGHEST)
    d_tokens_ref[0] = grad_middle + norm_back(grad_normed * gain_one, hat, rate)
    for lo, part in ((0, packed_grad), (3 * D, out_grad), (4 * D, side_grad)):
        hi = lo + part.shape[1]
        if has_total:
            part = part + total_ref[:, lo:hi]
        grads_ref[:, lo:hi] = part


def arrange_kernel(count, me_ref, *refs):
    out_ref = refs[-1]
    for k in range(count):
        out_ref[me_ref[0] ^ k] = refs[k][...]


def params():
    return pltpu.CompilerParams(vmem_limit_bytes=VMEM_BYTES)


def whole(shape):
    zeros = (0,) * len(shape)
    return pl.BlockSpec(tuple(shape), lambda i: zeros)


def of_batch(shape, batch):
    tail = (0,) * (len(shape) - 1)
    return pl.BlockSpec((1,) + tuple(shape[1:]), lambda i: (batch,) + tail)


SCALAR = pl.BlockSpec(memory_space=pltpu.SMEM)


def call(kernel, name, in_specs, outs, args, flops, grid=(1,)):
    moved = sum(a.size * a.dtype.itemsize for a in args)
    moved += sum(a.size * a.dtype.itemsize for a in outs)
    return pl.pallas_call(
        kernel,
        grid=grid,
        in_specs=in_specs,
        out_specs=[whole(o.shape) for o in outs],
        out_shape=outs,
        compiler_params=params(),
        cost_estimate=pl.CostEstimate(flops=flops, bytes_accessed=moved, transcendentals=0),
        name=name,
    )(*args)


def like(shape, dtype):
    return jax.ShapeDtypeStruct(tuple(shape), dtype)


def gather_rows(piece, axis, me):
    count = lax.axis_size(axis)
    pieces = [piece] + [
        lax.ppermute(piece, axis, xor_pairs(count, k)) for k in range(1, count)
    ]
    out = call(
        functools.partial(arrange_kernel, count),
        "arrange",
        [SCALAR] + [whole(piece.shape)] * count,
        [like((count,) + piece.shape, piece.dtype)],
        [me] + pieces,
        0,
    )[0]
    return out.reshape((count * piece.shape[0],) + piece.shape[1:])


def scatter_sum(parts, axis, me):
    count = lax.axis_size(axis)
    total = lax.dynamic_index_in_dim(parts, me, 0, keepdims=False).astype(f32)
    for k in range(1, count):
        sent = lax.dynamic_index_in_dim(parts, me ^ k, 0, keepdims=False)
        total += lax.ppermute(sent, axis, xor_pairs(count, k)).astype(f32)
    return total


def body(
    tokens,
    expert_index,
    expert_slot,
    route_kept,
    ln1_gain,
    w_qkv,
    w_out,
    ln2_gain,
    w_router,
    expert_in,
    expert_bias,
    expert_out,
    cotangent,
):
    groups = lax.axis_size("expert")
    owners = lax.axis_size("dp")
    capacity = 8 * (5 * SEQ // (16 * groups) + 1)
    slots = groups * capacity
    wide = expert_in.shape[2]
    me_expert = lax.axis_index("expert")
    me_owner = lax.axis_index("dp")
    me_e = me_expert.reshape(1).astype(jnp.int32)
    me_o = me_owner.reshape(1).astype(jnp.int32)
    side_width = LANES
    rows = w_qkv.shape[0]
    side = jnp.concatenate(
        [
            w_router,
            ln1_gain[:, None],
            ln2_gain[:, None],
            jnp.zeros((rows, side_width - groups - 2), bf16),
        ],
        axis=1,
    )
    dense = gather_rows(jnp.concatenate([w_qkv, w_out, side], axis=1), "dp", me_o)
    first = gather_rows(expert_in[0], "dp", me_o)
    second = gather_rows(expert_out[0], "dp", me_o)
    bias = lax.all_gather(expert_bias, "dp", axis=1, tiled=True)

    routes = [expert_index, expert_slot, route_kept]
    dense_width = dense.shape[1]
    state = []
    boxes = []
    for m in range(MB):
        shared = [tokens] + routes + [cotangent]
        shared_specs = [of_batch(a.shape, m) for a in shared]
        outs = call(
            functools.partial(forward_kernel, groups, capacity),
            "forward",
            [SCALAR] + shared_specs + [whole(dense.shape)],
            [
                like((SEQ, 3 * D), bf16),
                like((HEADS, SEQ, SEQ), bf16),
                like((SEQ, D), bf16),
                like((SEQ, D), f32),
                like((SEQ, groups), f32),
            ]
            + [like((2 * capacity, D), bf16)] * groups,
            [me_e] + shared + [dense],
            2 * SEQ * D * (4 * D + 3 * slots) + 4 * SEQ * SEQ * D,
        )
        state.append(outs[:5])
        sends = outs[5:]
        boxes.append(
            [sends[0]]
            + [lax.ppermute(sends[k], "expert", xor_pairs(groups, k)) for k in range(1, groups)]
        )

    actives, hiddens, returned = [], [], []
    for m in range(MB):
        args = list(boxes[m]) + [first, bias, second]
        outs = call(
            functools.partial(expert_kernel, groups, capacity),
            "experts",
            [whole(a.shape) for a in args],
            [like((2 * capacity, D), bf16)] * groups + [like((slots, wide), bf16)] * 2,
            args,
            8 * slots * D * wide,
        )
        actives.append(outs[groups])
        hiddens.append(outs[groups + 1])
        returned.append(
            [outs[0]]
            + [lax.ppermute(outs[k], "expert", xor_pairs(groups, k)) for k in range(1, groups)]
        )
    all_boxes = [box for m in range(MB) for box in boxes[m]]
    args = all_boxes + actives
    second_parts = call(
        functools.partial(second_grad_kernel, groups, capacity, owners),
        "second_grad",
        [whole(a.shape) for a in args],
        [like((owners, expert_out.shape[1], D), bf16)],
        args,
        2 * MB * slots * D * wide,
    )[0]
    args = all_boxes + hiddens
    first_parts = call(
        functools.partial(first_grad_kernel, groups, capacity, owners),
        "first_grad",
        [whole(a.shape) for a in args],
        [like((owners, expert_in.shape[1] + 8, wide), bf16)],
        args,
        2 * MB * slots * D * wide,
    )[0]
    d_second = scatter_sum(second_parts, "dp", me_owner)
    d_first = scatter_sum(first_parts, "dp", me_owner)

    outputs, token_grads = [], []
    total = None
    for m in range(MB):
        shared = [tokens] + routes + [cotangent]
        shared_specs = [of_batch(a.shape, m) for a in shared]
        rest = [dense] + list(state[m]) + list(returned[m]) + ([] if m == 0 else [total])
        outs = call(
            functools.partial(backward_kernel, groups, capacity, m > 0),
            "backward",
            [SCALAR] + shared_specs + [whole(a.shape) for a in rest],
            [
                like((1, SEQ, D), bf16),
                like((1, SEQ, D), f32),
                like((D, dense_width), f32),
            ],
            [me_e] + shared + rest,
            2 * SEQ * D * (8 * D + 3 * slots) + 8 * SEQ * SEQ * D,
        )
        outputs.append(outs[0])
        token_grads.append(outs[1])
        total = outs[2]
    low = total.astype(bf16)
    for k in (1 << b for b in range((groups - 1).bit_length())):
        low = (low.astype(f32) + lax.ppermute(low, "expert", xor_pairs(groups, k)).astype(f32)).astype(bf16)
    d_dense = scatter_sum(low.reshape(owners, rows, dense_width), "dp", me_owner)
    columns = expert_bias.shape[1]
    own_rows = expert_in.shape[1]
    d_bias = lax.dynamic_slice_in_dim(d_first[own_rows], me_owner * columns, columns, 0)
    return (
        jnp.stack(outputs, axis=0),
        jnp.stack(token_grads, axis=0),
        d_dense[:, 4 * D + groups],
        d_dense[:, : 3 * D],
        d_dense[:, 3 * D : 4 * D],
        d_dense[:, 4 * D + groups + 1],
        d_dense[:, 4 * D : 4 * D + groups],
        d_first[:own_rows][None],
        d_bias[None],
        d_second[None],
    )


def solution(mesh):
    images = P(None, ("dp", "expert"), None, None)
    weights = (
        P("dp"),
        P("dp", None),
        P("dp", None),
        P("dp"),
        P("dp", None),
        P("expert", "dp", None),
        P("expert", "dp"),
        P("expert", "dp", None),
    )
    return jax.shard_map(
        body,
        mesh=mesh,
        in_specs=(images,) * 4 + weights + (images,),
        out_specs=(images, images) + weights,
        check_vma=False,
    )
```

```python
import functools

import jax
import jax.numpy as jnp
from jax import lax
from jax.experimental import pallas as pl
from jax.experimental.pallas import tpu as pltpu
from jax.sharding import PartitionSpec as P

HEADS = 6
HEAD_DIM = 64
D = 384
SEQ = 197
MB = 3
LANES = 128
EPSILON = 1e-06
HIGHEST = lax.Precision.HIGHEST
VMEM_BYTES = 48 * 1024 * 1024
bf16 = jnp.bfloat16
f32 = jnp.float32


def dot(a, b, ca=1, cb=0, precision=None):
    return lax.dot_general(
        a, b, (((ca,), (cb,)), ((), ())), precision=precision, preferred_element_type=f32
    )


def xor_pairs(n, k):
    return [(i, i ^ k) for i in range(n)]


def spread_of(values):
    centre = jnp.mean(values, axis=-1, keepdims=True)
    centered = values - centre
    spread = jnp.mean(centered * centered, axis=-1, keepdims=True)
    rate = lax.rsqrt(spread + EPSILON)
    return centered * rate, rate


def norm_back(grad_hat, hat, rate):
    mean_one = jnp.mean(grad_hat, axis=-1, keepdims=True)
    mean_two = jnp.mean(grad_hat * hat, axis=-1, keepdims=True)
    return rate * (grad_hat - mean_one - hat * mean_two)


def side_rows(dense_ref):
    return jnp.transpose(dense_ref[:, 4 * D :].astype(f32))


def route_masks(index_ref, slot_ref, kept_ref, me, groups, capacity):
    index = index_ref[0, 0]
    target = jnp.where(kept_ref[0, 0] > 0, (index ^ me) * capacity + slot_ref[0, 0], -1)
    lanes = lax.broadcasted_iota(jnp.int32, (SEQ, groups * capacity), 1)
    places = [(lanes == target[:, k : k + 1]).astype(f32).astype(bf16) for k in range(2)]
    experts = lax.broadcasted_iota(jnp.int32, (SEQ, groups), 1)
    chosen = [(experts == index[:, k : k + 1]).astype(f32) for k in range(2)]
    return places, chosen


def half_mask(which):
    lanes = lax.broadcasted_iota(jnp.int32, (SEQ, LANES), 1)
    return (lanes < HEAD_DIM) if which == 0 else (lanes >= HEAD_DIM)


def forward_kernel(groups, capacity, me_ref, tokens_ref, index_ref, slot_ref, kept_ref, cot_ref, dense_ref, packed_ref, attn_ref, attended_ref, middle_ref, router_ref, *sends):
    me = me_ref[0]
    side = side_rows(dense_ref)
    gain_one = side[groups : groups + 1]
    gain_two = side[groups + 1 : groups + 2]
    inputs = tokens_ref[0, 0].astype(f32)
    hat, _ = spread_of(inputs)
    normed_low = (hat * gain_one).astype(bf16)
    packed = dot(normed_low, dense_ref[:, : 3 * D]).astype(bf16)
    packed_ref[...] = packed
    scale = HEAD_DIM ** (-0.5)
    parts = []
    for pair in range(HEADS // 2):
        lo = pair * LANES
        query = packed[:, lo : lo + LANES]
        keyed = packed[:, D + lo : D + lo + LANES]
        valued = packed[:, 2 * D + lo : 2 * D + lo + LANES]
        outs = []
        for which in range(2):
            masked = jnp.where(half_mask(which), query, jnp.zeros_like(query))
            scores = dot(masked, keyed, 1, 1) * scale
            top = jnp.max(scores, axis=-1, keepdims=True)
            raised = jnp.exp(scores - top)
            total = jnp.sum(raised, axis=-1, keepdims=True)
            attn_low = (raised * (1.0 / total)).astype(bf16)
            attn_ref[2 * pair + which] = attn_low
            outs.append(dot(attn_low, valued))
        parts.append(jnp.where(half_mask(0), outs[0], outs[1]))
    attended = jnp.concatenate(parts, axis=1).astype(bf16)
    attended_ref[...] = attended
    middle = inputs + dot(attended, dense_ref[:, 3 * D : 4 * D])
    middle_ref[...] = middle
    hat_two, _ = spread_of(middle)
    normed_two = hat_two * gain_two
    router_w = dense_ref[:, 4 * D :].astype(f32)[:, :groups]
    logits = dot(normed_two, router_w, precision=HIGHEST)
    raised = jnp.exp(logits - jnp.max(logits, axis=-1, keepdims=True))
    router = raised / jnp.sum(raised, axis=-1, keepdims=True)
    router_ref[...] = router
    places, chosen = route_masks(index_ref, slot_ref, kept_ref, me, groups, capacity)
    cot = cot_ref[0, 0].astype(f32)
    inbox = dot(places[0] + places[1], normed_two.astype(bf16), 0, 0).astype(bf16)
    grad_outbox = jnp.zeros((groups * capacity, D), f32)
    for k in range(2):
        gate = jnp.sum(chosen[k] * router, axis=-1, keepdims=True)
        grad_outbox += dot(places[k], (gate * cot).astype(bf16), 0, 0)
    grad_outbox = grad_outbox.astype(bf16)
    for g in range(groups):
        sends[g][:capacity] = inbox[g * capacity : (g + 1) * capacity]
        sends[g][capacity:] = grad_outbox[g * capacity : (g + 1) * capacity]


def expert_kernel(groups, capacity, *refs):
    boxes = refs[:groups]
    first_ref, bias_ref, second_ref = refs[groups : groups + 3]
    backs = refs[groups + 3 : 2 * groups + 3]
    active_ref, grad_hidden_ref = refs[2 * groups + 3 :]
    inbox = jnp.concatenate([box[:capacity] for box in boxes], axis=0)
    grad_outbox = jnp.concatenate([box[capacity:] for box in boxes], axis=0)
    wide = first_ref.shape[1]
    step = wide // 3
    outbox = jnp.zeros((groups * capacity, D), f32)
    grad_inbox = jnp.zeros((groups * capacity, D), f32)
    for at in range(0, wide, step):
        first = first_ref[:, at : at + step]
        second = second_ref[at : at + step, :]
        hidden = dot(inbox, first) + bias_ref[:, at : at + step].astype(f32)
        cdf = 0.5 + 0.5 * lax.erf(hidden * (0.5**0.5))
        density = jnp.exp(hidden * hidden * (-0.5)) * 0.3989422804014327
        active = (hidden * cdf).astype(bf16)
        grad_active = dot(grad_outbox, second, 1, 1)
        grad_hidden = ((cdf + hidden * density) * grad_active).astype(bf16)
        active_ref[:, at : at + step] = active
        grad_hidden_ref[:, at : at + step] = grad_hidden
        outbox += dot(active, second)
        grad_inbox += dot(grad_hidden, first, 1, 1)
    outbox = outbox.astype(bf16)
    grad_inbox = grad_inbox.astype(bf16)
    for g in range(groups):
        backs[g][:capacity] = outbox[g * capacity : (g + 1) * capacity]
        backs[g][capacity:] = grad_inbox[g * capacity : (g + 1) * capacity]


def place(keep_ref, send_ref, at, value):
    @pl.when((at & 1) == 0)
    def _():
        keep_ref[at >> 1] = value

    @pl.when((at & 1) == 1)
    def _():
        send_ref[at >> 1] = value


def second_grad_kernel(groups, capacity, owners, me_ref, *refs):
    boxes = [refs[m * groups : (m + 1) * groups] for m in range(MB)]
    actives = refs[MB * groups : MB * groups + MB]
    keep_ref, send_ref = refs[-2:]
    rows = keep_ref.shape[1]
    grads = [
        jnp.concatenate([box[capacity:] for box in boxes[m]], axis=0) for m in range(MB)
    ]
    wide = owners * rows
    step = wide // 2
    for at in range(0, wide, step):
        total = dot(actives[0][:, at : at + step], grads[0], 0, 0)
        for m in range(1, MB):
            total += dot(actives[m][:, at : at + step], grads[m], 0, 0)
        for j in range(step // rows):
            part = total[j * rows : (j + 1) * rows].astype(bf16)
            place(keep_ref, send_ref, (at // rows + j) ^ me_ref[1], part)


def first_grad_kernel(groups, capacity, owners, me_ref, *refs):
    boxes = [refs[m * groups : (m + 1) * groups] for m in range(MB)]
    hiddens = refs[MB * groups : MB * groups + MB]
    keep_ref, send_ref = refs[-2:]
    rows = D // owners
    extra = keep_ref.shape[1] - rows
    inboxes = [
        jnp.concatenate([box[:capacity] for box in boxes[m]], axis=0) for m in range(MB)
    ]
    wide = keep_ref.shape[2]
    step = wide // 3
    totals, biases = [], []
    for at in range(0, wide, step):
        total = dot(inboxes[0], hiddens[0][:, at : at + step], 0, 0)
        bias = jnp.sum(hiddens[0][:, at : at + step].astype(f32), axis=0, keepdims=True)
        for m in range(1, MB):
            total += dot(inboxes[m], hiddens[m][:, at : at + step], 0, 0)
            bias += jnp.sum(hiddens[m][:, at : at + step].astype(f32), axis=0, keepdims=True)
        totals.append(total)
        biases.append(jnp.broadcast_to(bias, (extra, step)))
    for j in range(owners):
        part = jnp.concatenate(
            [
                jnp.concatenate([total[j * rows : (j + 1) * rows], bias], axis=0)
                for total, bias in zip(totals, biases)
            ],
            axis=1,
        )
        place(keep_ref, send_ref, j ^ me_ref[1], part.astype(bf16))


def backward_kernel(groups, capacity, has_total, last, me_ref, tokens_ref, index_ref, slot_ref, kept_ref, cot_ref, dense_ref, packed_ref, attn_ref, attended_ref, middle_ref, router_ref, *refs):
    backs = refs[:groups]
    total_ref = refs[groups] if has_total else None
    if last:
        output_ref, d_tokens_ref, keep_ref, send_ref = refs[-4:]
    else:
        output_ref, d_tokens_ref, grads_ref = refs[-3:]
    me = me_ref[0]
    side = side_rows(dense_ref)
    gain_one = side[groups : groups + 1]
    gain_two = side[groups + 1 : groups + 2]
    middle = middle_ref[...]
    router = router_ref[...]
    cot = cot_ref[0, 0].astype(f32)
    places, chosen = route_masks(index_ref, slot_ref, kept_ref, me, groups, capacity)
    outbox = jnp.concatenate([box[:capacity] for box in backs], axis=0)
    grad_inbox = jnp.concatenate([box[capacity:] for box in backs], axis=0)
    mixed = middle
    grad_router = jnp.zeros((SEQ, groups), f32)
    for k in range(2):
        picked = dot(places[k], outbox)
        gate = jnp.sum(chosen[k] * router, axis=-1, keepdims=True)
        mixed = mixed + gate * picked
        grad_router += chosen[k] * jnp.sum(cot * picked, axis=-1, keepdims=True)
    output_ref[0] = mixed.astype(bf16)
    grad_logits = router * (grad_router - jnp.sum(router * grad_router, axis=-1, keepdims=True))
    router_w = dense_ref[:, 4 * D :].astype(f32)[:, :groups]
    grad_normed_two = dot(grad_logits, router_w, 1, 1, precision=HIGHEST) + dot(
        places[0] + places[1], grad_inbox
    )
    hat_two, rate_two = spread_of(middle)
    grad_middle = norm_back(grad_normed_two * gain_two, hat_two, rate_two) + cot
    lanes = lax.broadcasted_iota(jnp.int32, (SEQ, LANES), 1)
    column_one = (lanes == groups).astype(f32)
    column_two = (lanes == groups + 1).astype(f32)
    logits_wide = sum(
        jnp.where(lanes == e, grad_logits[:, e : e + 1], 0.0) for e in range(groups)
    )
    side_grad = dot(hat_two * gain_two, logits_wide, 0, 0, precision=HIGHEST)
    side_grad += dot(grad_normed_two * hat_two, column_two, 0, 0, precision=HIGHEST)
    grad_branch = grad_middle.astype(bf16)
    out_grad = dot(attended_ref[...], grad_branch, 0, 0)
    grad_attended = dot(grad_branch, dense_ref[:, 3 * D : 4 * D], 1, 1).astype(bf16)
    scale = HEAD_DIM ** (-0.5)
    first_half = half_mask(0)
    queries, keys, values = [], [], []
    for pair in range(HEADS // 2):
        lo = pair * LANES
        query = packed_ref[:, lo : lo + LANES]
        keyed = packed_ref[:, D + lo : D + lo + LANES]
        valued = packed_ref[:, 2 * D + lo : 2 * D + lo + LANES]
        pulled = grad_attended[:, lo : lo + LANES]
        q_outs, k_outs, v_outs = [], [], []
        for which in range(2):
            attn_low = attn_ref[2 * pair + which]
            attn = attn_low.astype(f32)
            masked = jnp.where(half_mask(which), pulled, jnp.zeros_like(pulled))
            weighted = dot(masked, valued, 1, 1)
            inner = jnp.sum(attn * weighted, axis=-1, keepdims=True)
            grad_scores = (attn * (weighted - inner)).astype(bf16)
            v_outs.append(dot(attn_low, pulled, 0, 0))
            q_outs.append(dot(grad_scores, keyed))
            k_outs.append(dot(grad_scores, query, 0, 0))
        queries.append(jnp.where(first_half, q_outs[0], q_outs[1]) * scale)
        keys.append(jnp.where(first_half, k_outs[0], k_outs[1]) * scale)
        values.append(jnp.where(first_half, v_outs[0], v_outs[1]))
    grad_packed = jnp.concatenate(queries + keys + values, axis=1).astype(bf16)
    grad_normed = dot(grad_packed, dense_ref[:, : 3 * D], 1, 1)
    hat, rate = spread_of(tokens_ref[0, 0].astype(f32))
    packed_grad = dot((hat * gain_one).astype(bf16), grad_packed, 0, 0)
    side_grad += dot(grad_normed * hat, column_one, 0, 0, precision=HIGHEST)
    d_tokens_ref[0] = grad_middle + norm_back(grad_normed * gain_one, hat, rate)
    pieces = []
    for lo, part in ((0, packed_grad), (3 * D, out_grad), (4 * D, side_grad)):
        hi = lo + part.shape[1]
        if has_total:
            part = part + total_ref[:, lo:hi]
        pieces.append(part)
        if not last:
            grads_ref[:, lo:hi] = part
    if last:
        joined = jnp.concatenate(pieces, axis=1).astype(bf16)
        left, right = split_halves(joined)
        core = me & 1
        rows = keep_ref.shape[1]
        for j in range(keep_ref.shape[0]):
            at = j ^ me_ref[1]
            cut = slice(j * rows, (j + 1) * rows)

            @pl.when(core == 0)
            def _(at=at, cut=cut):
                keep_ref[at] = left[cut]
                send_ref[at] = right[cut]

            @pl.when(core == 1)
            def _(at=at, cut=cut):
                keep_ref[at] = right[cut]
                send_ref[at] = left[cut]


def split_halves(joined):
    half = half_width(joined.shape[1])
    return joined[:, :half], joined[:, joined.shape[1] - half :]


def half_width(width):
    return -(-width // (2 * LANES)) * LANES


def join_halves(left, right, width):
    half = left.shape[1]
    return jnp.concatenate([left, right[:, 2 * half - width :]], axis=1)


def pack_kernel(me_ref, qkv_ref, out_ref, side_ref, first_ref, second_ref, bias_ref, half_ref, pack_ref):
    joined = jnp.concatenate([qkv_ref[...], out_ref[...], side_ref[...]], axis=1)
    left, right = split_halves(joined)

    @pl.when((me_ref[0] & 1) == 0)
    def _():
        half_ref[...] = left

    @pl.when((me_ref[0] & 1) == 1)
    def _():
        half_ref[...] = right

    rows = first_ref.shape[1]
    tall = second_ref.shape[1]
    pack_ref[:tall] = second_ref[0]
    for c in range(first_ref.shape[2] // D):
        pack_ref[tall + c * rows : tall + (c + 1) * rows] = first_ref[0, :, c * D : (c + 1) * D]
    pack_ref[2 * tall :] = bias_ref[...]


def arrange_kernel(count, me_ref, *refs):
    out_ref = refs[-1]
    for k in range(count):
        out_ref[me_ref[1] ^ k] = refs[k][...]


def join_kernel(me_ref, mine_ref, other_ref, out_ref):
    width = out_ref.shape[1]

    @pl.when((me_ref[0] & 1) == 0)
    def _():
        out_ref[...] = join_halves(mine_ref[...], other_ref[...], width)

    @pl.when((me_ref[0] & 1) == 1)
    def _():
        out_ref[...] = join_halves(other_ref[...], mine_ref[...], width)


def unpack_kernel(count, me_ref, *refs):
    first_ref, second_ref, bias_ref, table = refs[count:]
    rows = first_ref.shape[1]
    tall = second_ref.shape[1]
    for k in range(count):
        at = me_ref[1] ^ k
        second_ref[at] = refs[k][:tall]
        for c in range(first_ref.shape[2] // D):
            first_ref[at, :, c * D : (c + 1) * D] = refs[k][tall + c * rows : tall + (c + 1) * rows]
        table[at] = refs[k][2 * tall :]
    fold = D // tall
    for i in range(count // fold):
        line = table[fold * i][:1].astype(f32)
        for r in range(1, fold):
            line += table[fold * i + r][r : r + 1].astype(f32)
        bias_ref[:, i * D : (i + 1) * D] = line


def merge_kernel(keep_ref, got_ref, own_ref, *sends):
    for k in range(keep_ref.shape[0]):
        total = keep_ref[k].astype(f32) + got_ref[k].astype(f32)
        if k == 0:
            own_ref[...] = total
        else:
            sends[k - 1][...] = total.astype(bf16)


def deal_kernel(keep_ref, got_ref, own_ref, send_ref):
    for k in range(keep_ref.shape[0]):
        total = (keep_ref[k].astype(f32) + got_ref[k].astype(f32)).astype(bf16)
        if k % 2 == 0:
            own_ref[k // 2] = total
        else:
            send_ref[k // 2] = total


def total_kernel(own_ref, *refs):
    total = own_ref[...].astype(f32)
    for ref in refs[:-1]:
        total += ref[...].astype(f32)
    refs[-1][...] = total.astype(refs[-1].dtype)


def finish_kernel(me_ref, mine_ref, other_ref, qkv_ref, out_ref, side_ref):
    def write(left, right):
        joined = join_halves(left, right, 4 * D + LANES).astype(f32)
        qkv_ref[...] = joined[:, : 3 * D]
        out_ref[...] = joined[:, 3 * D : 4 * D]
        side_ref[...] = joined[:, 4 * D :]

    @pl.when((me_ref[0] & 1) == 0)
    def _():
        write(mine_ref[...], other_ref[...])

    @pl.when((me_ref[0] & 1) == 1)
    def _():
        write(other_ref[...], mine_ref[...])


def params():
    return pltpu.CompilerParams(vmem_limit_bytes=VMEM_BYTES)


def whole(shape):
    zeros = (0,) * len(shape)
    return pl.BlockSpec(tuple(shape), lambda i: zeros)


def of_batch(shape, batch):
    tail = (0,) * (len(shape) - 1)
    return pl.BlockSpec((1,) + tuple(shape[1:]), lambda i: (batch,) + tail)


SCALAR = pl.BlockSpec(memory_space=pltpu.SMEM)


def call(kernel, name, outs, args, us, in_specs=None, scratch=()):
    if in_specs is None:
        in_specs = [SCALAR if a.dtype == jnp.int32 else whole(a.shape) for a in args]
    moved = sum(a.size * a.dtype.itemsize for a in args)
    moved += sum(a.size * a.dtype.itemsize for a in outs)
    return pl.pallas_call(
        kernel,
        grid=(1,),
        in_specs=in_specs,
        out_specs=[whole(o.shape) for o in outs],
        out_shape=outs,
        scratch_shapes=list(scratch),
        compiler_params=params(),
        cost_estimate=pl.CostEstimate(flops=int(us * 1e9), bytes_accessed=moved, transcendentals=0),
        name=name,
    )(*args)


def like(shape, dtype):
    return jax.ShapeDtypeStruct(tuple(shape), dtype)


def send(value, axis, k):
    return lax.ppermute(value, axis, xor_pairs(lax.axis_size(axis), k))


def gather_pieces(own, axis):
    count = lax.axis_size(axis)
    pieces = [own] + [None] * (count - 1)
    order = sorted(range(2, count, 2), reverse=True)
    for k in order:
        pieces[k] = send(own, axis, k)
    for k in [0] + order:
        pieces[k + 1] = send(pieces[k], axis, 1)
    return pieces


def sum_rest(keep, got, axis):
    shape = keep.shape[1:]
    count = keep.shape[0]
    merged = call(
        merge_kernel,
        "merge",
        [like(shape, f32)] + [like(shape, bf16)] * (count - 1),
        [keep, got],
        2,
    )
    return [merged[0]] + [send(merged[k], axis, 2 * k) for k in reversed(range(1, count))]


def body(
    tokens,
    expert_index,
    expert_slot,
    route_kept,
    ln1_gain,
    w_qkv,
    w_out,
    ln2_gain,
    w_router,
    expert_in,
    expert_bias,
    expert_out,
    cotangent,
):
    groups = lax.axis_size("expert")
    owners = lax.axis_size("dp")
    capacity = 8 * (5 * SEQ // (16 * groups) + 1)
    slots = groups * capacity
    wide = expert_in.shape[2]
    rows = w_qkv.shape[0]
    tall = expert_out.shape[1]
    dense_width = 4 * D + LANES
    half = half_width(dense_width)
    me = jnp.stack([lax.axis_index("expert"), lax.axis_index("dp")]).astype(jnp.int32)
    side = jnp.concatenate(
        [
            w_router,
            ln1_gain[:, None],
            ln2_gain[:, None],
            jnp.zeros((rows, LANES - groups - 2), bf16),
        ],
        axis=1,
    )
    fold = D // tall
    bias_rows = jnp.pad(
        (jnp.eye(fold, dtype=bf16)[:, :, None] * expert_bias[0]).reshape(fold, D),
        ((0, 16 - fold), (0, 0)),
    )
    own_half, own_pack = call(
        pack_kernel,
        "pack",
        [like((rows, half), bf16), like((2 * tall + 16, D), bf16)],
        [me, w_qkv, w_out, side, expert_in, expert_out, bias_rows],
        2,
    )
    halves = gather_pieces(own_half, "dp")
    mine = call(
        functools.partial(arrange_kernel, owners),
        "arrange",
        [like((owners, rows, half), bf16)],
        [me] + halves,
        2,
    )[0].reshape(D, half)
    other = send(mine, "expert", 1)
    dense = call(join_kernel, "join", [like((D, dense_width), bf16)], [me, mine, other], 2)[0]
    packs = gather_pieces(own_pack, "dp")
    first, second, bias = call(
        functools.partial(unpack_kernel, owners),
        "unpack",
        [
            like((owners, rows, wide), bf16),
            like((owners, tall, D), bf16),
            like((1, wide), f32),
        ],
        [me] + packs,
        4,
        scratch=[pltpu.VMEM((owners, 16, D), bf16)],
    )
    first = first.reshape(D, wide)
    second = second.reshape(wide, D)

    routes = [expert_index, expert_slot, route_kept]
    state = []
    boxes = []
    for m in range(MB):
        shared = [tokens] + routes + [cotangent]
        outs = call(
            functools.partial(forward_kernel, groups, capacity),
            "forward",
            [
                like((SEQ, 3 * D), bf16),
                like((HEADS, SEQ, SEQ), bf16),
                like((SEQ, D), bf16),
                like((SEQ, D), f32),
                like((SEQ, groups), f32),
            ]
            + [like((2 * capacity, D), bf16)] * groups,
            [me] + shared + [dense],
            4,
            in_specs=[SCALAR] + [of_batch(a.shape, m) for a in shared] + [whole(dense.shape)],
        )
        state.append(outs[:5])
        sends = outs[5:]
        boxes.append(
            [sends[0]] + [send(sends[k], "expert", k) for k in reversed(range(1, groups))][::-1]
        )

    actives, hiddens, returned = [], [], []
    for m in range(MB):
        outs = call(
            functools.partial(expert_kernel, groups, capacity),
            "experts",
            [like((2 * capacity, D), bf16)] * groups + [like((slots, wide), bf16)] * 2,
            list(boxes[m]) + [first, bias, second],
            5,
        )
        actives.append(outs[groups])
        hiddens.append(outs[groups + 1])
        returned.append(
            [outs[0]] + [send(outs[k], "expert", k) for k in reversed(range(1, groups))][::-1]
        )
    all_boxes = [box for m in range(MB) for box in boxes[m]]
    second_keep, second_send = call(
        functools.partial(second_grad_kernel, groups, capacity, owners),
        "second_grad",
        [like((owners // 2, tall, D), bf16)] * 2,
        [me] + all_boxes + actives,
        5,
    )
    first_keep, first_send = call(
        functools.partial(first_grad_kernel, groups, capacity, owners),
        "first_grad",
        [like((owners // 2, rows + 8, wide), bf16)] * 2,
        [me] + all_boxes + hiddens,
        5,
    )
    dense_late, second_send, first_send = lax.optimization_barrier(
        (dense, second_send, first_send)
    )
    second_terms = sum_rest(second_keep, send(second_send, "dp", 1), "dp")
    first_terms = sum_rest(first_keep, send(first_send, "dp", 1), "dp")

    outputs, token_grads = [], []
    total = None
    for m in range(MB):
        last = m == MB - 1
        shared = [tokens] + routes + [cotangent]
        rest = [dense_late] + list(state[m]) + list(returned[m]) + ([] if m == 0 else [total])
        outs = call(
            functools.partial(backward_kernel, groups, capacity, m > 0, last),
            "backward",
            [like((1, SEQ, D), bf16), like((1, SEQ, D), f32)]
            + (
                [like((owners, rows, half), bf16)] * 2
                if last
                else [like((D, dense_width), f32)]
            ),
            [me] + shared + rest,
            8,
            in_specs=[SCALAR]
            + [of_batch(a.shape, m) for a in shared]
            + [whole(a.shape) for a in rest],
        )
        outputs.append(outs[0])
        token_grads.append(outs[1])
        total = outs[2]
        dense_send = outs[-1]
    keep, share = call(
        deal_kernel,
        "deal",
        [like((owners // 2, rows, half), bf16)] * 2,
        [total, send(dense_send, "expert", 1)],
        2,
    )
    dense_terms = sum_rest(keep, send(share, "dp", 1), "dp")
    reduced = call(total_kernel, "total", [like((rows, half), bf16)], dense_terms, 1)[0]
    bits = [1 << b for b in range(1, (groups - 1).bit_length())]
    for k in bits:
        reduced = call(
            total_kernel,
            "total",
            [like((rows, half), bf16)],
            [reduced, send(reduced, "expert", k)],
            1,
        )[0]
    d_qkv, d_out, d_side = call(
        finish_kernel,
        "finish",
        [like((rows, 3 * D), f32), like((rows, D), f32), like((rows, LANES), f32)],
        [me, reduced, send(reduced, "expert", 1)],
        1,
    )
    d_second = call(total_kernel, "total", [like((tall, D), f32)], second_terms, 1)[0]
    d_first = call(total_kernel, "total", [like((rows + 8, wide), f32)], first_terms, 1)[0]
    d_bias = lax.dynamic_slice_in_dim(d_first[rows], me[1] * tall, tall, 0)
    return (
        jnp.stack(outputs, axis=0),
        jnp.stack(token_grads, axis=0),
        d_side[:, groups],
        d_qkv,
        d_out,
        d_side[:, groups + 1],
        d_side[:, :groups],
        d_first[:rows][None],
        d_bias[None],
        d_second[None],
    )


def solution(mesh):
    images = P(None, ("dp", "expert"), None, None)
    weights = (
        P("dp"),
        P("dp", None),
        P("dp", None),
        P("dp"),
        P("dp", None),
        P("expert", "dp", None),
        P("expert", "dp"),
        P("expert", "dp", None),
    )
    return jax.shard_map(
        body,
        mesh=mesh,
        in_specs=(images,) * 4 + weights + (images,),
        out_specs=(images, images) + weights,
        check_vma=False,
    )
```

```python
import functools

import jax
import jax.numpy as jnp
from jax import lax
from jax.experimental import pallas as pl
from jax.experimental.pallas import tpu as pltpu
from jax.sharding import PartitionSpec as P

HEADS = 6
HEAD_DIM = 64
D = 384
SEQ = 197
MB = 3
LANES = 128
EPSILON = 1e-06
HIGHEST = lax.Precision.HIGHEST
VMEM_BYTES = 24 * 1024 * 1024
bf16 = jnp.bfloat16
f32 = jnp.float32


def dot(a, b, ca=1, cb=0, precision=None):
    return lax.dot_general(
        a, b, (((ca,), (cb,)), ((), ())), precision=precision, preferred_element_type=f32
    )


def xor_pairs(n, k):
    return [(i, i ^ k) for i in range(n)]


def spread_of(values):
    centre = jnp.mean(values, axis=-1, keepdims=True)
    centered = values - centre
    spread = jnp.mean(centered * centered, axis=-1, keepdims=True)
    rate = lax.rsqrt(spread + EPSILON)
    return centered * rate, rate


def norm_back(grad_hat, hat, rate):
    mean_one = jnp.mean(grad_hat, axis=-1, keepdims=True)
    mean_two = jnp.mean(grad_hat * hat, axis=-1, keepdims=True)
    return rate * (grad_hat - mean_one - hat * mean_two)


def side_rows(dense_ref):
    return jnp.transpose(dense_ref[:, 4 * D :].astype(f32))


def route_masks(index_ref, slot_ref, kept_ref, me, groups, capacity):
    index = index_ref[0, 0]
    target = jnp.where(kept_ref[0, 0] > 0, (index ^ me) * capacity + slot_ref[0, 0], -1)
    both = jnp.transpose(jnp.concatenate([index, target], axis=0).astype(f32)).astype(jnp.int32)
    index, target = both[:, :2], both[:, 2:]
    lanes = lax.broadcasted_iota(jnp.int32, (SEQ, groups * capacity), 1)
    places = [(lanes == target[:, k : k + 1]).astype(f32).astype(bf16) for k in range(2)]
    experts = lax.broadcasted_iota(jnp.int32, (SEQ, groups), 1)
    chosen = [(experts == index[:, k : k + 1]).astype(f32) for k in range(2)]
    return places, chosen


def half_mask(which):
    lanes = lax.broadcasted_iota(jnp.int32, (SEQ, LANES), 1)
    return (lanes < HEAD_DIM) if which == 0 else (lanes >= HEAD_DIM)


def forward_kernel(groups, capacity, me_ref, tokens_ref, index_ref, slot_ref, kept_ref, cot_ref, dense_ref, packed_ref, attn_ref, attended_ref, middle_ref, router_ref, *sends):
    me = me_ref[0]
    side = side_rows(dense_ref)
    gain_one = side[groups : groups + 1]
    gain_two = side[groups + 1 : groups + 2]
    inputs = tokens_ref[0, 0].astype(f32)
    hat, _ = spread_of(inputs)
    normed_low = (hat * gain_one).astype(bf16)
    packed = dot(normed_low, dense_ref[:, : 3 * D]).astype(bf16)
    packed_ref[...] = packed
    scale = HEAD_DIM ** (-0.5)
    parts = []
    for pair in range(HEADS // 2):
        lo = pair * LANES
        query = packed[:, lo : lo + LANES]
        keyed = packed[:, D + lo : D + lo + LANES]
        valued = packed[:, 2 * D + lo : 2 * D + lo + LANES]
        outs = []
        for which in range(2):
            masked = jnp.where(half_mask(which), query, jnp.zeros_like(query))
            scores = dot(masked, keyed, 1, 1) * scale
            top = jnp.max(scores, axis=-1, keepdims=True)
            raised = jnp.exp(scores - top)
            total = jnp.sum(raised, axis=-1, keepdims=True)
            attn_low = (raised * (1.0 / total)).astype(bf16)
            attn_ref[2 * pair + which] = attn_low
            outs.append(dot(attn_low, valued))
        parts.append(jnp.where(half_mask(0), outs[0], outs[1]))
    attended = jnp.concatenate(parts, axis=1).astype(bf16)
    attended_ref[...] = attended
    middle = inputs + dot(attended, dense_ref[:, 3 * D : 4 * D])
    middle_ref[...] = middle
    hat_two, _ = spread_of(middle)
    normed_two = hat_two * gain_two
    router_w = dense_ref[:, 4 * D :].astype(f32)[:, :groups]
    logits = dot(normed_two, router_w, precision=HIGHEST)
    raised = jnp.exp(logits - jnp.max(logits, axis=-1, keepdims=True))
    router = raised / jnp.sum(raised, axis=-1, keepdims=True)
    router_ref[...] = router
    places, chosen = route_masks(index_ref, slot_ref, kept_ref, me, groups, capacity)
    cot = cot_ref[0, 0].astype(f32)
    inbox = dot(places[0] + places[1], normed_two.astype(bf16), 0, 0).astype(bf16)
    grad_outbox = jnp.zeros((groups * capacity, D), f32)
    for k in range(2):
        gate = jnp.sum(chosen[k] * router, axis=-1, keepdims=True)
        grad_outbox += dot(places[k], (gate * cot).astype(bf16), 0, 0)
    grad_outbox = grad_outbox.astype(bf16)
    for g in range(groups):
        sends[g][:capacity] = inbox[g * capacity : (g + 1) * capacity]
        sends[g][capacity:] = grad_outbox[g * capacity : (g + 1) * capacity]


def expert_kernel(groups, capacity, *refs):
    boxes = refs[:groups]
    first_ref, bias_ref, second_ref = refs[groups : groups + 3]
    backs = refs[groups + 3 : 2 * groups + 3]
    active_ref, grad_hidden_ref = refs[2 * groups + 3 :]
    inbox = jnp.concatenate([box[:capacity] for box in boxes], axis=0)
    grad_outbox = jnp.concatenate([box[capacity:] for box in boxes], axis=0)
    wide = first_ref.shape[1]
    step = wide // 3
    outbox = jnp.zeros((groups * capacity, D), f32)
    grad_inbox = jnp.zeros((groups * capacity, D), f32)
    for at in range(0, wide, step):
        first = first_ref[:, at : at + step]
        second = second_ref[at : at + step, :]
        hidden = dot(inbox, first) + bias_ref[:, at : at + step].astype(f32)
        cdf = 0.5 + 0.5 * lax.erf(hidden * (0.5**0.5))
        density = jnp.exp(hidden * hidden * (-0.5)) * 0.3989422804014327
        active = (hidden * cdf).astype(bf16)
        grad_active = dot(grad_outbox, second, 1, 1)
        grad_hidden = ((cdf + hidden * density) * grad_active).astype(bf16)
        active_ref[:, at : at + step] = active
        grad_hidden_ref[:, at : at + step] = grad_hidden
        outbox += dot(active, second)
        grad_inbox += dot(grad_hidden, first, 1, 1)
    outbox = outbox.astype(bf16)
    grad_inbox = grad_inbox.astype(bf16)
    for g in range(groups):
        backs[g][:capacity] = outbox[g * capacity : (g + 1) * capacity]
        backs[g][capacity:] = grad_inbox[g * capacity : (g + 1) * capacity]


def place(keep_ref, send_ref, at, value):
    @pl.when((at & 1) == 0)
    def _():
        keep_ref[at >> 1] = value

    @pl.when((at & 1) == 1)
    def _():
        send_ref[at >> 1] = value


def second_grad_kernel(groups, capacity, owners, me_ref, *refs):
    boxes = [refs[m * groups : (m + 1) * groups] for m in range(MB)]
    actives = refs[MB * groups : MB * groups + MB]
    keep_ref, send_ref = refs[-2:]
    rows = keep_ref.shape[1]
    grads = [
        jnp.concatenate([box[capacity:] for box in boxes[m]], axis=0) for m in range(MB)
    ]
    wide = owners * rows
    step = wide // 2
    for at in range(0, wide, step):
        total = dot(actives[0][:, at : at + step], grads[0], 0, 0)
        for m in range(1, MB):
            total += dot(actives[m][:, at : at + step], grads[m], 0, 0)
        for j in range(step // rows):
            part = total[j * rows : (j + 1) * rows].astype(bf16)
            place(keep_ref, send_ref, (at // rows + j) ^ me_ref[1], part)


def first_grad_kernel(groups, capacity, owners, me_ref, *refs):
    boxes = [refs[m * groups : (m + 1) * groups] for m in range(MB)]
    hiddens = refs[MB * groups : MB * groups + MB]
    keep_ref, send_ref = refs[-2:]
    rows = D // owners
    extra = keep_ref.shape[1] - rows
    inboxes = [
        jnp.concatenate([box[:capacity] for box in boxes[m]], axis=0) for m in range(MB)
    ]
    wide = keep_ref.shape[2]
    step = wide // 3
    totals, biases = [], []
    for at in range(0, wide, step):
        total = dot(inboxes[0], hiddens[0][:, at : at + step], 0, 0)
        bias = jnp.sum(hiddens[0][:, at : at + step].astype(f32), axis=0, keepdims=True)
        for m in range(1, MB):
            total += dot(inboxes[m], hiddens[m][:, at : at + step], 0, 0)
            bias += jnp.sum(hiddens[m][:, at : at + step].astype(f32), axis=0, keepdims=True)
        totals.append(total)
        biases.append(jnp.broadcast_to(bias, (extra, step)))
    for j in range(owners):
        part = jnp.concatenate(
            [
                jnp.concatenate([total[j * rows : (j + 1) * rows], bias], axis=0)
                for total, bias in zip(totals, biases)
            ],
            axis=1,
        )
        place(keep_ref, send_ref, j ^ me_ref[1], part.astype(bf16))


def backward_kernel(groups, capacity, has_total, last, me_ref, tokens_ref, index_ref, slot_ref, kept_ref, cot_ref, dense_ref, packed_ref, attn_ref, attended_ref, middle_ref, router_ref, *refs):
    backs = refs[:groups]
    total_ref = refs[groups] if has_total else None
    if last:
        output_ref, d_tokens_ref, keep_ref, send_ref = refs[-4:]
    else:
        output_ref, d_tokens_ref, grads_ref = refs[-3:]
    me = me_ref[0]
    side = side_rows(dense_ref)
    gain_one = side[groups : groups + 1]
    gain_two = side[groups + 1 : groups + 2]
    middle = middle_ref[...]
    router = router_ref[...]
    cot = cot_ref[0, 0].astype(f32)
    places, chosen = route_masks(index_ref, slot_ref, kept_ref, me, groups, capacity)
    outbox = jnp.concatenate([box[:capacity] for box in backs], axis=0)
    grad_inbox = jnp.concatenate([box[capacity:] for box in backs], axis=0)
    mixed = middle
    grad_router = jnp.zeros((SEQ, groups), f32)
    for k in range(2):
        picked = dot(places[k], outbox)
        gate = jnp.sum(chosen[k] * router, axis=-1, keepdims=True)
        mixed = mixed + gate * picked
        grad_router += chosen[k] * jnp.sum(cot * picked, axis=-1, keepdims=True)
    output_ref[0, 0] = mixed.astype(bf16)
    grad_logits = router * (grad_router - jnp.sum(router * grad_router, axis=-1, keepdims=True))
    router_w = dense_ref[:, 4 * D :].astype(f32)[:, :groups]
    grad_normed_two = dot(grad_logits, router_w, 1, 1, precision=HIGHEST) + dot(
        places[0] + places[1], grad_inbox
    )
    hat_two, rate_two = spread_of(middle)
    grad_middle = norm_back(grad_normed_two * gain_two, hat_two, rate_two) + cot
    lanes = lax.broadcasted_iota(jnp.int32, (SEQ, LANES), 1)
    column_one = (lanes == groups).astype(f32)
    column_two = (lanes == groups + 1).astype(f32)
    logits_wide = sum(
        jnp.where(lanes == e, grad_logits[:, e : e + 1], 0.0) for e in range(groups)
    )
    side_grad = dot(hat_two * gain_two, logits_wide, 0, 0, precision=HIGHEST)
    side_grad += dot(grad_normed_two * hat_two, column_two, 0, 0, precision=HIGHEST)
    grad_branch = grad_middle.astype(bf16)
    out_grad = dot(attended_ref[...], grad_branch, 0, 0)
    grad_attended = dot(grad_branch, dense_ref[:, 3 * D : 4 * D], 1, 1).astype(bf16)
    scale = HEAD_DIM ** (-0.5)
    first_half = half_mask(0)
    queries, keys, values = [], [], []
    for pair in range(HEADS // 2):
        lo = pair * LANES
        query = packed_ref[:, lo : lo + LANES]
        keyed = packed_ref[:, D + lo : D + lo + LANES]
        valued = packed_ref[:, 2 * D + lo : 2 * D + lo + LANES]
        pulled = grad_attended[:, lo : lo + LANES]
        q_outs, k_outs, v_outs = [], [], []
        for which in range(2):
            attn_low = attn_ref[2 * pair + which]
            attn = attn_low.astype(f32)
            masked = jnp.where(half_mask(which), pulled, jnp.zeros_like(pulled))
            weighted = dot(masked, valued, 1, 1)
            inner = jnp.sum(attn * weighted, axis=-1, keepdims=True)
            grad_scores = (attn * (weighted - inner)).astype(bf16)
            v_outs.append(dot(attn_low, pulled, 0, 0))
            q_outs.append(dot(grad_scores, keyed))
            k_outs.append(dot(grad_scores, query, 0, 0))
        queries.append(jnp.where(first_half, q_outs[0], q_outs[1]) * scale)
        keys.append(jnp.where(first_half, k_outs[0], k_outs[1]) * scale)
        values.append(jnp.where(first_half, v_outs[0], v_outs[1]))
    grad_packed = jnp.concatenate(queries + keys + values, axis=1).astype(bf16)
    grad_normed = dot(grad_packed, dense_ref[:, : 3 * D], 1, 1)
    hat, rate = spread_of(tokens_ref[0, 0].astype(f32))
    packed_grad = dot((hat * gain_one).astype(bf16), grad_packed, 0, 0)
    side_grad += dot(grad_normed * hat, column_one, 0, 0, precision=HIGHEST)
    d_tokens_ref[0, 0] = grad_middle + norm_back(grad_normed * gain_one, hat, rate)
    pieces = []
    for lo, part in ((0, packed_grad), (3 * D, out_grad), (4 * D, side_grad)):
        hi = lo + part.shape[1]
        if has_total:
            part = part + total_ref[:, lo:hi]
        pieces.append(part)
        if not last:
            grads_ref[:, lo:hi] = part
    if last:
        joined = jnp.concatenate(pieces, axis=1).astype(bf16)
        left, right = split_halves(joined)
        core = me & 1
        rows = keep_ref.shape[1]
        for j in range(keep_ref.shape[0]):
            at = j ^ me_ref[1]
            cut = slice(j * rows, (j + 1) * rows)

            @pl.when(core == 0)
            def _(at=at, cut=cut):
                keep_ref[at] = left[cut]
                send_ref[at] = right[cut]

            @pl.when(core == 1)
            def _(at=at, cut=cut):
                keep_ref[at] = right[cut]
                send_ref[at] = left[cut]


def split_halves(joined):
    half = half_width(joined.shape[1])
    return joined[:, :half], joined[:, joined.shape[1] - half :]


def half_width(width):
    return -(-width // (2 * LANES)) * LANES


def join_halves(left, right, width):
    half = left.shape[1]
    return jnp.concatenate([left, right[:, 2 * half - width :]], axis=1)


def pack_kernel(me_ref, qkv_ref, out_ref, router_ref, one_ref, two_ref, first_ref, second_ref, bias_ref, half_ref, pack_ref):
    rows = qkv_ref.shape[0]
    lines = [router_ref[...].astype(f32), one_ref[...].astype(f32), two_ref[...].astype(f32)]
    used = sum(line.shape[0] for line in lines)
    lines.append(jnp.zeros((LANES - used, rows), f32))
    side = jnp.transpose(jnp.concatenate(lines, axis=0)).astype(bf16)
    joined = jnp.concatenate([qkv_ref[...], out_ref[...], side], axis=1)
    left, right = split_halves(joined)

    @pl.when((me_ref[0] & 1) == 0)
    def _():
        half_ref[...] = left

    @pl.when((me_ref[0] & 1) == 1)
    def _():
        half_ref[...] = right

    rows = first_ref.shape[1]
    tall = second_ref.shape[1]
    pack_ref[:tall] = second_ref[0]
    for c in range(first_ref.shape[2] // D):
        pack_ref[tall + c * rows : tall + (c + 1) * rows] = first_ref[0, :, c * D : (c + 1) * D]
    pack_ref[2 * tall :] = bias_ref[...]


def arrange_kernel(count, me_ref, *refs):
    out_ref = refs[-1]
    for k in range(count):
        out_ref[me_ref[1] ^ k] = refs[k][...]


def join_kernel(me_ref, mine_ref, other_ref, out_ref):
    width = out_ref.shape[1]

    @pl.when((me_ref[0] & 1) == 0)
    def _():
        out_ref[...] = join_halves(mine_ref[...], other_ref[...], width)

    @pl.when((me_ref[0] & 1) == 1)
    def _():
        out_ref[...] = join_halves(other_ref[...], mine_ref[...], width)


def unpack_kernel(count, me_ref, *refs):
    first_ref, second_ref, bias_ref, table = refs[count:]
    rows = first_ref.shape[1]
    tall = second_ref.shape[1]
    for k in range(count):
        at = me_ref[1] ^ k
        second_ref[at] = refs[k][:tall]
        for c in range(first_ref.shape[2] // D):
            first_ref[at, :, c * D : (c + 1) * D] = refs[k][tall + c * rows : tall + (c + 1) * rows]
        table[at] = refs[k][2 * tall :]
    fold = D // tall
    for i in range(count // fold):
        line = table[fold * i][:1].astype(f32)
        for r in range(1, fold):
            line += table[fold * i + r][r : r + 1].astype(f32)
        bias_ref[:, i * D : (i + 1) * D] = line


def merge_kernel(keep_ref, got_ref, own_ref, *sends):
    for k in range(keep_ref.shape[0]):
        total = keep_ref[k].astype(f32) + got_ref[k].astype(f32)
        if k == 0:
            own_ref[...] = total
        else:
            sends[k - 1][...] = total.astype(bf16)


def deal_kernel(keep_ref, got_ref, own_ref, send_ref):
    for k in range(keep_ref.shape[0]):
        total = (keep_ref[k].astype(f32) + got_ref[k].astype(f32)).astype(bf16)
        if k % 2 == 0:
            own_ref[k // 2] = total
        else:
            send_ref[k // 2] = total


def total_kernel(own_ref, *refs):
    total = own_ref[...].astype(f32)
    for ref in refs[:-1]:
        total += ref[...].astype(f32)
    refs[-1][...] = total.astype(refs[-1].dtype).reshape(refs[-1].shape)


def finish_kernel(groups, me_ref, *refs):
    terms, (qkv_ref, out_ref, router_ref, one_ref, two_ref) = refs[:-5], refs[-5:]
    mine = sum(ref[...].astype(f32) for ref in terms[0::2])
    other = sum(ref[...].astype(f32) for ref in terms[1::2])

    def write(left, right):
        joined = join_halves(left, right, 4 * D + LANES)
        qkv_ref[...] = joined[:, : 3 * D]
        out_ref[...] = joined[:, 3 * D : 4 * D]
        side = jnp.transpose(joined[:, 4 * D :])
        router_ref[...] = side[:groups]
        one_ref[...] = side[groups : groups + 1]
        two_ref[...] = side[groups + 1 : groups + 2]

    @pl.when((me_ref[0] & 1) == 0)
    def _():
        write(mine, other)

    @pl.when((me_ref[0] & 1) == 1)
    def _():
        write(other, mine)


def first_total_kernel(*refs):
    rows = refs[-2].shape[1]
    total = sum(ref[...].astype(f32) for ref in refs[:-2])
    refs[-2][0] = total[:rows]
    refs[-1][...] = total[rows:]


def params():
    return pltpu.CompilerParams(vmem_limit_bytes=VMEM_BYTES)


def whole(shape):
    zeros = (0,) * len(shape)
    return pl.BlockSpec(tuple(shape), lambda i: zeros)


def of_batch(shape, batch):
    tail = (0,) * (len(shape) - 1)
    return pl.BlockSpec((1,) + tuple(shape[1:]), lambda i: (batch,) + tail)


SCALAR = pl.BlockSpec(memory_space=pltpu.SMEM)


def call(kernel, name, outs, args, us, in_specs=None, scratch=(), out_specs=None, aliases=None):
    if in_specs is None:
        in_specs = [SCALAR if a.dtype == jnp.int32 else whole(a.shape) for a in args]
    moved = sum(a.size * a.dtype.itemsize for a in args)
    moved += sum(a.size * a.dtype.itemsize for a in outs)
    return pl.pallas_call(
        kernel,
        grid=(1,),
        in_specs=in_specs,
        out_specs=out_specs or [whole(o.shape) for o in outs],
        input_output_aliases=aliases or {},
        out_shape=outs,
        scratch_shapes=list(scratch),
        compiler_params=params(),
        cost_estimate=pl.CostEstimate(flops=int(us * 1e9), bytes_accessed=moved, transcendentals=0),
        name=name,
    )(*args)


def like(shape, dtype):
    return jax.ShapeDtypeStruct(tuple(shape), dtype)


def send(value, axis, k):
    return lax.ppermute(value, axis, xor_pairs(lax.axis_size(axis), k))


def after(value, *earlier):
    return lax.optimization_barrier((value,) + earlier)[0]


def sum_rest(keep, got, axis):
    shape = keep.shape[1:]
    count = keep.shape[0]
    merged = call(
        merge_kernel,
        "merge",
        [like(shape, f32)] + [like(shape, bf16)] * (count - 1),
        [keep, got],
        2,
    )
    return [merged[0]] + [send(merged[k], axis, 2 * k) for k in reversed(range(1, count))]


def body(
    tokens,
    expert_index,
    expert_slot,
    route_kept,
    ln1_gain,
    w_qkv,
    w_out,
    ln2_gain,
    w_router,
    expert_in,
    expert_bias,
    expert_out,
    cotangent,
):
    groups = lax.axis_size("expert")
    owners = lax.axis_size("dp")
    capacity = 8 * (5 * SEQ // (16 * groups) + 1)
    slots = groups * capacity
    wide = expert_in.shape[2]
    rows = w_qkv.shape[0]
    tall = expert_out.shape[1]
    dense_width = 4 * D + LANES
    half = half_width(dense_width)
    me = jnp.stack([lax.axis_index("expert"), lax.axis_index("dp")]).astype(jnp.int32)
    fold = D // tall
    bias_rows = jnp.pad(
        (jnp.eye(fold, dtype=bf16)[:, :, None] * expert_bias[0]).reshape(fold, D),
        ((0, 16 - fold), (0, 0)),
    )
    own_half, own_pack = call(
        pack_kernel,
        "pack",
        [like((rows, half), bf16), like((2 * tall + 16, D), bf16)],
        [me, w_qkv, w_out, w_router.T, ln1_gain[None], ln2_gain[None], expert_in, expert_out, bias_rows],
        2,
    )
    far = sorted(range(2, owners, 2), reverse=True)
    halves = [own_half] + [None] * (owners - 1)
    for k in far:
        halves[k] = send(own_half, "dp", k)
    halves[1] = send(own_half, "dp", 1)
    for k in far:
        halves[k + 1] = send(halves[k], "dp", 1)
    packs = [own_pack] + [None] * (owners - 1)
    packs[1] = send(own_pack, "dp", 1)
    own_late = after(own_pack, *[halves[k] for k in far])
    direct = [k for k in far if k == 2 or k >= 4 and k % 4 == 0]
    for k in direct:
        packs[k] = send(own_late, "dp", k)
    mine = call(
        functools.partial(arrange_kernel, owners),
        "arrange",
        [like((owners, rows, half), bf16)],
        [me] + halves,
        2,
    )[0].reshape(D, half)
    other = send(mine, "expert", 1)
    dense = call(join_kernel, "join", [like((D, dense_width), bf16)], [me, mine, other], 2)[0]

    routes = [jnp.swapaxes(a, 2, 3) for a in (expert_index, expert_slot, route_kept)]
    state = []
    boxes = []
    for m in range(MB):
        shared = [tokens] + routes + [cotangent]
        outs = call(
            functools.partial(forward_kernel, groups, capacity),
            "forward",
            [
                like((SEQ, 3 * D), bf16),
                like((HEADS, SEQ, SEQ), bf16),
                like((SEQ, D), bf16),
                like((SEQ, D), f32),
                like((SEQ, groups), f32),
            ]
            + [like((2 * capacity, D), bf16)] * groups,
            [me] + shared + [dense],
            4,
            in_specs=[SCALAR] + [of_batch(a.shape, m) for a in shared] + [whole(dense.shape)],
        )
        state.append(outs[:5])
        sends = outs[5:]
        boxes.append(
            [sends[0]] + [send(sends[k], "expert", k) for k in reversed(range(1, groups))][::-1]
        )
    for k in direct:
        late = after(packs[k], state[0][4])
        if k + 2 < owners and k >= 4:
            packs[k + 2] = send(late, "dp", 2)
        packs[k + 1] = send(late, "dp", 1)
    for k in far:
        if k not in direct:
            packs[k + 1] = send(after(packs[k], state[1][4]), "dp", 1)
    first, second, bias = call(
        functools.partial(unpack_kernel, owners),
        "unpack",
        [
            like((owners, rows, wide), bf16),
            like((owners, tall, D), bf16),
            like((1, wide), f32),
        ],
        [me] + packs,
        4,
        scratch=[pltpu.VMEM((owners, 16, D), bf16)],
    )
    first = first.reshape(D, wide)
    second = second.reshape(wide, D)

    actives, hiddens, returned = [], [], []
    for m in range(MB):
        outs = call(
            functools.partial(expert_kernel, groups, capacity),
            "experts",
            [like((2 * capacity, D), bf16)] * groups + [like((slots, wide), bf16)] * 2,
            list(boxes[m]) + [first, bias, second],
            5,
        )
        actives.append(outs[groups])
        hiddens.append(outs[groups + 1])
        returned.append(
            [outs[0]] + [send(outs[k], "expert", k) for k in reversed(range(1, groups))][::-1]
        )
    all_boxes = [box for m in range(MB) for box in boxes[m]]
    second_keep, second_send = call(
        functools.partial(second_grad_kernel, groups, capacity, owners),
        "second_grad",
        [like((owners // 2, tall, D), bf16)] * 2,
        [me] + all_boxes + actives,
        5,
    )
    second_got = send(second_send, "dp", 1)
    first_keep, first_send = call(
        functools.partial(first_grad_kernel, groups, capacity, owners),
        "first_grad",
        [like((owners // 2, rows + 8, wide), bf16)] * 2,
        [after(me, second_send)] + all_boxes + hiddens,
        5,
    )

    output = token_grads = total = None
    gates_to = [first_send, None, None]
    for m in range(MB):
        last = m == MB - 1
        shared = [tokens] + routes + [cotangent]
        dense_late = dense if gates_to[m] is None else after(dense, gates_to[m])
        rest = [dense_late] + list(state[m]) + list(returned[m]) + ([] if m == 0 else [total])
        carried = [] if m == 0 else [output, token_grads]
        at = 1 + len(shared) + len(rest)
        outs = call(
            functools.partial(backward_kernel, groups, capacity, m > 0, last),
            "backward",
            [like(tokens.shape, bf16), like(tokens.shape, f32)]
            + (
                [like((owners, rows, half), bf16)] * 2
                if last
                else [like((D, dense_width), f32)]
            ),
            [me] + shared + rest + carried,
            7,
            in_specs=[SCALAR]
            + [of_batch(a.shape, m) for a in shared]
            + [whole(a.shape) for a in rest]
            + [pl.BlockSpec(memory_space=pl.ANY)] * len(carried),
            out_specs=[of_batch(tokens.shape, m)] * 2
            + [whole((owners, rows, half))] * 2 * last
            + [whole((D, dense_width))] * (not last),
            aliases={} if m == 0 else {at: 0, at + 1: 1},
        )
        output, token_grads, total = outs[:3]
        dense_send = outs[-1]
        if m == 1:
            second_got = after(second_got, total)
            second_terms = sum_rest(second_keep, second_got, "dp")
            first_got = send(after(first_send, second_got), "dp", 1)
            gates_to[2] = second_terms[0]
    keep, share = call(
        deal_kernel,
        "deal",
        [like((owners // 2, rows, half), bf16)] * 2,
        [total, send(dense_send, "expert", 1)],
        2,
    )
    dense_got = send(share, "dp", 1)
    first_terms = sum_rest(first_keep, after(first_got, share), "dp")
    dense_terms = sum_rest(keep, dense_got, "dp")
    reduced = call(total_kernel, "total", [like((rows, half), bf16)], dense_terms, 1)[0]
    spread = [reduced] + [send(reduced, "expert", k) for k in range(1, groups)]
    d_qkv, d_out, d_router, d_one, d_two = call(
        functools.partial(finish_kernel, groups),
        "finish",
        [
            like((rows, 3 * D), f32),
            like((rows, D), f32),
            like((groups, rows), f32),
            like((1, rows), f32),
            like((1, rows), f32),
        ],
        [me] + spread,
        1,
    )
    d_second = call(total_kernel, "total", [like((1, tall, D), f32)], second_terms, 1)[0]
    d_first, d_biases = call(
        first_total_kernel,
        "total",
        [like((1, rows, wide), f32), like((8, wide), f32)],
        first_terms,
        1,
    )
    d_bias = lax.dynamic_slice(d_biases, (0, me[1] * tall), (1, tall))
    return (
        output,
        token_grads,
        d_one[0],
        d_qkv,
        d_out,
        d_two[0],
        d_router.T,
        d_first,
        d_bias,
        d_second,
    )


def solution(mesh):
    images = P(None, ("dp", "expert"), None, None)
    weights = (
        P("dp"),
        P("dp", None),
        P("dp", None),
        P("dp"),
        P("dp", None),
        P("expert", "dp", None),
        P("expert", "dp"),
        P("expert", "dp", None),
    )
    return jax.shard_map(
        body,
        mesh=mesh,
        in_specs=(images,) * 4 + weights + (images,),
        out_specs=(images, images) + weights,
        check_vma=False,
    )
```

```python
import functools

import jax
import jax.numpy as jnp
from jax import lax
from jax.experimental import pallas as pl
from jax.experimental.pallas import tpu as pltpu
from jax.sharding import PartitionSpec as P

HEADS = 6
HEAD_DIM = 64
D = 384
SEQ = 197
MB = 3
LANES = 128
EPSILON = 1e-06
HIGHEST = lax.Precision.HIGHEST
VMEM_BYTES = 24 * 1024 * 1024
bf16 = jnp.bfloat16
f32 = jnp.float32


def dot(a, b, ca=1, cb=0, precision=None):
    return lax.dot_general(
        a, b, (((ca,), (cb,)), ((), ())), precision=precision, preferred_element_type=f32
    )


def xor_pairs(n, k):
    return [(i, i ^ k) for i in range(n)]


def spread_of(values):
    centre = jnp.mean(values, axis=-1, keepdims=True)
    centered = values - centre
    spread = jnp.mean(centered * centered, axis=-1, keepdims=True)
    rate = lax.rsqrt(spread + EPSILON)
    return centered * rate, rate


def norm_back(grad_hat, hat, rate):
    mean_one = jnp.mean(grad_hat, axis=-1, keepdims=True)
    mean_two = jnp.mean(grad_hat * hat, axis=-1, keepdims=True)
    return rate * (grad_hat - mean_one - hat * mean_two)


def side_rows(dense_ref):
    return jnp.transpose(dense_ref[:, 4 * D :].astype(f32))


def route_masks(index_ref, slot_ref, kept_ref, me, groups, capacity):
    index = index_ref[0, 0]
    target = jnp.where(kept_ref[0, 0] > 0, (index ^ me) * capacity + slot_ref[0, 0], -1)
    both = jnp.transpose(jnp.concatenate([index, target], axis=0).astype(f32)).astype(jnp.int32)
    index, target = both[:, :2], both[:, 2:]
    lanes = lax.broadcasted_iota(jnp.int32, (SEQ, groups * capacity), 1)
    places = [(lanes == target[:, k : k + 1]).astype(f32).astype(bf16) for k in range(2)]
    experts = lax.broadcasted_iota(jnp.int32, (SEQ, groups), 1)
    chosen = [(experts == index[:, k : k + 1]).astype(f32) for k in range(2)]
    return places, chosen


def half_mask(which):
    lanes = lax.broadcasted_iota(jnp.int32, (SEQ, LANES), 1)
    return (lanes < HEAD_DIM) if which == 0 else (lanes >= HEAD_DIM)


def forward_kernel(groups, capacity, me_ref, tokens_ref, index_ref, slot_ref, kept_ref, cot_ref, dense_ref, packed_ref, attn_ref, attended_ref, middle_ref, router_ref, *sends):
    me = me_ref[0]
    side = side_rows(dense_ref)
    gain_one = side[groups : groups + 1]
    gain_two = side[groups + 1 : groups + 2]
    inputs = tokens_ref[0, 0].astype(f32)
    hat, _ = spread_of(inputs)
    normed_low = (hat * gain_one).astype(bf16)
    packed = dot(normed_low, dense_ref[:, : 3 * D]).astype(bf16)
    packed_ref[...] = packed
    scale = HEAD_DIM ** (-0.5)
    parts = []
    for pair in range(HEADS // 2):
        lo = pair * LANES
        query = packed[:, lo : lo + LANES]
        keyed = packed[:, D + lo : D + lo + LANES]
        valued = packed[:, 2 * D + lo : 2 * D + lo + LANES]
        outs = []
        for which in range(2):
            masked = jnp.where(half_mask(which), query, jnp.zeros_like(query))
            scores = dot(masked, keyed, 1, 1) * scale
            top = jnp.max(scores, axis=-1, keepdims=True)
            raised = jnp.exp(scores - top)
            total = jnp.sum(raised, axis=-1, keepdims=True)
            attn_low = (raised * (1.0 / total)).astype(bf16)
            attn_ref[2 * pair + which] = attn_low
            outs.append(dot(attn_low, valued))
        parts.append(jnp.where(half_mask(0), outs[0], outs[1]))
    attended = jnp.concatenate(parts, axis=1).astype(bf16)
    attended_ref[...] = attended
    middle = inputs + dot(attended, dense_ref[:, 3 * D : 4 * D])
    middle_ref[...] = middle
    hat_two, _ = spread_of(middle)
    normed_two = hat_two * gain_two
    router_w = dense_ref[:, 4 * D :].astype(f32)[:, :groups]
    logits = dot(normed_two, router_w, precision=HIGHEST)
    raised = jnp.exp(logits - jnp.max(logits, axis=-1, keepdims=True))
    router = raised / jnp.sum(raised, axis=-1, keepdims=True)
    router_ref[...] = router
    places, chosen = route_masks(index_ref, slot_ref, kept_ref, me, groups, capacity)
    cot = cot_ref[0, 0].astype(f32)
    inbox = dot(places[0] + places[1], normed_two.astype(bf16), 0, 0).astype(bf16)
    grad_outbox = jnp.zeros((groups * capacity, D), f32)
    for k in range(2):
        gate = jnp.sum(chosen[k] * router, axis=-1, keepdims=True)
        grad_outbox += dot(places[k], (gate * cot).astype(bf16), 0, 0)
    grad_outbox = grad_outbox.astype(bf16)
    for g in range(groups):
        sends[g][:capacity] = inbox[g * capacity : (g + 1) * capacity]
        sends[g][capacity:] = grad_outbox[g * capacity : (g + 1) * capacity]


def expert_kernel(groups, capacity, *refs):
    boxes = refs[:groups]
    first_ref, bias_ref, second_ref = refs[groups : groups + 3]
    backs = refs[groups + 3 : 2 * groups + 3]
    active_ref, grad_hidden_ref = refs[2 * groups + 3 :]
    inbox = jnp.concatenate([box[:capacity] for box in boxes], axis=0)
    grad_outbox = jnp.concatenate([box[capacity:] for box in boxes], axis=0)
    wide = first_ref.shape[1]
    step = wide // 3
    outbox = jnp.zeros((groups * capacity, D), f32)
    grad_inbox = jnp.zeros((groups * capacity, D), f32)
    for at in range(0, wide, step):
        first = first_ref[:, at : at + step]
        second = second_ref[at : at + step, :]
        hidden = dot(inbox, first) + bias_ref[:, at : at + step].astype(f32)
        cdf = 0.5 + 0.5 * lax.erf(hidden * (0.5**0.5))
        density = jnp.exp(hidden * hidden * (-0.5)) * 0.3989422804014327
        active = (hidden * cdf).astype(bf16)
        grad_active = dot(grad_outbox, second, 1, 1)
        grad_hidden = ((cdf + hidden * density) * grad_active).astype(bf16)
        active_ref[:, at : at + step] = active
        grad_hidden_ref[:, at : at + step] = grad_hidden
        outbox += dot(active, second)
        grad_inbox += dot(grad_hidden, first, 1, 1)
    outbox = outbox.astype(bf16)
    grad_inbox = grad_inbox.astype(bf16)
    for g in range(groups):
        backs[g][:capacity] = outbox[g * capacity : (g + 1) * capacity]
        backs[g][capacity:] = grad_inbox[g * capacity : (g + 1) * capacity]


def place(keep_ref, send_ref, at, value):
    @pl.when((at & 1) == 0)
    def _():
        keep_ref[at >> 1] = value

    @pl.when((at & 1) == 1)
    def _():
        send_ref[at >> 1] = value


def second_grad_kernel(groups, capacity, owners, me_ref, *refs):
    boxes = [refs[m * groups : (m + 1) * groups] for m in range(MB)]
    actives = refs[MB * groups : MB * groups + MB]
    keep_ref, send_ref = refs[-2:]
    rows = keep_ref.shape[1]
    grads = [
        jnp.concatenate([box[capacity:] for box in boxes[m]], axis=0) for m in range(MB)
    ]
    wide = owners * rows
    step = wide // 2
    for at in range(0, wide, step):
        total = dot(actives[0][:, at : at + step], grads[0], 0, 0)
        for m in range(1, MB):
            total += dot(actives[m][:, at : at + step], grads[m], 0, 0)
        for j in range(step // rows):
            part = total[j * rows : (j + 1) * rows].astype(bf16)
            place(keep_ref, send_ref, (at // rows + j) ^ me_ref[1], part)


def first_grad_kernel(groups, capacity, owners, me_ref, *refs):
    boxes = [refs[m * groups : (m + 1) * groups] for m in range(MB)]
    hiddens = refs[MB * groups : MB * groups + MB]
    keep_ref, send_ref = refs[-2:]
    rows = D // owners
    extra = keep_ref.shape[1] - rows
    inboxes = [
        jnp.concatenate([box[:capacity] for box in boxes[m]], axis=0) for m in range(MB)
    ]
    wide = keep_ref.shape[2]
    step = wide // 3
    totals, biases = [], []
    for at in range(0, wide, step):
        total = dot(inboxes[0], hiddens[0][:, at : at + step], 0, 0)
        bias = jnp.sum(hiddens[0][:, at : at + step].astype(f32), axis=0, keepdims=True)
        for m in range(1, MB):
            total += dot(inboxes[m], hiddens[m][:, at : at + step], 0, 0)
            bias += jnp.sum(hiddens[m][:, at : at + step].astype(f32), axis=0, keepdims=True)
        totals.append(total)
        biases.append(jnp.broadcast_to(bias, (extra, step)))
    for j in range(owners):
        part = jnp.concatenate(
            [
                jnp.concatenate([total[j * rows : (j + 1) * rows], bias], axis=0)
                for total, bias in zip(totals, biases)
            ],
            axis=1,
        )
        place(keep_ref, send_ref, j ^ me_ref[1], part.astype(bf16))


def backward_kernel(groups, capacity, has_total, last, me_ref, tokens_ref, index_ref, slot_ref, kept_ref, cot_ref, dense_ref, packed_ref, attn_ref, attended_ref, middle_ref, router_ref, *refs):
    backs = refs[:groups]
    total_ref = refs[groups] if has_total else None
    if last:
        output_ref, d_tokens_ref, keep_ref, send_ref = refs[-4:]
    else:
        output_ref, d_tokens_ref, grads_ref = refs[-3:]
    me = me_ref[0]
    side = side_rows(dense_ref)
    gain_one = side[groups : groups + 1]
    gain_two = side[groups + 1 : groups + 2]
    middle = middle_ref[...]
    router = router_ref[...]
    cot = cot_ref[0, 0].astype(f32)
    places, chosen = route_masks(index_ref, slot_ref, kept_ref, me, groups, capacity)
    outbox = jnp.concatenate([box[:capacity] for box in backs], axis=0)
    grad_inbox = jnp.concatenate([box[capacity:] for box in backs], axis=0)
    mixed = middle
    grad_router = jnp.zeros((SEQ, groups), f32)
    for k in range(2):
        picked = dot(places[k], outbox)
        gate = jnp.sum(chosen[k] * router, axis=-1, keepdims=True)
        mixed = mixed + gate * picked
        grad_router += chosen[k] * jnp.sum(cot * picked, axis=-1, keepdims=True)
    output_ref[0, 0] = mixed.astype(bf16)
    grad_logits = router * (grad_router - jnp.sum(router * grad_router, axis=-1, keepdims=True))
    router_w = dense_ref[:, 4 * D :].astype(f32)[:, :groups]
    grad_normed_two = dot(grad_logits, router_w, 1, 1, precision=HIGHEST) + dot(
        places[0] + places[1], grad_inbox
    )
    hat_two, rate_two = spread_of(middle)
    grad_middle = norm_back(grad_normed_two * gain_two, hat_two, rate_two) + cot
    lanes = lax.broadcasted_iota(jnp.int32, (SEQ, LANES), 1)
    column_one = (lanes == groups).astype(f32)
    column_two = (lanes == groups + 1).astype(f32)
    logits_wide = sum(
        jnp.where(lanes == e, grad_logits[:, e : e + 1], 0.0) for e in range(groups)
    )
    side_grad = dot(hat_two * gain_two, logits_wide, 0, 0, precision=HIGHEST)
    side_grad += dot(grad_normed_two * hat_two, column_two, 0, 0, precision=HIGHEST)
    grad_branch = grad_middle.astype(bf16)
    out_grad = dot(attended_ref[...], grad_branch, 0, 0)
    grad_attended = dot(grad_branch, dense_ref[:, 3 * D : 4 * D], 1, 1).astype(bf16)
    scale = HEAD_DIM ** (-0.5)
    first_half = half_mask(0)
    queries, keys, values = [], [], []
    for pair in range(HEADS // 2):
        lo = pair * LANES
        query = packed_ref[:, lo : lo + LANES]
        keyed = packed_ref[:, D + lo : D + lo + LANES]
        valued = packed_ref[:, 2 * D + lo : 2 * D + lo + LANES]
        pulled = grad_attended[:, lo : lo + LANES]
        q_outs, k_outs, v_outs = [], [], []
        for which in range(2):
            attn_low = attn_ref[2 * pair + which]
            attn = attn_low.astype(f32)
            masked = jnp.where(half_mask(which), pulled, jnp.zeros_like(pulled))
            weighted = dot(masked, valued, 1, 1)
            inner = jnp.sum(attn * weighted, axis=-1, keepdims=True)
            grad_scores = (attn * (weighted - inner)).astype(bf16)
            v_outs.append(dot(attn_low, pulled, 0, 0))
            q_outs.append(dot(grad_scores, keyed))
            k_outs.append(dot(grad_scores, query, 0, 0))
        queries.append(jnp.where(first_half, q_outs[0], q_outs[1]) * scale)
        keys.append(jnp.where(first_half, k_outs[0], k_outs[1]) * scale)
        values.append(jnp.where(first_half, v_outs[0], v_outs[1]))
    grad_packed = jnp.concatenate(queries + keys + values, axis=1).astype(bf16)
    grad_normed = dot(grad_packed, dense_ref[:, : 3 * D], 1, 1)
    hat, rate = spread_of(tokens_ref[0, 0].astype(f32))
    packed_grad = dot((hat * gain_one).astype(bf16), grad_packed, 0, 0)
    side_grad += dot(grad_normed * hat, column_one, 0, 0, precision=HIGHEST)
    d_tokens_ref[0, 0] = grad_middle + norm_back(grad_normed * gain_one, hat, rate)
    pieces = []
    for lo, part in ((0, packed_grad), (3 * D, out_grad), (4 * D, side_grad)):
        hi = lo + part.shape[1]
        if has_total:
            part = part + total_ref[:, lo:hi]
        pieces.append(part)
        if not last:
            grads_ref[:, lo:hi] = part
    if last:
        joined = jnp.concatenate(pieces, axis=1).astype(bf16)
        left, right = split_halves(joined)
        core = me & 1
        rows = keep_ref.shape[1]
        for j in range(keep_ref.shape[0]):
            at = j ^ me_ref[1]
            cut = slice(j * rows, (j + 1) * rows)

            @pl.when(core == 0)
            def _(at=at, cut=cut):
                keep_ref[at] = left[cut]
                send_ref[at] = right[cut]

            @pl.when(core == 1)
            def _(at=at, cut=cut):
                keep_ref[at] = right[cut]
                send_ref[at] = left[cut]


def split_halves(joined):
    half = half_width(joined.shape[1])
    return joined[:, :half], joined[:, joined.shape[1] - half :]


def half_width(width):
    return -(-width // (2 * LANES)) * LANES


def join_halves(left, right, width):
    half = left.shape[1]
    return jnp.concatenate([left, right[:, 2 * half - width :]], axis=1)


def pack_kernel(me_ref, router_ref, one_ref, two_ref, bias_ref, qkv_hbm, out_hbm, first_hbm, second_hbm, half_ref, pack_ref, qkv_ref, out_ref, first_ref, second_ref, sems):
    copies = [
        pltpu.make_async_copy(source, target, sems.at[i])
        for i, (source, target) in enumerate(
            [
                (qkv_hbm, qkv_ref),
                (out_hbm, out_ref),
                (first_hbm, first_ref),
                (second_hbm, second_ref),
            ]
        )
    ]
    for copy in copies:
        copy.start()
    rows = qkv_ref.shape[0]
    lines = [router_ref[...].astype(f32), one_ref[...].astype(f32), two_ref[...].astype(f32)]
    used = sum(line.shape[0] for line in lines)
    lines.append(jnp.zeros((LANES - used, rows), f32))
    side = jnp.transpose(jnp.concatenate(lines, axis=0)).astype(bf16)
    copies[0].wait()
    copies[1].wait()
    joined = jnp.concatenate([qkv_ref[...], out_ref[...], side], axis=1)
    left, right = split_halves(joined)

    @pl.when((me_ref[0] & 1) == 0)
    def _():
        half_ref[...] = left

    @pl.when((me_ref[0] & 1) == 1)
    def _():
        half_ref[...] = right

    tall = second_ref.shape[1]
    fold = D // tall
    at_row = lax.broadcasted_iota(jnp.int32, (tall, D), 0)
    at_lane = lax.broadcasted_iota(jnp.int32, (tall, D), 1)
    line_at = lax.broadcasted_iota(jnp.int32, (16, D), 0)
    lines = jnp.zeros((16, D), f32)
    for r in range(fold):
        spots = (at_lane == at_row + r * tall).astype(f32).astype(bf16)
        lines = jnp.where(line_at == r, dot(bias_ref[...], spots), lines)
    pack_ref[2 * tall :] = lines.astype(bf16)
    copies[2].wait()
    copies[3].wait()
    pack_ref[:tall] = second_ref[0]
    for c in range(first_ref.shape[2] // D):
        pack_ref[tall + c * rows : tall + (c + 1) * rows] = first_ref[0, :, c * D : (c + 1) * D]


def arrange_kernel(count, me_ref, *refs):
    out_ref = refs[-1]
    for k in range(count):
        out_ref[me_ref[1] ^ k] = refs[k][...]


def join_kernel(me_ref, mine_ref, other_ref, out_ref):
    width = out_ref.shape[1]

    @pl.when((me_ref[0] & 1) == 0)
    def _():
        out_ref[...] = join_halves(mine_ref[...], other_ref[...], width)

    @pl.when((me_ref[0] & 1) == 1)
    def _():
        out_ref[...] = join_halves(other_ref[...], mine_ref[...], width)


def unpack_kernel(count, me_ref, *refs):
    first_ref, second_ref, bias_ref, table = refs[count:]
    rows = first_ref.shape[1]
    tall = second_ref.shape[1]
    for k in range(count):
        at = me_ref[1] ^ k
        second_ref[at] = refs[k][:tall]
        for c in range(first_ref.shape[2] // D):
            first_ref[at, :, c * D : (c + 1) * D] = refs[k][tall + c * rows : tall + (c + 1) * rows]
        table[at] = refs[k][2 * tall :]
    fold = D // tall
    for i in range(count // fold):
        line = table[fold * i][:1].astype(f32)
        for r in range(1, fold):
            line += table[fold * i + r][r : r + 1].astype(f32)
        bias_ref[:, i * D : (i + 1) * D] = line


def merge_kernel(keep_ref, got_ref, own_ref, *sends):
    for k in range(keep_ref.shape[0]):
        total = keep_ref[k].astype(f32) + got_ref[k].astype(f32)
        if k == 0:
            own_ref[...] = total
        else:
            sends[k - 1][...] = total.astype(bf16)


def deal_kernel(keep_ref, got_ref, own_ref, send_ref):
    for k in range(keep_ref.shape[0]):
        total = (keep_ref[k].astype(f32) + got_ref[k].astype(f32)).astype(bf16)
        if k % 2 == 0:
            own_ref[k // 2] = total
        else:
            send_ref[k // 2] = total


def total_kernel(own_ref, *refs):
    total = own_ref[...].astype(f32)
    for ref in refs[:-1]:
        total += ref[...].astype(f32)
    refs[-1][...] = total.astype(refs[-1].dtype).reshape(refs[-1].shape)


def finish_kernel(groups, me_ref, *refs):
    terms, (qkv_ref, out_ref, router_ref, one_ref, two_ref) = refs[:-5], refs[-5:]
    mine = sum(ref[...].astype(f32) for ref in terms[0::2])
    other = sum(ref[...].astype(f32) for ref in terms[1::2])

    def write(left, right):
        joined = join_halves(left, right, 4 * D + LANES)
        qkv_ref[...] = joined[:, : 3 * D]
        out_ref[...] = joined[:, 3 * D : 4 * D]
        side = jnp.transpose(joined[:, 4 * D :])
        router_ref[...] = side[:groups]
        one_ref[...] = side[groups : groups + 1]
        two_ref[...] = side[groups + 1 : groups + 2]

    @pl.when((me_ref[0] & 1) == 0)
    def _():
        write(mine, other)

    @pl.when((me_ref[0] & 1) == 1)
    def _():
        write(other, mine)


def first_total_kernel(*refs):
    rows = refs[-2].shape[1]
    total = sum(ref[...].astype(f32) for ref in refs[:-2])
    refs[-2][0] = total[:rows]
    refs[-1][...] = total[rows:]


def whole(shape):
    zeros = (0,) * len(shape)
    return pl.BlockSpec(tuple(shape), lambda i: zeros)


def of_batch(shape, batch):
    tail = (0,) * (len(shape) - 1)
    return pl.BlockSpec((1,) + tuple(shape[1:]), lambda i: (batch,) + tail)


SCALAR = pl.BlockSpec(memory_space=pltpu.SMEM)
FAR = pltpu.HBM


def call(kernel, name, outs, args, us, in_specs=None, scratch=(), out_specs=None, aliases=None, vmem=VMEM_BYTES):
    if in_specs is None:
        in_specs = [SCALAR if a.dtype == jnp.int32 else whole(a.shape) for a in args]
    moved = sum(a.size * a.dtype.itemsize for a in args)
    moved += sum(a.size * a.dtype.itemsize for a in outs)
    return pl.pallas_call(
        kernel,
        grid=(1,),
        in_specs=in_specs,
        out_specs=out_specs or [whole(o.shape) for o in outs],
        input_output_aliases=aliases or {},
        out_shape=outs,
        scratch_shapes=list(scratch),
        compiler_params=pltpu.CompilerParams(vmem_limit_bytes=vmem),
        cost_estimate=pl.CostEstimate(flops=int(us * 1e+09), bytes_accessed=moved, transcendentals=0),
        name=name,
    )(*args)


def like(shape, dtype):
    return jax.ShapeDtypeStruct(tuple(shape), dtype)


def send(value, axis, k):
    return lax.ppermute(value, axis, xor_pairs(lax.axis_size(axis), k))


def after(value, *earlier):
    return lax.optimization_barrier((value,) + earlier)[0]


def sum_rest(keep, got, axis):
    shape = keep.shape[1:]
    count = keep.shape[0]
    merged = call(
        merge_kernel,
        "merge",
        [like(shape, f32)] + [like(shape, bf16)] * (count - 1),
        [keep, got],
        2,
    )
    return [merged[0]] + [send(merged[k], axis, 2 * k) for k in reversed(range(1, count))]


def deal(keep, got, us=2):
    shape = (keep.shape[0] // 2,) + keep.shape[1:]
    return call(deal_kernel, "deal", [like(shape, bf16)] * 2, [keep, got], us)


def body(
    tokens,
    expert_index,
    expert_slot,
    route_kept,
    ln1_gain,
    w_qkv,
    w_out,
    ln2_gain,
    w_router,
    expert_in,
    expert_bias,
    expert_out,
    cotangent,
):
    groups = lax.axis_size("expert")
    owners = lax.axis_size("dp")
    capacity = 8 * (5 * SEQ // (16 * groups) + 1)
    slots = groups * capacity
    wide = expert_in.shape[2]
    rows = w_qkv.shape[0]
    tall = expert_out.shape[1]
    dense_width = 4 * D + LANES
    half = half_width(dense_width)
    me = jnp.stack([lax.axis_index("expert"), lax.axis_index("dp")]).astype(jnp.int32)
    far_args = [w_qkv, w_out, expert_in, expert_out]
    near_args = [me, w_router.T, ln1_gain[None], ln2_gain[None], expert_bias]
    own_half, own_pack = call(
        pack_kernel,
        "pack",
        [like((rows, half), bf16), like((2 * tall + 16, D), bf16)],
        near_args + far_args,
        2,
        in_specs=[SCALAR]
        + [whole(a.shape) for a in near_args[1:]]
        + [pl.BlockSpec(memory_space=FAR)] * len(far_args),
        scratch=[pltpu.VMEM(a.shape, a.dtype) for a in far_args]
        + [pltpu.SemaphoreType.DMA((len(far_args),))],
        vmem=60 * 1024 * 1024,
    )
    far = sorted(range(2, owners, 2), reverse=True)
    halves = [own_half] + [None] * (owners - 1)
    for k in far:
        halves[k] = send(own_half, "dp", k)
    halves[1] = send(own_half, "dp", 1)
    for k in far:
        halves[k + 1] = send(halves[k], "dp", 1)
    packs = [own_pack] + [None] * (owners - 1)
    packs[1] = send(own_pack, "dp", 1)
    own_late = after(own_pack, *[halves[k] for k in far])
    direct = [k for k in far if k == 2 or k >= 4 and k % 4 == 0]
    for k in direct:
        packs[k] = send(own_late, "dp", k)
    mine = call(
        functools.partial(arrange_kernel, owners),
        "arrange",
        [like((owners, rows, half), bf16)],
        [after(me, packs[1])] + halves,
        2,
    )[0].reshape(D, half)
    other = send(mine, "expert", 1)
    dense = call(join_kernel, "join", [like((D, dense_width), bf16)], [me, mine, other], 2)[0]

    routes = [
        after(jnp.swapaxes(a, 2, 3), halves[far[0]])
        for a in (expert_index, expert_slot, route_kept)
    ]
    state = []
    boxes = []
    for m in range(MB):
        shared = [tokens] + routes + [cotangent]
        ready = after(dense, packs[direct[0]], *boxes[0]) if m == MB - 1 else dense
        ready = after(dense, state[0][4]) if m == 1 else ready
        outs = call(
            functools.partial(forward_kernel, groups, capacity),
            "forward",
            [
                like((SEQ, 3 * D), bf16),
                like((HEADS, SEQ, SEQ), bf16),
                like((SEQ, D), bf16),
                like((SEQ, D), f32),
                like((SEQ, groups), f32),
            ]
            + [like((2 * capacity, D), bf16)] * groups,
            [me] + shared + [ready],
            4,
            in_specs=[SCALAR] + [of_batch(a.shape, m) for a in shared] + [whole(dense.shape)],
        )
        state.append(outs[:5])
        sends = outs[5:]
        boxes.append(
            [sends[0]] + [send(sends[k], "expert", k) for k in reversed(range(1, groups))][::-1]
        )
    for k in direct:
        late = after(packs[k], state[1][4])
        if k + 2 < owners and k >= 4:
            packs[k + 2] = send(late, "dp", 2)
        packs[k + 1] = send(late, "dp", 1)
    for k in far:
        if k not in direct:
            packs[k + 1] = send(after(packs[k], state[2][4]), "dp", 1)
    first, second, bias = call(
        functools.partial(unpack_kernel, owners),
        "unpack",
        [
            like((owners, rows, wide), bf16),
            like((owners, tall, D), bf16),
            like((1, wide), f32),
        ],
        [after(me, *boxes[1])] + packs,
        4,
        scratch=[pltpu.VMEM((owners, 16, D), bf16)],
    )
    first = first.reshape(D, wide)
    second = second.reshape(wide, D)

    actives, hiddens, returned = [], [], []
    for m in range(MB):
        outs = call(
            functools.partial(expert_kernel, groups, capacity),
            "experts",
            [like((2 * capacity, D), bf16)] * groups + [like((slots, wide), bf16)] * 2,
            list(boxes[m]) + [first, after(bias, hiddens[m - 1]) if m else bias, second],
            5,
        )
        actives.append(outs[groups])
        hiddens.append(outs[groups + 1])
        returned.append(
            [outs[0]] + [send(outs[k], "expert", k) for k in reversed(range(1, groups))][::-1]
        )
    all_boxes = [box for m in range(MB) for box in boxes[m]]
    second_keep, second_send = call(
        functools.partial(second_grad_kernel, groups, capacity, owners),
        "second_grad",
        [like((owners // 2, tall, D), bf16)] * 2,
        [me] + all_boxes + actives,
        5,
    )
    second_got = send(second_send, "dp", 1)
    first_keep, first_send = call(
        functools.partial(first_grad_kernel, groups, capacity, owners),
        "first_grad",
        [like((owners // 2, rows + 8, wide), bf16)] * 2,
        [after(me, second_send, *returned[0])] + all_boxes + hiddens,
        5,
    )

    first_got = send(first_send, "dp", 1)
    output = token_grads = total = None
    gates_to = [[first_send], [], []]
    for m in range(MB):
        last = m == MB - 1
        shared = [tokens] + routes + [cotangent]
        dense_late = after(dense, *gates_to[m]) if gates_to[m] else dense
        rest = [dense_late] + list(state[m]) + list(returned[m]) + ([] if m == 0 else [total])
        carried = [] if m == 0 else [output, token_grads]
        at = 1 + len(shared) + len(rest)
        outs = call(
            functools.partial(backward_kernel, groups, capacity, m > 0, last),
            "backward",
            [like(tokens.shape, bf16), like(tokens.shape, f32)]
            + (
                [like((owners, rows, half), bf16)] * 2
                if last
                else [like((D, dense_width), f32)]
            ),
            [me] + shared + rest + carried,
            7,
            in_specs=[SCALAR]
            + [of_batch(a.shape, m) for a in shared]
            + [whole(a.shape) for a in rest]
            + [pl.BlockSpec(memory_space=pl.ANY)] * len(carried),
            out_specs=[of_batch(tokens.shape, m)] * 2
            + [whole((owners, rows, half))] * 2 * last
            + [whole((D, dense_width))] * (not last),
            aliases={} if m == 0 else {at: 0, at + 1: 1},
        )
        output, token_grads, total = outs[:3]
        if m == MB - 2:
            second_keep, second_send = deal(second_keep, after(second_got, total))
            gates_to[m + 1] = [second_send]
        dense_send = outs[-1]
    second_got = send(second_send, "dp", 2)
    keep, share = deal(after(total, first_got), send(dense_send, "expert", 1))
    dense_got = send(share, "dp", 1)
    second_stage, first_stage = [second_keep, second_got], [first_keep, after(first_got, share)]
    first_keep, first_send = deal(*first_stage)
    bit = 2
    first_stage = [first_keep, send(first_send, "dp", bit)]
    while bit * 2 < owners:
        second_keep, second_send = deal(second_stage[0], after(second_stage[1], first_send), 1)
        second_stage = [second_keep, send(second_send, "dp", 2 * bit)]
        first_keep, first_send = deal(*first_stage, 1)
        bit *= 2
        first_stage = [first_keep, send(first_send, "dp", bit)]
    dense_terms = sum_rest(keep, dense_got, "dp")
    dense_terms[0] = after(dense_terms[0], first_send)
    reduced = call(total_kernel, "total", [like((rows, half), bf16)], dense_terms, 1)[0]
    spread = [reduced] + [send(reduced, "expert", k) for k in range(1, groups)]
    d_qkv, d_out, d_router, d_one, d_two = call(
        functools.partial(finish_kernel, groups),
        "finish",
        [
            like((rows, 3 * D), f32),
            like((rows, D), f32),
            like((groups, rows), f32),
            like((1, rows), f32),
            like((1, rows), f32),
        ],
        [me] + spread,
        1,
    )
    d_second = call(
        total_kernel, "total", [like((1, tall, D), f32)], [a[0] for a in second_stage], 1
    )[0]
    d_first, d_biases = call(
        first_total_kernel,
        "total",
        [like((1, rows, wide), f32), like((8, wide), f32)],
        [a[0] for a in first_stage],
        1,
    )
    d_bias = lax.dynamic_slice(d_biases, (0, me[1] * tall), (1, tall))
    return (
        output,
        token_grads,
        d_one[0],
        d_qkv,
        d_out,
        d_two[0],
        d_router.T,
        d_first,
        d_bias,
        d_second,
    )


def solution(mesh):
    images = P(None, ("dp", "expert"), None, None)
    weights = (
        P("dp"),
        P("dp", None),
        P("dp", None),
        P("dp"),
        P("dp", None),
        P("expert", "dp", None),
        P("expert", "dp"),
        P("expert", "dp", None),
    )
    return jax.shard_map(
        body,
        mesh=mesh,
        in_specs=(images,) * 4 + weights + (images,),
        out_specs=(images, images) + weights,
        check_vma=False,
    )
```

```python
import functools

import jax
import jax.numpy as jnp
from jax import lax
from jax.experimental import pallas as pl
from jax.experimental.pallas import tpu as pltpu
from jax.sharding import PartitionSpec as P

HEADS = 6
HEAD_DIM = 64
D = 384
SEQ = 197
MB = 3
LANES = 128
EPSILON = 1e-06
HIGHEST = lax.Precision.HIGHEST
VMEM_BYTES = 24 * 1024 * 1024
bf16 = jnp.bfloat16
f32 = jnp.float32


def dot(a, b, ca=1, cb=0, precision=None):
    return lax.dot_general(
        a, b, (((ca,), (cb,)), ((), ())), precision=precision, preferred_element_type=f32
    )


def xor_pairs(n, k):
    return [(i, i ^ k) for i in range(n)]


def spread_of(values):
    centre = jnp.mean(values, axis=-1, keepdims=True)
    centered = values - centre
    spread = jnp.mean(centered * centered, axis=-1, keepdims=True)
    rate = lax.rsqrt(spread + EPSILON)
    return centered * rate, rate


def norm_back(grad_hat, hat, rate):
    mean_one = jnp.mean(grad_hat, axis=-1, keepdims=True)
    mean_two = jnp.mean(grad_hat * hat, axis=-1, keepdims=True)
    return rate * (grad_hat - mean_one - hat * mean_two)


def route_masks(index_ref, slot_ref, kept_ref, me, groups, capacity):
    index = index_ref[0, 0]
    target = jnp.where(kept_ref[0, 0] > 0, (index ^ me) * capacity + slot_ref[0, 0], -1)
    both = jnp.transpose(jnp.concatenate([index, target], axis=0).astype(f32)).astype(jnp.int32)
    index, target = both[:, :2], both[:, 2:]
    lanes = lax.broadcasted_iota(jnp.int32, (SEQ, groups * capacity), 1)
    places = [(lanes == target[:, k : k + 1]).astype(f32).astype(bf16) for k in range(2)]
    experts = lax.broadcasted_iota(jnp.int32, (SEQ, groups), 1)
    chosen = [(experts == index[:, k : k + 1]).astype(f32) for k in range(2)]
    return places, chosen


def half_mask(which):
    lanes = lax.broadcasted_iota(jnp.int32, (SEQ, LANES), 1)
    return (lanes < HEAD_DIM) if which == 0 else (lanes >= HEAD_DIM)


def forward_kernel(groups, capacity, me_ref, tokens_ref, index_ref, slot_ref, kept_ref, cot_ref, dense_ref, side_ref, packed_ref, attn_ref, attended_ref, middle_ref, router_ref, *sends):
    me = me_ref[0]
    side = side_ref[...]
    gain_one = side[groups : groups + 1]
    gain_two = side[groups + 1 : groups + 2]
    inputs = tokens_ref[0, 0].astype(f32)
    hat, _ = spread_of(inputs)
    normed_low = (hat * gain_one).astype(bf16)
    packed = dot(normed_low, dense_ref[:, : 3 * D]).astype(bf16)
    packed_ref[...] = packed
    scale = HEAD_DIM ** (-0.5)
    parts = []
    for pair in range(HEADS // 2):
        lo = pair * LANES
        query = packed[:, lo : lo + LANES]
        keyed = packed[:, D + lo : D + lo + LANES]
        valued = packed[:, 2 * D + lo : 2 * D + lo + LANES]
        outs = []
        for which in range(2):
            masked = jnp.where(half_mask(which), query, jnp.zeros_like(query))
            scores = dot(masked, keyed, 1, 1) * scale
            top = jnp.max(scores, axis=-1, keepdims=True)
            raised = jnp.exp(scores - top)
            total = jnp.sum(raised, axis=-1, keepdims=True)
            attn_low = (raised * (1.0 / total)).astype(bf16)
            attn_ref[2 * pair + which] = attn_low
            outs.append(dot(attn_low, valued))
        parts.append(jnp.where(half_mask(0), outs[0], outs[1]))
    attended = jnp.concatenate(parts, axis=1).astype(bf16)
    attended_ref[...] = attended
    middle = inputs + dot(attended, dense_ref[:, 3 * D : 4 * D])
    middle_ref[...] = middle
    hat_two, _ = spread_of(middle)
    normed_two = hat_two * gain_two
    logits = dot(normed_two, side[:groups], 1, 1, precision=HIGHEST)
    raised = jnp.exp(logits - jnp.max(logits, axis=-1, keepdims=True))
    router = raised / jnp.sum(raised, axis=-1, keepdims=True)
    router_ref[...] = router
    places, chosen = route_masks(index_ref, slot_ref, kept_ref, me, groups, capacity)
    cot = cot_ref[0, 0].astype(f32)
    inbox = dot(places[0] + places[1], normed_two.astype(bf16), 0, 0).astype(bf16)
    grad_outbox = jnp.zeros((groups * capacity, D), f32)
    for k in range(2):
        gate = jnp.sum(chosen[k] * router, axis=-1, keepdims=True)
        grad_outbox += dot(places[k], (gate * cot).astype(bf16), 0, 0)
    grad_outbox = grad_outbox.astype(bf16)
    for g in range(groups):
        sends[g][:capacity] = inbox[g * capacity : (g + 1) * capacity]
        sends[g][capacity:] = grad_outbox[g * capacity : (g + 1) * capacity]


def expert_kernel(groups, capacity, *refs):
    boxes = refs[:groups]
    first_ref, bias_ref, second_ref = refs[groups : groups + 3]
    backs = refs[groups + 3 : 2 * groups + 3]
    active_ref, grad_hidden_ref = refs[2 * groups + 3 :]
    inbox = jnp.concatenate([box[:capacity] for box in boxes], axis=0)
    grad_outbox = jnp.concatenate([box[capacity:] for box in boxes], axis=0)
    wide = first_ref.shape[1]
    step = wide // 3
    outbox = jnp.zeros((groups * capacity, D), f32)
    grad_inbox = jnp.zeros((groups * capacity, D), f32)
    for at in range(0, wide, step):
        first = first_ref[:, at : at + step]
        second = second_ref[at : at + step, :]
        hidden = dot(inbox, first) + bias_ref[:, at : at + step].astype(f32)
        cdf = 0.5 + 0.5 * lax.erf(hidden * (0.5**0.5))
        density = jnp.exp(hidden * hidden * (-0.5)) * 0.3989422804014327
        active = (hidden * cdf).astype(bf16)
        grad_active = dot(grad_outbox, second, 1, 1)
        grad_hidden = ((cdf + hidden * density) * grad_active).astype(bf16)
        active_ref[:, at : at + step] = active
        grad_hidden_ref[:, at : at + step] = grad_hidden
        outbox += dot(active, second)
        grad_inbox += dot(grad_hidden, first, 1, 1)
    outbox = outbox.astype(bf16)
    grad_inbox = grad_inbox.astype(bf16)
    for g in range(groups):
        backs[g][:capacity] = outbox[g * capacity : (g + 1) * capacity]
        backs[g][capacity:] = grad_inbox[g * capacity : (g + 1) * capacity]


def place(keep_ref, send_ref, at, value):
    @pl.when((at & 1) == 0)
    def _():
        keep_ref[at >> 1] = value

    @pl.when((at & 1) == 1)
    def _():
        send_ref[at >> 1] = value


def second_grad_kernel(groups, capacity, owners, me_ref, *refs):
    boxes = [refs[m * groups : (m + 1) * groups] for m in range(MB)]
    actives = refs[MB * groups : MB * groups + MB]
    keep_ref, send_ref = refs[-2:]
    rows = keep_ref.shape[1]
    grads = [
        jnp.concatenate([box[capacity:] for box in boxes[m]], axis=0) for m in range(MB)
    ]
    wide = owners * rows
    step = wide // 2
    for at in range(0, wide, step):
        total = dot(actives[0][:, at : at + step], grads[0], 0, 0)
        for m in range(1, MB):
            total += dot(actives[m][:, at : at + step], grads[m], 0, 0)
        for j in range(step // rows):
            part = total[j * rows : (j + 1) * rows].astype(bf16)
            place(keep_ref, send_ref, (at // rows + j) ^ me_ref[1], part)


def first_grad_kernel(groups, capacity, owners, me_ref, *refs):
    boxes = [refs[m * groups : (m + 1) * groups] for m in range(MB)]
    hiddens = refs[MB * groups : MB * groups + MB]
    keep_ref, send_ref = refs[-2:]
    rows = D // owners
    extra = keep_ref.shape[1] - rows
    inboxes = [
        jnp.concatenate([box[:capacity] for box in boxes[m]], axis=0) for m in range(MB)
    ]
    wide = keep_ref.shape[2]
    step = wide // 3
    totals, biases = [], []
    for at in range(0, wide, step):
        total = dot(inboxes[0], hiddens[0][:, at : at + step], 0, 0)
        bias = jnp.sum(hiddens[0][:, at : at + step].astype(f32), axis=0, keepdims=True)
        for m in range(1, MB):
            total += dot(inboxes[m], hiddens[m][:, at : at + step], 0, 0)
            bias += jnp.sum(hiddens[m][:, at : at + step].astype(f32), axis=0, keepdims=True)
        totals.append(total)
        biases.append(jnp.broadcast_to(bias, (extra, step)))
    for j in range(owners):
        part = jnp.concatenate(
            [
                jnp.concatenate([total[j * rows : (j + 1) * rows], bias], axis=0)
                for total, bias in zip(totals, biases)
            ],
            axis=1,
        )
        place(keep_ref, send_ref, j ^ me_ref[1], part.astype(bf16))


def backward_kernel(groups, capacity, has_total, last, me_ref, tokens_ref, index_ref, slot_ref, kept_ref, cot_ref, dense_ref, side_ref, packed_ref, attn_ref, attended_ref, middle_ref, router_ref, *refs):
    backs = refs[:groups]
    total_ref, side_total_ref = refs[groups : groups + 2] if has_total else (None, None)
    if last:
        output_ref, d_tokens_ref, keep_ref, send_ref = refs[-4:]
    else:
        output_ref, d_tokens_ref, grads_ref, side_grads_ref = refs[-4:]
    me = me_ref[0]
    side = side_ref[...]
    gain_one = side[groups : groups + 1]
    gain_two = side[groups + 1 : groups + 2]
    middle = middle_ref[...]
    router = router_ref[...]
    cot = cot_ref[0, 0].astype(f32)
    places, chosen = route_masks(index_ref, slot_ref, kept_ref, me, groups, capacity)
    outbox = jnp.concatenate([box[:capacity] for box in backs], axis=0)
    grad_inbox = jnp.concatenate([box[capacity:] for box in backs], axis=0)
    mixed = middle
    grad_router = jnp.zeros((SEQ, groups), f32)
    for k in range(2):
        picked = dot(places[k], outbox)
        gate = jnp.sum(chosen[k] * router, axis=-1, keepdims=True)
        mixed = mixed + gate * picked
        grad_router += chosen[k] * jnp.sum(cot * picked, axis=-1, keepdims=True)
    output_ref[0, 0] = mixed.astype(bf16)
    grad_logits = router * (grad_router - jnp.sum(router * grad_router, axis=-1, keepdims=True))
    grad_normed_two = dot(grad_logits, side[:groups], precision=HIGHEST) + dot(
        places[0] + places[1], grad_inbox
    )
    hat_two, rate_two = spread_of(middle)
    grad_middle = norm_back(grad_normed_two * gain_two, hat_two, rate_two) + cot
    lanes = lax.broadcasted_iota(jnp.int32, (SEQ, LANES), 1)
    logits_wide = sum(
        jnp.where(lanes == e, grad_logits[:, e : e + 1], 0.0) for e in range(groups)
    )
    lines = lax.broadcasted_iota(jnp.int32, (LANES, D), 0)
    side_grad = dot(logits_wide, hat_two * gain_two, 0, 0, precision=HIGHEST)
    two_grad = jnp.sum(grad_normed_two * hat_two, axis=0, keepdims=True)
    side_grad = jnp.where(lines == groups + 1, two_grad, side_grad)
    grad_branch = grad_middle.astype(bf16)
    out_grad = dot(attended_ref[...], grad_branch, 0, 0)
    grad_attended = dot(grad_branch, dense_ref[:, 3 * D : 4 * D], 1, 1).astype(bf16)
    scale = HEAD_DIM ** (-0.5)
    first_half = half_mask(0)
    queries, keys, values = [], [], []
    for pair in range(HEADS // 2):
        lo = pair * LANES
        query = packed_ref[:, lo : lo + LANES]
        keyed = packed_ref[:, D + lo : D + lo + LANES]
        valued = packed_ref[:, 2 * D + lo : 2 * D + lo + LANES]
        pulled = grad_attended[:, lo : lo + LANES]
        q_outs, k_outs, v_outs = [], [], []
        for which in range(2):
            attn_low = attn_ref[2 * pair + which]
            attn = attn_low.astype(f32)
            masked = jnp.where(half_mask(which), pulled, jnp.zeros_like(pulled))
            weighted = dot(masked, valued, 1, 1)
            inner = jnp.sum(attn * weighted, axis=-1, keepdims=True)
            grad_scores = (attn * (weighted - inner)).astype(bf16)
            v_outs.append(dot(attn_low, pulled, 0, 0))
            q_outs.append(dot(grad_scores, keyed))
            k_outs.append(dot(grad_scores, query, 0, 0))
        queries.append(jnp.where(first_half, q_outs[0], q_outs[1]) * scale)
        keys.append(jnp.where(first_half, k_outs[0], k_outs[1]) * scale)
        values.append(jnp.where(first_half, v_outs[0], v_outs[1]))
    grad_packed = jnp.concatenate(queries + keys + values, axis=1).astype(bf16)
    grad_normed = dot(grad_packed, dense_ref[:, : 3 * D], 1, 1)
    hat, rate = spread_of(tokens_ref[0, 0].astype(f32))
    packed_grad = dot((hat * gain_one).astype(bf16), grad_packed, 0, 0)
    one_grad = jnp.sum(grad_normed * hat, axis=0, keepdims=True)
    side_grad = jnp.where(lines == groups, one_grad, side_grad)
    d_tokens_ref[0, 0] = grad_middle + norm_back(grad_normed * gain_one, hat, rate)
    grads = [packed_grad, out_grad]
    if has_total:
        grads = [packed_grad + total_ref[:, : 3 * D], out_grad + total_ref[:, 3 * D :]]
        side_grad = side_grad + side_total_ref[...]
    if not last:
        grads_ref[:, : 3 * D] = grads[0]
        grads_ref[:, 3 * D :] = grads[1]
        side_grads_ref[...] = side_grad
    if last:
        joined = jnp.concatenate(grads + [jnp.transpose(side_grad)], axis=1).astype(bf16)
        left, right = split_halves(joined)
        core = me & 1
        rows = keep_ref.shape[1]
        for j in range(keep_ref.shape[0]):
            at = j ^ me_ref[1]
            cut = slice(j * rows, (j + 1) * rows)

            @pl.when(core == 0)
            def _(at=at, cut=cut):
                keep_ref[at] = left[cut]
                send_ref[at] = right[cut]

            @pl.when(core == 1)
            def _(at=at, cut=cut):
                keep_ref[at] = right[cut]
                send_ref[at] = left[cut]


def split_halves(joined):
    half = half_width(joined.shape[1])
    return joined[:, :half], joined[:, joined.shape[1] - half :]


def half_width(width):
    return -(-width // (2 * LANES)) * LANES


def join_halves(left, right, width):
    half = left.shape[1]
    return jnp.concatenate([left, right[:, 2 * half - width :]], axis=1)


def pack_kernel(me_ref, router_ref, one_ref, two_ref, bias_ref, qkv_hbm, out_hbm, first_hbm, second_hbm, half_ref, pack_ref, qkv_ref, out_ref, first_ref, second_ref, sems):
    copies = [
        pltpu.make_async_copy(source, target, sems.at[i])
        for i, (source, target) in enumerate(
            [
                (qkv_hbm, qkv_ref),
                (out_hbm, out_ref),
                (first_hbm, first_ref),
                (second_hbm, second_ref),
            ]
        )
    ]
    for copy in copies:
        copy.start()
    rows = qkv_ref.shape[0]
    lines = [router_ref[...].astype(f32), one_ref[...].astype(f32), two_ref[...].astype(f32)]
    used = sum(line.shape[0] for line in lines)
    lines.append(jnp.zeros((LANES - used, rows), f32))
    side = jnp.transpose(jnp.concatenate(lines, axis=0)).astype(bf16)
    copies[0].wait()
    copies[1].wait()
    joined = jnp.concatenate([qkv_ref[...], out_ref[...], side], axis=1)
    left, right = split_halves(joined)

    @pl.when((me_ref[0] & 1) == 0)
    def _():
        half_ref[...] = left

    @pl.when((me_ref[0] & 1) == 1)
    def _():
        half_ref[...] = right

    tall = second_ref.shape[1]
    fold = D // tall
    at_row = lax.broadcasted_iota(jnp.int32, (tall, D), 0)
    at_lane = lax.broadcasted_iota(jnp.int32, (tall, D), 1)
    line_at = lax.broadcasted_iota(jnp.int32, (16, D), 0)
    lines = jnp.zeros((16, D), f32)
    for r in range(fold):
        spots = (at_lane == at_row + r * tall).astype(f32).astype(bf16)
        lines = jnp.where(line_at == r, dot(bias_ref[...], spots), lines)
    pack_ref[2 * tall :] = lines.astype(bf16)
    copies[2].wait()
    copies[3].wait()
    pack_ref[:tall] = second_ref[0]
    for c in range(first_ref.shape[2] // D):
        pack_ref[tall + c * rows : tall + (c + 1) * rows] = first_ref[0, :, c * D : (c + 1) * D]


def arrange_kernel(count, me_ref, *refs):
    out_ref = refs[-1]
    for k in range(count):
        out_ref[me_ref[1] ^ k] = refs[k][...]


def join_kernel(me_ref, mine_ref, other_ref, out_ref, side_ref):
    def write(left, right):
        joined = join_halves(left, right, 4 * D + LANES)
        out_ref[...] = joined[:, : 4 * D]
        side_ref[...] = jnp.transpose(joined[:, 4 * D :].astype(f32))

    @pl.when((me_ref[0] & 1) == 0)
    def _():
        write(mine_ref[...], other_ref[...])

    @pl.when((me_ref[0] & 1) == 1)
    def _():
        write(other_ref[...], mine_ref[...])


def unpack_kernel(count, me_ref, *refs):
    first_ref, second_ref, bias_ref, table = refs[count:]
    rows = first_ref.shape[1]
    tall = second_ref.shape[1]
    for k in range(count):
        at = me_ref[1] ^ k
        second_ref[at] = refs[k][:tall]
        for c in range(first_ref.shape[2] // D):
            first_ref[at, :, c * D : (c + 1) * D] = refs[k][tall + c * rows : tall + (c + 1) * rows]
        table[at] = refs[k][2 * tall :]
    fold = D // tall
    for i in range(count // fold):
        line = table[fold * i][:1].astype(f32)
        for r in range(1, fold):
            line += table[fold * i + r][r : r + 1].astype(f32)
        bias_ref[:, i * D : (i + 1) * D] = line


def merge_kernel(keep_ref, got_ref, own_ref, *sends):
    for k in range(keep_ref.shape[0]):
        total = keep_ref[k].astype(f32) + got_ref[k].astype(f32)
        if k == 0:
            own_ref[...] = total
        else:
            sends[k - 1][...] = total.astype(bf16)


def deal_kernel(keep_ref, got_ref, own_ref, send_ref):
    for k in range(keep_ref.shape[0]):
        total = (keep_ref[k].astype(f32) + got_ref[k].astype(f32)).astype(bf16)
        if k % 2 == 0:
            own_ref[k // 2] = total
        else:
            send_ref[k // 2] = total


def total_kernel(own_ref, *refs):
    total = own_ref[...].astype(f32)
    for ref in refs[:-1]:
        total += ref[...].astype(f32)
    refs[-1][...] = total.astype(refs[-1].dtype).reshape(refs[-1].shape)


def finish_kernel(groups, me_ref, *refs):
    terms, (qkv_ref, out_ref, router_ref, one_ref, two_ref) = refs[:-5], refs[-5:]
    mine = sum(ref[...].astype(f32) for ref in terms[0::2])
    other = sum(ref[...].astype(f32) for ref in terms[1::2])

    def write(left, right):
        joined = join_halves(left, right, 4 * D + LANES)
        qkv_ref[...] = joined[:, : 3 * D]
        out_ref[...] = joined[:, 3 * D : 4 * D]
        side = jnp.transpose(joined[:, 4 * D :])
        router_ref[...] = side[:groups]
        one_ref[...] = side[groups : groups + 1]
        two_ref[...] = side[groups + 1 : groups + 2]

    @pl.when((me_ref[0] & 1) == 0)
    def _():
        write(mine, other)

    @pl.when((me_ref[0] & 1) == 1)
    def _():
        write(other, mine)


def first_total_kernel(*refs):
    rows = refs[-2].shape[1]
    total = sum(ref[...].astype(f32) for ref in refs[:-2])
    refs[-2][0] = total[:rows]
    refs[-1][...] = total[rows:]


def whole(shape):
    zeros = (0,) * len(shape)
    return pl.BlockSpec(tuple(shape), lambda i: zeros)


def of_batch(shape, batch):
    tail = (0,) * (len(shape) - 1)
    return pl.BlockSpec((1,) + tuple(shape[1:]), lambda i: (batch,) + tail)


SCALAR = pl.BlockSpec(memory_space=pltpu.SMEM)
FAR = pltpu.HBM


def call(kernel, name, outs, args, us, in_specs=None, scratch=(), out_specs=None, aliases=None, vmem=VMEM_BYTES):
    if in_specs is None:
        in_specs = [SCALAR if a.dtype == jnp.int32 else whole(a.shape) for a in args]
    moved = sum(a.size * a.dtype.itemsize for a in args)
    moved += sum(a.size * a.dtype.itemsize for a in outs)
    return pl.pallas_call(
        kernel,
        grid=(1,),
        in_specs=in_specs,
        out_specs=out_specs or [whole(o.shape) for o in outs],
        input_output_aliases=aliases or {},
        out_shape=outs,
        scratch_shapes=list(scratch),
        compiler_params=pltpu.CompilerParams(vmem_limit_bytes=vmem),
        cost_estimate=pl.CostEstimate(flops=int(us * 1e+09), bytes_accessed=moved, transcendentals=0),
        name=name,
    )(*args)


def like(shape, dtype):
    return jax.ShapeDtypeStruct(tuple(shape), dtype)


def send(value, axis, k):
    return lax.ppermute(value, axis, xor_pairs(lax.axis_size(axis), k))


def after(value, *earlier):
    return lax.optimization_barrier((value,) + earlier)[0]


def sum_rest(keep, got, axis):
    shape = keep.shape[1:]
    count = keep.shape[0]
    merged = call(
        merge_kernel,
        "merge",
        [like(shape, f32)] + [like(shape, bf16)] * (count - 1),
        [keep, got],
        2,
    )
    return [merged[0]] + [send(merged[k], axis, 2 * k) for k in reversed(range(1, count))]


def deal(keep, got, us=2):
    shape = (keep.shape[0] // 2,) + keep.shape[1:]
    return call(deal_kernel, "deal", [like(shape, bf16)] * 2, [keep, got], us)


def body(
    tokens,
    expert_index,
    expert_slot,
    route_kept,
    ln1_gain,
    w_qkv,
    w_out,
    ln2_gain,
    w_router,
    expert_in,
    expert_bias,
    expert_out,
    cotangent,
):
    groups = lax.axis_size("expert")
    owners = lax.axis_size("dp")
    capacity = 8 * (5 * SEQ // (16 * groups) + 1)
    slots = groups * capacity
    wide = expert_in.shape[2]
    rows = w_qkv.shape[0]
    tall = expert_out.shape[1]
    dense_width = 4 * D + LANES
    half = half_width(dense_width)
    me = jnp.stack([lax.axis_index("expert"), lax.axis_index("dp")]).astype(jnp.int32)
    far_args = [w_qkv, w_out, expert_in, expert_out]
    near_args = [me, w_router.T, ln1_gain[None], ln2_gain[None], expert_bias]
    own_half, own_pack = call(
        pack_kernel,
        "pack",
        [like((rows, half), bf16), like((2 * tall + 16, D), bf16)],
        near_args + far_args,
        2,
        in_specs=[SCALAR]
        + [whole(a.shape) for a in near_args[1:]]
        + [pl.BlockSpec(memory_space=FAR)] * len(far_args),
        scratch=[pltpu.VMEM(a.shape, a.dtype) for a in far_args]
        + [pltpu.SemaphoreType.DMA((len(far_args),))],
        vmem=60 * 1024 * 1024,
    )
    far = sorted(range(2, owners, 2), reverse=True)
    halves = [own_half] + [None] * (owners - 1)
    for k in far:
        halves[k] = send(own_half, "dp", k)
    halves[1] = send(own_half, "dp", 1)
    for k in far:
        halves[k + 1] = send(halves[k], "dp", 1)
    packs = [own_pack] + [None] * (owners - 1)
    packs[1] = send(own_pack, "dp", 1)
    own_late = after(own_pack, *[halves[k] for k in far])
    direct = [k for k in far if k == 2 or k >= 4 and k % 4 == 0]
    for k in direct:
        packs[k] = send(own_late, "dp", k)
    mine = call(
        functools.partial(arrange_kernel, owners),
        "arrange",
        [like((owners, rows, half), bf16)],
        [after(me, packs[1])] + halves,
        2,
    )[0].reshape(D, half)
    other = send(mine, "expert", 1)
    dense, side = call(
        join_kernel, "join", [like((D, 4 * D), bf16), like((LANES, D), f32)], [me, mine, other], 2
    )

    routes = [
        after(jnp.swapaxes(a, 2, 3), halves[far[0]])
        for a in (expert_index, expert_slot, route_kept)
    ]
    state = []
    boxes = []
    for m in range(MB):
        shared = [tokens] + routes + [cotangent]
        ready = after(dense, packs[direct[0]], *boxes[0]) if m == MB - 1 else dense
        ready = after(dense, state[0][4]) if m == 1 else ready
        outs = call(
            functools.partial(forward_kernel, groups, capacity),
            "forward",
            [
                like((SEQ, 3 * D), bf16),
                like((HEADS, SEQ, SEQ), bf16),
                like((SEQ, D), bf16),
                like((SEQ, D), f32),
                like((SEQ, groups), f32),
            ]
            + [like((2 * capacity, D), bf16)] * groups,
            [me] + shared + [ready, side],
            4,
            in_specs=[SCALAR] + [of_batch(a.shape, m) for a in shared] + [whole(dense.shape), whole(side.shape)],
        )
        state.append(outs[:5])
        sends = outs[5:]
        boxes.append(
            [sends[0]] + [send(sends[k], "expert", k) for k in reversed(range(1, groups))][::-1]
        )
    for k in direct:
        late = after(packs[k], state[1][4])
        if k + 2 < owners and k >= 4:
            packs[k + 2] = send(late, "dp", 2)
        packs[k + 1] = send(late, "dp", 1)
    for k in far:
        if k not in direct:
            packs[k + 1] = send(after(packs[k], state[2][4]), "dp", 1)
    first, second, bias = call(
        functools.partial(unpack_kernel, owners),
        "unpack",
        [
            like((owners, rows, wide), bf16),
            like((owners, tall, D), bf16),
            like((1, wide), f32),
        ],
        [after(me, *boxes[1])] + packs,
        4,
        scratch=[pltpu.VMEM((owners, 16, D), bf16)],
    )
    first = first.reshape(D, wide)
    second = second.reshape(wide, D)

    actives, hiddens, returned = [], [], []
    for m in range(MB):
        outs = call(
            functools.partial(expert_kernel, groups, capacity),
            "experts",
            [like((2 * capacity, D), bf16)] * groups + [like((slots, wide), bf16)] * 2,
            list(boxes[m]) + [first, after(bias, hiddens[m - 1]) if m else bias, second],
            5,
        )
        actives.append(outs[groups])
        hiddens.append(outs[groups + 1])
        returned.append(
            [outs[0]] + [send(outs[k], "expert", k) for k in reversed(range(1, groups))][::-1]
        )
    all_boxes = [box for m in range(MB) for box in boxes[m]]
    second_keep, second_send = call(
        functools.partial(second_grad_kernel, groups, capacity, owners),
        "second_grad",
        [like((owners // 2, tall, D), bf16)] * 2,
        [me] + all_boxes + actives,
        5,
    )
    second_got = send(second_send, "dp", 1)
    first_keep, first_send = call(
        functools.partial(first_grad_kernel, groups, capacity, owners),
        "first_grad",
        [like((owners // 2, rows + 8, wide), bf16)] * 2,
        [after(me, second_send, *returned[0])] + all_boxes + hiddens,
        5,
    )

    first_got = send(first_send, "dp", 1)
    output = token_grads = total = None
    gates_to = [[first_send], [], []]
    for m in range(MB):
        last = m == MB - 1
        shared = [tokens] + routes + [cotangent]
        dense_late = after(dense, *gates_to[m]) if gates_to[m] else dense
        rest = [dense_late, side] + list(state[m]) + list(returned[m])
        rest += [] if m == 0 else [total, side_total]
        carried = [] if m == 0 else [output, token_grads]
        at = 1 + len(shared) + len(rest)
        outs = call(
            functools.partial(backward_kernel, groups, capacity, m > 0, last),
            "backward",
            [like(tokens.shape, bf16), like(tokens.shape, f32)]
            + (
                [like((owners, rows, half), bf16)] * 2
                if last
                else [like((D, 4 * D), f32), like((LANES, D), f32)]
            ),
            [me] + shared + rest + carried,
            7,
            in_specs=[SCALAR]
            + [of_batch(a.shape, m) for a in shared]
            + [whole(a.shape) for a in rest]
            + [pl.BlockSpec(memory_space=pl.ANY)] * len(carried),
            out_specs=[of_batch(tokens.shape, m)] * 2
            + [whole((owners, rows, half))] * 2 * last
            + [whole((D, 4 * D)), whole((LANES, D))] * (not last),
            aliases={} if m == 0 else {at: 0, at + 1: 1},
        )
        output, token_grads, total, side_total = outs
        if m == MB - 2:
            second_keep, second_send = deal(second_keep, after(second_got, total))
            gates_to[m + 1] = [second_send]
        dense_send = outs[-1]
    second_got = send(second_send, "dp", 2)
    keep, share = deal(after(total, first_got), send(dense_send, "expert", 1))
    dense_got = send(share, "dp", 1)
    second_stage, first_stage = [second_keep, second_got], [first_keep, after(first_got, share)]
    first_keep, first_send = deal(*first_stage)
    bit = 2
    first_stage = [first_keep, send(first_send, "dp", bit)]
    dense_terms = sum_rest(keep, dense_got, "dp")
    while bit * 2 < owners:
        second_keep, second_send = deal(second_stage[0], after(second_stage[1], first_send), 1)
        second_stage = [second_keep, send(second_send, "dp", 2 * bit)]
        first_keep, first_send = deal(first_stage[0], after(first_stage[1], dense_terms[0]), 1)
        bit *= 2
        first_stage = [first_keep, send(first_send, "dp", bit)]
    dense_terms[0] = after(dense_terms[0], first_send)
    reduced = call(total_kernel, "total", [like((rows, half), bf16)], dense_terms, 1)[0]
    spread = [reduced] + [send(reduced, "expert", k) for k in range(1, groups)]
    d_qkv, d_out, d_router, d_one, d_two = call(
        functools.partial(finish_kernel, groups),
        "finish",
        [
            like((rows, 3 * D), f32),
            like((rows, D), f32),
            like((groups, rows), f32),
            like((1, rows), f32),
            like((1, rows), f32),
        ],
        [me] + spread,
        1,
    )
    d_second = call(
        total_kernel, "total", [like((1, tall, D), f32)], [a[0] for a in second_stage], 1
    )[0]
    d_first, d_biases = call(
        first_total_kernel,
        "total",
        [like((1, rows, wide), f32), like((8, wide), f32)],
        [a[0] for a in first_stage],
        1,
    )
    d_bias = lax.dynamic_slice(d_biases, (0, me[1] * tall), (1, tall))
    return (
        output,
        token_grads,
        d_one[0],
        d_qkv,
        d_out,
        d_two[0],
        d_router.T,
        d_first,
        d_bias,
        d_second,
    )


def solution(mesh):
    images = P(None, ("dp", "expert"), None, None)
    weights = (
        P("dp"),
        P("dp", None),
        P("dp", None),
        P("dp"),
        P("dp", None),
        P("expert", "dp", None),
        P("expert", "dp"),
        P("expert", "dp", None),
    )
    return jax.shard_map(
        body,
        mesh=mesh,
        in_specs=(images,) * 4 + weights + (images,),
        out_specs=(images, images) + weights,
        check_vma=False,
    )
```

```python
import functools

import jax
import jax.numpy as jnp
from jax import lax
from jax.experimental import pallas as pl
from jax.experimental.pallas import tpu as pltpu
from jax.sharding import PartitionSpec as P

HEADS = 6
HEAD_DIM = 64
D = 384
SEQ = 197
MB = 3
LANES = 128
EPSILON = 1e-06
HIGHEST = lax.Precision.HIGHEST
VMEM_BYTES = 24 * 1024 * 1024
bf16 = jnp.bfloat16
f32 = jnp.float32


def dot(a, b, ca=1, cb=0, precision=None):
    return lax.dot_general(
        a, b, (((ca,), (cb,)), ((), ())), precision=precision, preferred_element_type=f32
    )


def xor_pairs(n, k):
    return [(i, i ^ k) for i in range(n)]


def spread_of(values):
    centre = jnp.mean(values, axis=-1, keepdims=True)
    centered = values - centre
    spread = jnp.mean(centered * centered, axis=-1, keepdims=True)
    rate = lax.rsqrt(spread + EPSILON)
    return centered * rate, rate


def norm_back(grad_hat, hat, rate):
    mean_one = jnp.mean(grad_hat, axis=-1, keepdims=True)
    mean_two = jnp.mean(grad_hat * hat, axis=-1, keepdims=True)
    return rate * (grad_hat - mean_one - hat * mean_two)


def route_masks(index_ref, slot_ref, kept_ref, me, groups, capacity):
    index = index_ref[0, 0]
    target = jnp.where(kept_ref[0, 0] > 0, (index ^ me) * capacity + slot_ref[0, 0], -1)
    both = jnp.transpose(jnp.concatenate([index, target], axis=0).astype(f32)).astype(jnp.int32)
    index, target = both[:, :2], both[:, 2:]
    lanes = lax.broadcasted_iota(jnp.int32, (SEQ, groups * capacity), 1)
    places = [(lanes == target[:, k : k + 1]).astype(f32).astype(bf16) for k in range(2)]
    experts = lax.broadcasted_iota(jnp.int32, (SEQ, groups), 1)
    chosen = [(experts == index[:, k : k + 1]).astype(f32) for k in range(2)]
    return places, chosen


def half_mask(which):
    lanes = lax.broadcasted_iota(jnp.int32, (SEQ, LANES), 1)
    return (lanes < HEAD_DIM) if which == 0 else (lanes >= HEAD_DIM)


def forward_kernel(groups, capacity, me_ref, tokens_ref, index_ref, slot_ref, kept_ref, cot_ref, dense_ref, side_ref, packed_ref, attn_ref, attended_ref, middle_ref, router_ref, *sends):
    me = me_ref[0]
    side = side_ref[...]
    gain_one = side[groups : groups + 1]
    gain_two = side[groups + 1 : groups + 2]
    inputs = tokens_ref[0, 0].astype(f32)
    hat, _ = spread_of(inputs)
    normed_low = (hat * gain_one).astype(bf16)
    packed = dot(normed_low, dense_ref[:, : 3 * D]).astype(bf16)
    packed_ref[...] = packed
    scale = HEAD_DIM ** (-0.5)
    parts = []
    for pair in range(HEADS // 2):
        lo = pair * LANES
        query = packed[:, lo : lo + LANES]
        keyed = packed[:, D + lo : D + lo + LANES]
        valued = packed[:, 2 * D + lo : 2 * D + lo + LANES]
        outs = []
        for which in range(2):
            masked = jnp.where(half_mask(which), query, jnp.zeros_like(query))
            scores = dot(masked, keyed, 1, 1) * scale
            top = jnp.max(scores, axis=-1, keepdims=True)
            raised = jnp.exp(scores - top)
            total = jnp.sum(raised, axis=-1, keepdims=True)
            attn_low = (raised * (1.0 / total)).astype(bf16)
            attn_ref[2 * pair + which] = attn_low
            outs.append(dot(attn_low, valued))
        parts.append(jnp.where(half_mask(0), outs[0], outs[1]))
    attended = jnp.concatenate(parts, axis=1).astype(bf16)
    attended_ref[...] = attended
    middle = inputs + dot(attended, dense_ref[:, 3 * D : 4 * D])
    middle_ref[...] = middle
    hat_two, _ = spread_of(middle)
    normed_two = hat_two * gain_two
    logits = dot(normed_two, side[:groups], 1, 1, precision=HIGHEST)
    raised = jnp.exp(logits - jnp.max(logits, axis=-1, keepdims=True))
    router = raised / jnp.sum(raised, axis=-1, keepdims=True)
    router_ref[...] = router
    places, chosen = route_masks(index_ref, slot_ref, kept_ref, me, groups, capacity)
    cot = cot_ref[0, 0].astype(f32)
    inbox = dot(places[0] + places[1], normed_two.astype(bf16), 0, 0).astype(bf16)
    grad_outbox = jnp.zeros((groups * capacity, D), f32)
    for k in range(2):
        gate = jnp.sum(chosen[k] * router, axis=-1, keepdims=True)
        grad_outbox += dot(places[k], (gate * cot).astype(bf16), 0, 0)
    grad_outbox = grad_outbox.astype(bf16)
    for g in range(groups):
        sends[g][:capacity] = inbox[g * capacity : (g + 1) * capacity]
        sends[g][capacity:] = grad_outbox[g * capacity : (g + 1) * capacity]


def expert_kernel(groups, capacity, *refs):
    boxes = refs[:groups]
    first_ref, bias_ref, second_ref = refs[groups : groups + 3]
    backs = refs[groups + 3 : 2 * groups + 3]
    active_ref, grad_hidden_ref = refs[2 * groups + 3 :]
    inbox = jnp.concatenate([box[:capacity] for box in boxes], axis=0)
    grad_outbox = jnp.concatenate([box[capacity:] for box in boxes], axis=0)
    wide = first_ref.shape[1]
    step = wide // 3
    outbox = jnp.zeros((groups * capacity, D), f32)
    grad_inbox = jnp.zeros((groups * capacity, D), f32)
    for at in range(0, wide, step):
        first = first_ref[:, at : at + step]
        second = second_ref[at : at + step, :]
        hidden = dot(inbox, first) + bias_ref[:, at : at + step].astype(f32)
        cdf = 0.5 + 0.5 * lax.erf(hidden * (0.5**0.5))
        density = jnp.exp(hidden * hidden * (-0.5)) * 0.3989422804014327
        active = (hidden * cdf).astype(bf16)
        grad_active = dot(grad_outbox, second, 1, 1)
        grad_hidden = ((cdf + hidden * density) * grad_active).astype(bf16)
        active_ref[:, at : at + step] = active
        grad_hidden_ref[:, at : at + step] = grad_hidden
        outbox += dot(active, second)
        grad_inbox += dot(grad_hidden, first, 1, 1)
    outbox = outbox.astype(bf16)
    grad_inbox = grad_inbox.astype(bf16)
    for g in range(groups):
        backs[g][:capacity] = outbox[g * capacity : (g + 1) * capacity]
        backs[g][capacity:] = grad_inbox[g * capacity : (g + 1) * capacity]


def place(keep_ref, send_ref, at, value):
    @pl.when((at & 1) == 0)
    def _():
        keep_ref[at >> 1] = value

    @pl.when((at & 1) == 1)
    def _():
        send_ref[at >> 1] = value


def second_grad_kernel(groups, capacity, owners, me_ref, *refs):
    boxes = [refs[m * groups : (m + 1) * groups] for m in range(MB)]
    actives = refs[MB * groups : MB * groups + MB]
    keep_ref, send_ref = refs[-2:]
    rows = keep_ref.shape[1]
    grads = [
        jnp.concatenate([box[capacity:] for box in boxes[m]], axis=0) for m in range(MB)
    ]
    wide = owners * rows
    step = wide // 2
    for at in range(0, wide, step):
        total = dot(actives[0][:, at : at + step], grads[0], 0, 0)
        for m in range(1, MB):
            total += dot(actives[m][:, at : at + step], grads[m], 0, 0)
        for j in range(step // rows):
            part = total[j * rows : (j + 1) * rows].astype(bf16)
            place(keep_ref, send_ref, (at // rows + j) ^ me_ref[1], part)


def first_grad_kernel(groups, capacity, owners, me_ref, *refs):
    boxes = [refs[m * groups : (m + 1) * groups] for m in range(MB)]
    hiddens = refs[MB * groups : MB * groups + MB]
    keep_ref, send_ref = refs[-2:]
    rows = D // owners
    extra = keep_ref.shape[1] - rows
    inboxes = [
        jnp.concatenate([box[:capacity] for box in boxes[m]], axis=0) for m in range(MB)
    ]
    wide = keep_ref.shape[2]
    step = wide // 3
    totals, biases = [], []
    for at in range(0, wide, step):
        total = dot(inboxes[0], hiddens[0][:, at : at + step], 0, 0)
        bias = jnp.sum(hiddens[0][:, at : at + step].astype(f32), axis=0, keepdims=True)
        for m in range(1, MB):
            total += dot(inboxes[m], hiddens[m][:, at : at + step], 0, 0)
            bias += jnp.sum(hiddens[m][:, at : at + step].astype(f32), axis=0, keepdims=True)
        totals.append(total)
        biases.append(jnp.broadcast_to(bias, (extra, step)))
    for j in range(owners):
        part = jnp.concatenate(
            [
                jnp.concatenate([total[j * rows : (j + 1) * rows], bias], axis=0)
                for total, bias in zip(totals, biases)
            ],
            axis=1,
        )
        place(keep_ref, send_ref, j ^ me_ref[1], part.astype(bf16))


def backward_kernel(groups, capacity, has_total, last, me_ref, tokens_ref, index_ref, slot_ref, kept_ref, cot_ref, dense_ref, side_ref, packed_ref, attn_ref, attended_ref, middle_ref, router_ref, *refs):
    backs = refs[:groups]
    total_ref, side_total_ref = refs[groups : groups + 2] if has_total else (None, None)
    if last:
        output_ref, d_tokens_ref, keep_ref, send_ref = refs[-4:]
    else:
        output_ref, d_tokens_ref, grads_ref, side_grads_ref = refs[-4:]
    me = me_ref[0]
    side = side_ref[...]
    gain_one = side[groups : groups + 1]
    gain_two = side[groups + 1 : groups + 2]
    middle = middle_ref[...]
    router = router_ref[...]
    cot = cot_ref[0, 0].astype(f32)
    places, chosen = route_masks(index_ref, slot_ref, kept_ref, me, groups, capacity)
    outbox = jnp.concatenate([box[:capacity] for box in backs], axis=0)
    grad_inbox = jnp.concatenate([box[capacity:] for box in backs], axis=0)
    mixed = middle
    grad_router = jnp.zeros((SEQ, groups), f32)
    for k in range(2):
        picked = dot(places[k], outbox)
        gate = jnp.sum(chosen[k] * router, axis=-1, keepdims=True)
        mixed = mixed + gate * picked
        grad_router += chosen[k] * jnp.sum(cot * picked, axis=-1, keepdims=True)
    output_ref[0, 0] = mixed.astype(bf16)
    grad_logits = router * (grad_router - jnp.sum(router * grad_router, axis=-1, keepdims=True))
    grad_normed_two = dot(grad_logits, side[:groups], precision=HIGHEST) + dot(
        places[0] + places[1], grad_inbox
    )
    hat_two, rate_two = spread_of(middle)
    grad_middle = norm_back(grad_normed_two * gain_two, hat_two, rate_two) + cot
    lanes = lax.broadcasted_iota(jnp.int32, (SEQ, LANES), 1)
    logits_wide = sum(
        jnp.where(lanes == e, grad_logits[:, e : e + 1], 0.0) for e in range(groups)
    )
    lines = lax.broadcasted_iota(jnp.int32, (LANES, D), 0)
    side_grad = dot(logits_wide, hat_two * gain_two, 0, 0, precision=HIGHEST)
    two_grad = jnp.sum(grad_normed_two * hat_two, axis=0, keepdims=True)
    side_grad = jnp.where(lines == groups + 1, two_grad, side_grad)
    grad_branch = grad_middle.astype(bf16)
    out_grad = dot(attended_ref[...], grad_branch, 0, 0)
    grad_attended = dot(grad_branch, dense_ref[:, 3 * D : 4 * D], 1, 1).astype(bf16)
    scale = HEAD_DIM ** (-0.5)
    first_half = half_mask(0)
    queries, keys, values = [], [], []
    for pair in range(HEADS // 2):
        lo = pair * LANES
        query = packed_ref[:, lo : lo + LANES]
        keyed = packed_ref[:, D + lo : D + lo + LANES]
        valued = packed_ref[:, 2 * D + lo : 2 * D + lo + LANES]
        pulled = grad_attended[:, lo : lo + LANES]
        q_outs, k_outs, v_outs = [], [], []
        for which in range(2):
            attn_low = attn_ref[2 * pair + which]
            attn = attn_low.astype(f32)
            masked = jnp.where(half_mask(which), pulled, jnp.zeros_like(pulled))
            weighted = dot(masked, valued, 1, 1)
            inner = jnp.sum(attn * weighted, axis=-1, keepdims=True)
            grad_scores = (attn * (weighted - inner)).astype(bf16)
            v_outs.append(dot(attn_low, pulled, 0, 0))
            q_outs.append(dot(grad_scores, keyed))
            k_outs.append(dot(grad_scores, query, 0, 0))
        queries.append(jnp.where(first_half, q_outs[0], q_outs[1]) * scale)
        keys.append(jnp.where(first_half, k_outs[0], k_outs[1]) * scale)
        values.append(jnp.where(first_half, v_outs[0], v_outs[1]))
    grad_packed = jnp.concatenate(queries + keys + values, axis=1).astype(bf16)
    grad_normed = dot(grad_packed, dense_ref[:, : 3 * D], 1, 1)
    hat, rate = spread_of(tokens_ref[0, 0].astype(f32))
    packed_grad = dot((hat * gain_one).astype(bf16), grad_packed, 0, 0)
    one_grad = jnp.sum(grad_normed * hat, axis=0, keepdims=True)
    side_grad = jnp.where(lines == groups, one_grad, side_grad)
    d_tokens_ref[0, 0] = grad_middle + norm_back(grad_normed * gain_one, hat, rate)
    grads = [packed_grad, out_grad]
    if has_total:
        grads = [packed_grad + total_ref[:, : 3 * D], out_grad + total_ref[:, 3 * D :]]
        side_grad = side_grad + side_total_ref[...]
    if not last:
        grads_ref[:, : 3 * D] = grads[0]
        grads_ref[:, 3 * D :] = grads[1]
        side_grads_ref[...] = side_grad
    if last:
        joined = jnp.concatenate(grads + [jnp.transpose(side_grad)], axis=1).astype(bf16)
        left, right = split_halves(joined)
        core = me & 1
        rows = keep_ref.shape[1]
        for j in range(keep_ref.shape[0]):
            at = j ^ me_ref[1]
            cut = slice(j * rows, (j + 1) * rows)

            @pl.when(core == 0)
            def _(at=at, cut=cut):
                keep_ref[at] = left[cut]
                send_ref[at] = right[cut]

            @pl.when(core == 1)
            def _(at=at, cut=cut):
                keep_ref[at] = right[cut]
                send_ref[at] = left[cut]


def split_halves(joined):
    half = half_width(joined.shape[1])
    return joined[:, :half], joined[:, joined.shape[1] - half :]


def half_width(width):
    return -(-width // (2 * LANES)) * LANES


def join_halves(left, right, width):
    half = left.shape[1]
    return jnp.concatenate([left, right[:, 2 * half - width :]], axis=1)


def pack_kernel(me_ref, router_ref, one_ref, two_ref, bias_ref, qkv_hbm, out_hbm, first_hbm, second_hbm, half_ref, pack_ref, qkv_ref, out_ref, first_ref, second_ref, sems):
    copies = [
        pltpu.make_async_copy(source, target, sems.at[i])
        for i, (source, target) in enumerate(
            [
                (qkv_hbm, qkv_ref),
                (out_hbm, out_ref),
                (first_hbm, first_ref),
                (second_hbm, second_ref),
            ]
        )
    ]
    for copy in copies:
        copy.start()
    rows = qkv_ref.shape[0]
    lines = [router_ref[...].astype(f32), one_ref[...].astype(f32), two_ref[...].astype(f32)]
    used = sum(line.shape[0] for line in lines)
    lines.append(jnp.zeros((LANES - used, rows), f32))
    side = jnp.transpose(jnp.concatenate(lines, axis=0)).astype(bf16)
    copies[0].wait()
    copies[1].wait()
    joined = jnp.concatenate([qkv_ref[...], out_ref[...], side], axis=1)
    left, right = split_halves(joined)

    @pl.when((me_ref[0] & 1) == 0)
    def _():
        half_ref[...] = left

    @pl.when((me_ref[0] & 1) == 1)
    def _():
        half_ref[...] = right

    tall = second_ref.shape[1]
    fold = D // tall
    at_row = lax.broadcasted_iota(jnp.int32, (tall, D), 0)
    at_lane = lax.broadcasted_iota(jnp.int32, (tall, D), 1)
    line_at = lax.broadcasted_iota(jnp.int32, (16, D), 0)
    lines = jnp.zeros((16, D), f32)
    for r in range(fold):
        spots = (at_lane == at_row + r * tall).astype(f32).astype(bf16)
        lines = jnp.where(line_at == r, dot(bias_ref[...], spots), lines)
    pack_ref[2 * tall :] = lines.astype(bf16)
    copies[2].wait()
    copies[3].wait()
    pack_ref[:tall] = second_ref[0]
    for c in range(first_ref.shape[2] // D):
        pack_ref[tall + c * rows : tall + (c + 1) * rows] = first_ref[0, :, c * D : (c + 1) * D]


def arrange_kernel(count, me_ref, *refs):
    out_ref = refs[-1]
    for k in range(count):
        out_ref[me_ref[1] ^ k] = refs[k][...]


def join_kernel(me_ref, mine_ref, other_ref, out_ref, side_ref):
    def write(left, right):
        joined = join_halves(left, right, 4 * D + LANES)
        out_ref[...] = joined[:, : 4 * D]
        side_ref[...] = jnp.transpose(joined[:, 4 * D :].astype(f32))

    @pl.when((me_ref[0] & 1) == 0)
    def _():
        write(mine_ref[...], other_ref[...])

    @pl.when((me_ref[0] & 1) == 1)
    def _():
        write(other_ref[...], mine_ref[...])


def unpack_kernel(count, me_ref, *refs):
    first_ref, second_ref, bias_ref, table = refs[count:]
    rows = first_ref.shape[1]
    tall = second_ref.shape[1]
    for k in range(count):
        at = me_ref[1] ^ k
        second_ref[at] = refs[k][:tall]
        for c in range(first_ref.shape[2] // D):
            first_ref[at, :, c * D : (c + 1) * D] = refs[k][tall + c * rows : tall + (c + 1) * rows]
        table[at] = refs[k][2 * tall :]
    fold = D // tall
    for i in range(count // fold):
        line = table[fold * i][:1].astype(f32)
        for r in range(1, fold):
            line += table[fold * i + r][r : r + 1].astype(f32)
        bias_ref[:, i * D : (i + 1) * D] = line


def merge_kernel(keep_ref, got_ref, own_ref, *sends):
    for k in range(keep_ref.shape[0]):
        total = keep_ref[k].astype(f32) + got_ref[k].astype(f32)
        if k == 0:
            own_ref[...] = total
        else:
            sends[k - 1][...] = total.astype(bf16)


def deal_kernel(keep_ref, got_ref, own_ref, send_ref):
    for k in range(keep_ref.shape[0]):
        total = (keep_ref[k].astype(f32) + got_ref[k].astype(f32)).astype(bf16)
        if k % 2 == 0:
            own_ref[k // 2] = total
        else:
            send_ref[k // 2] = total


def total_kernel(own_ref, *refs):
    total = own_ref[...].astype(f32)
    for ref in refs[:-1]:
        total += ref[...].astype(f32)
    refs[-1][...] = total.astype(refs[-1].dtype).reshape(refs[-1].shape)


def finish_kernel(groups, me_ref, *refs):
    terms, (qkv_ref, out_ref, router_ref, one_ref, two_ref) = refs[:-5], refs[-5:]
    mine = sum(ref[...].astype(f32) for ref in terms[0::2])
    other = sum(ref[...].astype(f32) for ref in terms[1::2])

    def write(left, right):
        joined = join_halves(left, right, 4 * D + LANES)
        qkv_ref[...] = joined[:, : 3 * D]
        out_ref[...] = joined[:, 3 * D : 4 * D]
        side = jnp.transpose(joined[:, 4 * D :])
        router_ref[...] = side[:groups]
        one_ref[...] = side[groups : groups + 1]
        two_ref[...] = side[groups + 1 : groups + 2]

    @pl.when((me_ref[0] & 1) == 0)
    def _():
        write(mine, other)

    @pl.when((me_ref[0] & 1) == 1)
    def _():
        write(other, mine)


def first_total_kernel(*refs):
    rows = refs[-2].shape[1]
    total = sum(ref[...].astype(f32) for ref in refs[:-2])
    refs[-2][0] = total[:rows]
    refs[-1][...] = total[rows:]


def whole(shape):
    zeros = (0,) * len(shape)
    return pl.BlockSpec(tuple(shape), lambda i: zeros)


def of_batch(shape, batch):
    tail = (0,) * (len(shape) - 1)
    return pl.BlockSpec((1,) + tuple(shape[1:]), lambda i: (batch,) + tail)


SCALAR = pl.BlockSpec(memory_space=pltpu.SMEM)
FAR = pltpu.HBM


def call(kernel, name, outs, args, us, in_specs=None, scratch=(), out_specs=None, aliases=None, vmem=VMEM_BYTES):
    if in_specs is None:
        in_specs = [SCALAR if a.dtype == jnp.int32 else whole(a.shape) for a in args]
    moved = sum(a.size * a.dtype.itemsize for a in args)
    moved += sum(a.size * a.dtype.itemsize for a in outs)
    return pl.pallas_call(
        kernel,
        grid=(1,),
        in_specs=in_specs,
        out_specs=out_specs or [whole(o.shape) for o in outs],
        input_output_aliases=aliases or {},
        out_shape=outs,
        scratch_shapes=list(scratch),
        compiler_params=pltpu.CompilerParams(vmem_limit_bytes=vmem),
        cost_estimate=pl.CostEstimate(flops=int(us * 1e+09), bytes_accessed=moved, transcendentals=0),
        name=name,
    )(*args)


def like(shape, dtype):
    return jax.ShapeDtypeStruct(tuple(shape), dtype)


def send(value, axis, k):
    return lax.ppermute(value, axis, xor_pairs(lax.axis_size(axis), k))


def after(value, *earlier):
    return lax.optimization_barrier((value,) + earlier)[0]


def sum_rest(keep, got, axis):
    shape = keep.shape[1:]
    count = keep.shape[0]
    merged = call(
        merge_kernel,
        "merge",
        [like(shape, f32)] + [like(shape, bf16)] * (count - 1),
        [keep, got],
        2,
    )
    return [merged[0]] + [send(merged[k], axis, 2 * k) for k in reversed(range(1, count))]


def deal(keep, got, us=2):
    shape = (keep.shape[0] // 2,) + keep.shape[1:]
    return call(deal_kernel, "deal", [like(shape, bf16)] * 2, [keep, got], us)


def body(
    tokens,
    expert_index,
    expert_slot,
    route_kept,
    ln1_gain,
    w_qkv,
    w_out,
    ln2_gain,
    w_router,
    expert_in,
    expert_bias,
    expert_out,
    cotangent,
):
    groups = lax.axis_size("expert")
    owners = lax.axis_size("dp")
    capacity = 8 * (5 * SEQ // (16 * groups) + 1)
    slots = groups * capacity
    wide = expert_in.shape[2]
    rows = w_qkv.shape[0]
    tall = expert_out.shape[1]
    dense_width = 4 * D + LANES
    half = half_width(dense_width)
    me = jnp.stack([lax.axis_index("expert"), lax.axis_index("dp")]).astype(jnp.int32)
    far_args = [w_qkv, w_out, expert_in, expert_out]
    core = lax.axis_index("expert").astype(jnp.int32).reshape(1)
    near_args = [core, w_router.T, ln1_gain[None], ln2_gain[None], expert_bias]
    own_half, own_pack = call(
        pack_kernel,
        "pack",
        [like((rows, half), bf16), like((2 * tall + 16, D), bf16)],
        near_args + far_args,
        2,
        in_specs=[SCALAR]
        + [whole(a.shape) for a in near_args[1:]]
        + [pl.BlockSpec(memory_space=FAR)] * len(far_args),
        scratch=[pltpu.VMEM(a.shape, a.dtype) for a in far_args]
        + [pltpu.SemaphoreType.DMA((len(far_args),))],
        vmem=60 * 1024 * 1024,
    )
    far = sorted(range(2, owners, 2), reverse=True)
    halves = [own_half] + [None] * (owners - 1)
    for k in far:
        halves[k] = send(own_half, "dp", k)
    halves[1] = send(own_half, "dp", 1)
    for k in far:
        halves[k + 1] = send(halves[k], "dp", 1)
    packs = [own_pack] + [None] * (owners - 1)
    packs[1] = send(own_pack, "dp", 1)
    own_late = after(own_pack, *[halves[k] for k in far])
    direct = [k for k in far if k == 2 or k >= 4 and k % 4 == 0]
    for k in direct:
        packs[k] = send(own_late, "dp", k)
    mine = call(
        functools.partial(arrange_kernel, owners),
        "arrange",
        [like((owners, rows, half), bf16)],
        [after(me, packs[1])] + halves,
        2,
    )[0].reshape(D, half)
    other = send(mine, "expert", 1)
    dense, side = call(
        join_kernel, "join", [like((D, 4 * D), bf16), like((LANES, D), f32)], [me, mine, other], 2
    )

    routes = [
        after(jnp.swapaxes(a, 2, 3), halves[far[0]])
        for a in (expert_index, expert_slot, route_kept)
    ]
    state = []
    boxes = []
    for m in range(MB):
        shared = [tokens] + routes + [cotangent]
        ready = after(dense, packs[direct[0]], *boxes[0]) if m == MB - 1 else dense
        ready = after(dense, state[0][4]) if m == 1 else ready
        outs = call(
            functools.partial(forward_kernel, groups, capacity),
            "forward",
            [
                like((SEQ, 3 * D), bf16),
                like((HEADS, SEQ, SEQ), bf16),
                like((SEQ, D), bf16),
                like((SEQ, D), f32),
                like((SEQ, groups), f32),
            ]
            + [like((2 * capacity, D), bf16)] * groups,
            [me] + shared + [ready, side],
            4,
            in_specs=[SCALAR] + [of_batch(a.shape, m) for a in shared] + [whole(dense.shape), whole(side.shape)],
        )
        state.append(outs[:5])
        sends = outs[5:]
        boxes.append(
            [sends[0]] + [send(sends[k], "expert", k) for k in reversed(range(1, groups))][::-1]
        )
    for k in direct:
        late = after(packs[k], state[1][4])
        if k + 2 < owners and k >= 4:
            packs[k + 2] = send(late, "dp", 2)
        packs[k + 1] = send(late, "dp", 1)
    for k in far:
        if k not in direct:
            packs[k + 1] = send(after(packs[k], state[2][4]), "dp", 1)
    first, second, bias = call(
        functools.partial(unpack_kernel, owners),
        "unpack",
        [
            like((owners, rows, wide), bf16),
            like((owners, tall, D), bf16),
            like((1, wide), f32),
        ],
        [after(me, *boxes[1])] + packs,
        4,
        scratch=[pltpu.VMEM((owners, 16, D), bf16)],
    )
    first = first.reshape(D, wide)
    second = second.reshape(wide, D)

    actives, hiddens, returned = [], [], []
    for m in range(MB):
        outs = call(
            functools.partial(expert_kernel, groups, capacity),
            "experts",
            [like((2 * capacity, D), bf16)] * groups + [like((slots, wide), bf16)] * 2,
            list(boxes[m]) + [first, after(bias, hiddens[m - 1]) if m else bias, second],
            5,
        )
        actives.append(outs[groups])
        hiddens.append(outs[groups + 1])
        returned.append(
            [outs[0]] + [send(outs[k], "expert", k) for k in reversed(range(1, groups))][::-1]
        )
    all_boxes = [box for m in range(MB) for box in boxes[m]]
    second_keep, second_send = call(
        functools.partial(second_grad_kernel, groups, capacity, owners),
        "second_grad",
        [like((owners // 2, tall, D), bf16)] * 2,
        [me] + all_boxes + actives,
        5,
    )
    second_got = send(second_send, "dp", 1)
    first_keep, first_send = call(
        functools.partial(first_grad_kernel, groups, capacity, owners),
        "first_grad",
        [like((owners // 2, rows + 8, wide), bf16)] * 2,
        [after(me, second_send, *returned[0])] + all_boxes + hiddens,
        5,
    )

    first_got = send(first_send, "dp", 1)
    output = token_grads = total = None
    gates_to = [[first_send], [], []]
    for m in range(MB):
        last = m == MB - 1
        shared = [tokens] + routes + [cotangent]
        dense_late = after(dense, *gates_to[m]) if gates_to[m] else dense
        rest = [dense_late, side] + list(state[m]) + list(returned[m])
        rest += [] if m == 0 else [total, side_total]
        carried = [] if m == 0 else [output, token_grads]
        at = 1 + len(shared) + len(rest)
        outs = call(
            functools.partial(backward_kernel, groups, capacity, m > 0, last),
            "backward",
            [like(tokens.shape, bf16), like(tokens.shape, f32)]
            + (
                [like((owners, rows, half), bf16)] * 2
                if last
                else [like((D, 4 * D), f32), like((LANES, D), f32)]
            ),
            [me] + shared + rest + carried,
            7,
            in_specs=[SCALAR]
            + [of_batch(a.shape, m) for a in shared]
            + [whole(a.shape) for a in rest]
            + [pl.BlockSpec(memory_space=pl.ANY)] * len(carried),
            out_specs=[of_batch(tokens.shape, m)] * 2
            + [whole((owners, rows, half))] * 2 * last
            + [whole((D, 4 * D)), whole((LANES, D))] * (not last),
            aliases={} if m == 0 else {at: 0, at + 1: 1},
        )
        output, token_grads, total, side_total = outs
        if m == MB - 2:
            second_keep, second_send = deal(second_keep, after(second_got, total))
            gates_to[m + 1] = [second_send]
        dense_send = outs[-1]
    second_got = send(second_send, "dp", 2)
    keep, share = deal(after(total, first_got), send(dense_send, "expert", 1))
    dense_got = send(share, "dp", 1)
    second_stage, first_stage = [second_keep, second_got], [first_keep, after(first_got, share)]
    first_keep, first_send = deal(*first_stage)
    bit = 2
    first_stage = [first_keep, send(first_send, "dp", bit)]
    dense_terms = sum_rest(keep, dense_got, "dp")
    while bit * 2 < owners:
        second_keep, second_send = deal(second_stage[0], after(second_stage[1], first_send), 1)
        second_stage = [second_keep, send(second_send, "dp", 2 * bit)]
        first_keep, first_send = deal(first_stage[0], after(first_stage[1], dense_terms[0]), 1)
        bit *= 2
        first_stage = [first_keep, send(first_send, "dp", bit)]
    dense_terms[0] = after(dense_terms[0], first_send)
    reduced = call(total_kernel, "total", [like((rows, half), bf16)], dense_terms, 1)[0]
    spread = [reduced] + [send(reduced, "expert", k) for k in range(1, groups)]
    d_qkv, d_out, d_router, d_one, d_two = call(
        functools.partial(finish_kernel, groups),
        "finish",
        [
            like((rows, 3 * D), f32),
            like((rows, D), f32),
            like((groups, rows), f32),
            like((1, rows), f32),
            like((1, rows), f32),
        ],
        [me] + spread,
        1,
    )
    d_second = call(
        total_kernel, "total", [like((1, tall, D), f32)], [a[0] for a in second_stage], 1
    )[0]
    d_first, d_biases = call(
        first_total_kernel,
        "total",
        [like((1, rows, wide), f32), like((8, wide), f32)],
        [a[0] for a in first_stage],
        1,
    )
    d_bias = lax.dynamic_slice(d_biases, (0, me[1] * tall), (1, tall))
    return (
        output,
        token_grads,
        d_one[0],
        d_qkv,
        d_out,
        d_two[0],
        d_router.T,
        d_first,
        d_bias,
        d_second,
    )


def solution(mesh):
    images = P(None, ("dp", "expert"), None, None)
    weights = (
        P("dp"),
        P("dp", None),
        P("dp", None),
        P("dp"),
        P("dp", None),
        P("expert", "dp", None),
        P("expert", "dp"),
        P("expert", "dp", None),
    )
    return jax.shard_map(
        body,
        mesh=mesh,
        in_specs=(images,) * 4 + weights + (images,),
        out_specs=(images, images) + weights,
        check_vma=False,
    )
```

```python
import functools

import jax
import jax.numpy as jnp
from jax import lax
from jax.experimental import pallas as pl
from jax.experimental.pallas import tpu as pltpu
from jax.sharding import PartitionSpec as P

HEADS = 6
HEAD_DIM = 64
D = 384
SEQ = 197
MB = 3
LANES = 128
EPSILON = 1e-06
HIGHEST = lax.Precision.HIGHEST
VMEM_BYTES = 24 * 1024 * 1024
bf16 = jnp.bfloat16
f32 = jnp.float32


def dot(a, b, ca=1, cb=0, precision=None):
    return lax.dot_general(
        a, b, (((ca,), (cb,)), ((), ())), precision=precision, preferred_element_type=f32
    )


def xor_pairs(n, k):
    return [(i, i ^ k) for i in range(n)]


def spread_of(values):
    centre = jnp.mean(values, axis=-1, keepdims=True)
    centered = values - centre
    spread = jnp.mean(centered * centered, axis=-1, keepdims=True)
    rate = lax.rsqrt(spread + EPSILON)
    return centered * rate, rate


def norm_back(grad_hat, hat, rate):
    mean_one = jnp.mean(grad_hat, axis=-1, keepdims=True)
    mean_two = jnp.mean(grad_hat * hat, axis=-1, keepdims=True)
    return rate * (grad_hat - mean_one - hat * mean_two)


def route_masks(index_ref, slot_ref, kept_ref, me, groups, capacity):
    index = index_ref[0, 0]
    target = jnp.where(kept_ref[0, 0] > 0, (index ^ me) * capacity + slot_ref[0, 0], -1)
    both = jnp.transpose(jnp.concatenate([index, target], axis=0).astype(f32)).astype(jnp.int32)
    index, target = both[:, :2], both[:, 2:]
    lanes = lax.broadcasted_iota(jnp.int32, (SEQ, groups * capacity), 1)
    places = [(lanes == target[:, k : k + 1]).astype(f32).astype(bf16) for k in range(2)]
    experts = lax.broadcasted_iota(jnp.int32, (SEQ, groups), 1)
    chosen = [(experts == index[:, k : k + 1]).astype(f32) for k in range(2)]
    return places, chosen


def half_mask(which):
    lanes = lax.broadcasted_iota(jnp.int32, (SEQ, LANES), 1)
    return (lanes < HEAD_DIM) if which == 0 else (lanes >= HEAD_DIM)


def forward_kernel(groups, capacity, me_ref, tokens_ref, index_ref, slot_ref, kept_ref, cot_ref, dense_ref, side_ref, packed_ref, attn_ref, attended_ref, middle_ref, router_ref, *sends):
    me = me_ref[0]
    side = side_ref[...]
    gain_one = side[groups : groups + 1]
    gain_two = side[groups + 1 : groups + 2]
    inputs = tokens_ref[0, 0].astype(f32)
    hat, _ = spread_of(inputs)
    normed_low = (hat * gain_one).astype(bf16)
    packed = dot(normed_low, dense_ref[:, : 3 * D]).astype(bf16)
    packed_ref[...] = packed
    scale = HEAD_DIM ** (-0.5)
    parts = []
    for pair in range(HEADS // 2):
        lo = pair * LANES
        query = packed[:, lo : lo + LANES]
        keyed = packed[:, D + lo : D + lo + LANES]
        valued = packed[:, 2 * D + lo : 2 * D + lo + LANES]
        outs = []
        for which in range(2):
            masked = jnp.where(half_mask(which), query, jnp.zeros_like(query))
            scores = dot(masked, keyed, 1, 1) * scale
            top = jnp.max(scores, axis=-1, keepdims=True)
            raised = jnp.exp(scores - top)
            total = jnp.sum(raised, axis=-1, keepdims=True)
            attn_low = (raised * (1.0 / total)).astype(bf16)
            attn_ref[2 * pair + which] = attn_low
            outs.append(dot(attn_low, valued))
        parts.append(jnp.where(half_mask(0), outs[0], outs[1]))
    attended = jnp.concatenate(parts, axis=1).astype(bf16)
    attended_ref[...] = attended
    middle = inputs + dot(attended, dense_ref[:, 3 * D : 4 * D])
    middle_ref[...] = middle
    hat_two, _ = spread_of(middle)
    normed_two = hat_two * gain_two
    logits = dot(normed_two, side[:groups], 1, 1, precision=HIGHEST)
    raised = jnp.exp(logits - jnp.max(logits, axis=-1, keepdims=True))
    router = raised / jnp.sum(raised, axis=-1, keepdims=True)
    router_ref[...] = router
    places, chosen = route_masks(index_ref, slot_ref, kept_ref, me, groups, capacity)
    cot = cot_ref[0, 0].astype(f32)
    inbox = dot(places[0] + places[1], normed_two.astype(bf16), 0, 0).astype(bf16)
    grad_outbox = jnp.zeros((groups * capacity, D), f32)
    for k in range(2):
        gate = jnp.sum(chosen[k] * router, axis=-1, keepdims=True)
        grad_outbox += dot(places[k], (gate * cot).astype(bf16), 0, 0)
    grad_outbox = grad_outbox.astype(bf16)
    for g in range(groups):
        sends[g][:capacity] = inbox[g * capacity : (g + 1) * capacity]
        sends[g][capacity:] = grad_outbox[g * capacity : (g + 1) * capacity]


def expert_kernel(groups, capacity, *refs):
    boxes = refs[:groups]
    first_ref, bias_ref, second_ref = refs[groups : groups + 3]
    backs = refs[groups + 3 : 2 * groups + 3]
    active_ref, grad_hidden_ref = refs[2 * groups + 3 :]
    inbox = jnp.concatenate([box[:capacity] for box in boxes], axis=0)
    grad_outbox = jnp.concatenate([box[capacity:] for box in boxes], axis=0)
    wide = first_ref.shape[1]
    step = wide // 2
    outbox = jnp.zeros((groups * capacity, D), f32)
    grad_inbox = jnp.zeros((groups * capacity, D), f32)
    for at in range(0, wide, step):
        first = first_ref[:, at : at + step]
        second = second_ref[at : at + step, :]
        hidden = dot(inbox, first) + bias_ref[:, at : at + step].astype(f32)
        cdf = 0.5 + 0.5 * lax.erf(hidden * (0.5**0.5))
        density = jnp.exp(hidden * hidden * (-0.5)) * 0.3989422804014327
        active = (hidden * cdf).astype(bf16)
        grad_active = dot(grad_outbox, second, 1, 1)
        grad_hidden = ((cdf + hidden * density) * grad_active).astype(bf16)
        active_ref[:, at : at + step] = active
        grad_hidden_ref[:, at : at + step] = grad_hidden
        outbox += dot(active, second)
        grad_inbox += dot(grad_hidden, first, 1, 1)
    outbox = outbox.astype(bf16)
    grad_inbox = grad_inbox.astype(bf16)
    for g in range(groups):
        backs[g][:capacity] = outbox[g * capacity : (g + 1) * capacity]
        backs[g][capacity:] = grad_inbox[g * capacity : (g + 1) * capacity]


def place(keep_ref, send_ref, at, value):
    @pl.when((at & 1) == 0)
    def _():
        keep_ref[at >> 1] = value

    @pl.when((at & 1) == 1)
    def _():
        send_ref[at >> 1] = value


def second_grad_kernel(groups, capacity, owners, me_ref, *refs):
    boxes = [refs[m * groups : (m + 1) * groups] for m in range(MB)]
    actives = refs[MB * groups : MB * groups + MB]
    keep_ref, send_ref = refs[-2:]
    rows = keep_ref.shape[1]
    grads = [
        jnp.concatenate([box[capacity:] for box in boxes[m]], axis=0) for m in range(MB)
    ]
    wide = owners * rows
    step = wide // 2
    for at in range(0, wide, step):
        total = dot(actives[0][:, at : at + step], grads[0], 0, 0)
        for m in range(1, MB):
            total += dot(actives[m][:, at : at + step], grads[m], 0, 0)
        for j in range(step // rows):
            part = total[j * rows : (j + 1) * rows].astype(bf16)
            place(keep_ref, send_ref, (at // rows + j) ^ me_ref[1], part)


def first_grad_kernel(groups, capacity, owners, me_ref, *refs):
    boxes = [refs[m * groups : (m + 1) * groups] for m in range(MB)]
    hiddens = refs[MB * groups : MB * groups + MB]
    keep_ref, send_ref = refs[-2:]
    rows = D // owners
    extra = keep_ref.shape[1] - rows
    inboxes = [
        jnp.concatenate([box[:capacity] for box in boxes[m]], axis=0) for m in range(MB)
    ]
    wide = keep_ref.shape[2]
    step = wide // 3
    totals, biases = [], []
    for at in range(0, wide, step):
        total = dot(inboxes[0], hiddens[0][:, at : at + step], 0, 0)
        bias = jnp.sum(hiddens[0][:, at : at + step].astype(f32), axis=0, keepdims=True)
        for m in range(1, MB):
            total += dot(inboxes[m], hiddens[m][:, at : at + step], 0, 0)
            bias += jnp.sum(hiddens[m][:, at : at + step].astype(f32), axis=0, keepdims=True)
        totals.append(total)
        biases.append(jnp.broadcast_to(bias, (extra, step)))
    for j in range(owners):
        part = jnp.concatenate(
            [
                jnp.concatenate([total[j * rows : (j + 1) * rows], bias], axis=0)
                for total, bias in zip(totals, biases)
            ],
            axis=1,
        )
        place(keep_ref, send_ref, j ^ me_ref[1], part.astype(bf16))


def backward_kernel(groups, capacity, has_total, last, me_ref, tokens_ref, index_ref, slot_ref, kept_ref, cot_ref, dense_ref, side_ref, packed_ref, attn_ref, attended_ref, middle_ref, router_ref, *refs):
    backs = refs[:groups]
    total_ref, side_total_ref = refs[groups : groups + 2] if has_total else (None, None)
    if last:
        output_ref, d_tokens_ref, keep_ref, send_ref = refs[-4:]
    else:
        output_ref, d_tokens_ref, grads_ref, side_grads_ref = refs[-4:]
    me = me_ref[0]
    side = side_ref[...]
    gain_one = side[groups : groups + 1]
    gain_two = side[groups + 1 : groups + 2]
    middle = middle_ref[...]
    router = router_ref[...]
    cot = cot_ref[0, 0].astype(f32)
    places, chosen = route_masks(index_ref, slot_ref, kept_ref, me, groups, capacity)
    outbox = jnp.concatenate([box[:capacity] for box in backs], axis=0)
    grad_inbox = jnp.concatenate([box[capacity:] for box in backs], axis=0)
    mixed = middle
    grad_router = jnp.zeros((SEQ, groups), f32)
    for k in range(2):
        picked = dot(places[k], outbox)
        gate = jnp.sum(chosen[k] * router, axis=-1, keepdims=True)
        mixed = mixed + gate * picked
        grad_router += chosen[k] * jnp.sum(cot * picked, axis=-1, keepdims=True)
    output_ref[0, 0] = mixed.astype(bf16)
    grad_logits = router * (grad_router - jnp.sum(router * grad_router, axis=-1, keepdims=True))
    grad_normed_two = dot(grad_logits, side[:groups], precision=HIGHEST) + dot(
        places[0] + places[1], grad_inbox
    )
    hat_two, rate_two = spread_of(middle)
    grad_middle = norm_back(grad_normed_two * gain_two, hat_two, rate_two) + cot
    lanes = lax.broadcasted_iota(jnp.int32, (SEQ, LANES), 1)
    logits_wide = sum(
        jnp.where(lanes == e, grad_logits[:, e : e + 1], 0.0) for e in range(groups)
    )
    lines = lax.broadcasted_iota(jnp.int32, (LANES, D), 0)
    side_grad = dot(logits_wide, hat_two * gain_two, 0, 0, precision=HIGHEST)
    two_grad = jnp.sum(grad_normed_two * hat_two, axis=0, keepdims=True)
    side_grad = jnp.where(lines == groups + 1, two_grad, side_grad)
    grad_branch = grad_middle.astype(bf16)
    out_grad = dot(attended_ref[...], grad_branch, 0, 0)
    grad_attended = dot(grad_branch, dense_ref[:, 3 * D : 4 * D], 1, 1).astype(bf16)
    scale = HEAD_DIM ** (-0.5)
    first_half = half_mask(0)
    queries, keys, values = [], [], []
    for pair in range(HEADS // 2):
        lo = pair * LANES
        query = packed_ref[:, lo : lo + LANES]
        keyed = packed_ref[:, D + lo : D + lo + LANES]
        valued = packed_ref[:, 2 * D + lo : 2 * D + lo + LANES]
        pulled = grad_attended[:, lo : lo + LANES]
        q_outs, k_outs, v_outs = [], [], []
        for which in range(2):
            attn_low = attn_ref[2 * pair + which]
            attn = attn_low.astype(f32)
            masked = jnp.where(half_mask(which), pulled, jnp.zeros_like(pulled))
            weighted = dot(masked, valued, 1, 1)
            inner = jnp.sum(attn * weighted, axis=-1, keepdims=True)
            grad_scores = (attn * (weighted - inner)).astype(bf16)
            v_outs.append(dot(attn_low, pulled, 0, 0))
            q_outs.append(dot(grad_scores, keyed))
            k_outs.append(dot(grad_scores, query, 0, 0))
        queries.append(jnp.where(first_half, q_outs[0], q_outs[1]) * scale)
        keys.append(jnp.where(first_half, k_outs[0], k_outs[1]) * scale)
        values.append(jnp.where(first_half, v_outs[0], v_outs[1]))
    grad_packed = jnp.concatenate(queries + keys + values, axis=1).astype(bf16)
    grad_normed = dot(grad_packed, dense_ref[:, : 3 * D], 1, 1)
    hat, rate = spread_of(tokens_ref[0, 0].astype(f32))
    packed_grad = dot((hat * gain_one).astype(bf16), grad_packed, 0, 0)
    one_grad = jnp.sum(grad_normed * hat, axis=0, keepdims=True)
    side_grad = jnp.where(lines == groups, one_grad, side_grad)
    d_tokens_ref[0, 0] = grad_middle + norm_back(grad_normed * gain_one, hat, rate)
    grads = [packed_grad, out_grad]
    if has_total:
        grads = [packed_grad + total_ref[:, : 3 * D], out_grad + total_ref[:, 3 * D :]]
        side_grad = side_grad + side_total_ref[...]
    if not last:
        grads_ref[:, : 3 * D] = grads[0]
        grads_ref[:, 3 * D :] = grads[1]
        side_grads_ref[...] = side_grad
    if last:
        joined = jnp.concatenate(grads + [jnp.transpose(side_grad)], axis=1).astype(bf16)
        left, right = split_halves(joined)
        core = me & 1
        rows = keep_ref.shape[1]
        for j in range(keep_ref.shape[0]):
            at = j ^ me_ref[1]
            cut = slice(j * rows, (j + 1) * rows)

            @pl.when(core == 0)
            def _(at=at, cut=cut):
                keep_ref[at] = left[cut]
                send_ref[at] = right[cut]

            @pl.when(core == 1)
            def _(at=at, cut=cut):
                keep_ref[at] = right[cut]
                send_ref[at] = left[cut]


def split_halves(joined):
    half = half_width(joined.shape[1])
    return joined[:, :half], joined[:, joined.shape[1] - half :]


def half_width(width):
    return -(-width // (2 * LANES)) * LANES


def join_halves(left, right, width):
    half = left.shape[1]
    return jnp.concatenate([left, right[:, 2 * half - width :]], axis=1)


def pack_kernel(me_ref, router_ref, one_ref, two_ref, bias_ref, qkv_hbm, out_hbm, first_hbm, second_hbm, half_ref, pack_ref, qkv_ref, out_ref, first_ref, second_ref, sems):
    copies = [
        pltpu.make_async_copy(source, target, sems.at[i])
        for i, (source, target) in enumerate(
            [
                (qkv_hbm, qkv_ref),
                (out_hbm, out_ref),
                (first_hbm, first_ref),
                (second_hbm, second_ref),
            ]
        )
    ]
    for copy in copies:
        copy.start()
    rows = qkv_ref.shape[0]
    lines = [router_ref[...].astype(f32), one_ref[...].astype(f32), two_ref[...].astype(f32)]
    used = sum(line.shape[0] for line in lines)
    lines.append(jnp.zeros((LANES - used, rows), f32))
    side = jnp.transpose(jnp.concatenate(lines, axis=0)).astype(bf16)
    copies[0].wait()
    copies[1].wait()
    joined = jnp.concatenate([qkv_ref[...], out_ref[...], side], axis=1)
    left, right = split_halves(joined)

    @pl.when((me_ref[0] & 1) == 0)
    def _():
        half_ref[...] = left

    @pl.when((me_ref[0] & 1) == 1)
    def _():
        half_ref[...] = right

    tall = second_ref.shape[1]
    fold = D // tall
    at_row = lax.broadcasted_iota(jnp.int32, (tall, D), 0)
    at_lane = lax.broadcasted_iota(jnp.int32, (tall, D), 1)
    line_at = lax.broadcasted_iota(jnp.int32, (16, D), 0)
    lines = jnp.zeros((16, D), f32)
    for r in range(fold):
        spots = (at_lane == at_row + r * tall).astype(f32).astype(bf16)
        lines = jnp.where(line_at == r, dot(bias_ref[...], spots), lines)
    pack_ref[2 * tall :] = lines.astype(bf16)
    copies[2].wait()
    copies[3].wait()
    pack_ref[:tall] = second_ref[0]
    for c in range(first_ref.shape[2] // D):
        pack_ref[tall + c * rows : tall + (c + 1) * rows] = first_ref[0, :, c * D : (c + 1) * D]


def arrange_kernel(count, me_ref, *refs):
    out_ref = refs[-1]
    for k in range(count):
        out_ref[me_ref[1] ^ k] = refs[k][...]


def join_kernel(me_ref, mine_ref, other_ref, out_ref, side_ref):
    def write(left, right):
        joined = join_halves(left, right, 4 * D + LANES)
        out_ref[...] = joined[:, : 4 * D]
        side_ref[...] = jnp.transpose(joined[:, 4 * D :].astype(f32))

    @pl.when((me_ref[0] & 1) == 0)
    def _():
        write(mine_ref[...], other_ref[...])

    @pl.when((me_ref[0] & 1) == 1)
    def _():
        write(other_ref[...], mine_ref[...])


def unpack_kernel(count, me_ref, *refs):
    first_ref, second_ref, bias_ref, table = refs[count:]
    rows = first_ref.shape[1]
    tall = second_ref.shape[1]
    for k in range(count):
        at = me_ref[1] ^ k
        second_ref[at] = refs[k][:tall]
        for c in range(first_ref.shape[2] // D):
            first_ref[at, :, c * D : (c + 1) * D] = refs[k][tall + c * rows : tall + (c + 1) * rows]
        table[at] = refs[k][2 * tall :]
    fold = D // tall
    for i in range(count // fold):
        line = table[fold * i][:1].astype(f32)
        for r in range(1, fold):
            line += table[fold * i + r][r : r + 1].astype(f32)
        bias_ref[:, i * D : (i + 1) * D] = line


def merge_kernel(keep_ref, got_ref, own_ref, *sends):
    for k in range(keep_ref.shape[0]):
        total = keep_ref[k].astype(f32) + got_ref[k].astype(f32)
        if k == 0:
            own_ref[...] = total
        else:
            sends[k - 1][...] = total.astype(bf16)


def deal_kernel(keep_ref, got_ref, own_ref, send_ref):
    for k in range(keep_ref.shape[0]):
        total = (keep_ref[k].astype(f32) + got_ref[k].astype(f32)).astype(bf16)
        if k % 2 == 0:
            own_ref[k // 2] = total
        else:
            send_ref[k // 2] = total


def total_kernel(own_ref, *refs):
    total = own_ref[...].astype(f32)
    for ref in refs[:-1]:
        total += ref[...].astype(f32)
    refs[-1][...] = total.astype(refs[-1].dtype).reshape(refs[-1].shape)


def finish_kernel(groups, me_ref, *refs):
    terms, (qkv_ref, out_ref, router_ref, one_ref, two_ref) = refs[:-5], refs[-5:]
    mine = sum(ref[...].astype(f32) for ref in terms[0::2])
    other = sum(ref[...].astype(f32) for ref in terms[1::2])

    def write(left, right):
        joined = join_halves(left, right, 4 * D + LANES)
        qkv_ref[...] = joined[:, : 3 * D]
        out_ref[...] = joined[:, 3 * D : 4 * D]
        side = jnp.transpose(joined[:, 4 * D :])
        router_ref[...] = side[:groups]
        one_ref[...] = side[groups : groups + 1]
        two_ref[...] = side[groups + 1 : groups + 2]

    @pl.when((me_ref[0] & 1) == 0)
    def _():
        write(mine, other)

    @pl.when((me_ref[0] & 1) == 1)
    def _():
        write(other, mine)


def first_total_kernel(*refs):
    rows = refs[-2].shape[1]
    total = sum(ref[...].astype(f32) for ref in refs[:-2])
    refs[-2][0] = total[:rows]
    refs[-1][...] = total[rows:]


def whole(shape):
    zeros = (0,) * len(shape)
    return pl.BlockSpec(tuple(shape), lambda i: zeros)


def of_batch(shape, batch):
    tail = (0,) * (len(shape) - 1)
    return pl.BlockSpec((1,) + tuple(shape[1:]), lambda i: (batch,) + tail)


SCALAR = pl.BlockSpec(memory_space=pltpu.SMEM)
FAR = pltpu.HBM


def call(kernel, name, outs, args, us, in_specs=None, scratch=(), out_specs=None, aliases=None, vmem=VMEM_BYTES):
    if in_specs is None:
        in_specs = [SCALAR if a.dtype == jnp.int32 else whole(a.shape) for a in args]
    moved = sum(a.size * a.dtype.itemsize for a in args)
    moved += sum(a.size * a.dtype.itemsize for a in outs)
    return pl.pallas_call(
        kernel,
        grid=(1,),
        in_specs=in_specs,
        out_specs=out_specs or [whole(o.shape) for o in outs],
        input_output_aliases=aliases or {},
        out_shape=outs,
        scratch_shapes=list(scratch),
        compiler_params=pltpu.CompilerParams(vmem_limit_bytes=vmem),
        cost_estimate=pl.CostEstimate(flops=int(us * 1e+09), bytes_accessed=moved, transcendentals=0),
        name=name,
    )(*args)


def like(shape, dtype):
    return jax.ShapeDtypeStruct(tuple(shape), dtype)


def send(value, axis, k):
    return lax.ppermute(value, axis, xor_pairs(lax.axis_size(axis), k))


def after(value, *earlier):
    return lax.optimization_barrier((value,) + earlier)[0]


def sum_rest(keep, got, axis):
    shape = keep.shape[1:]
    count = keep.shape[0]
    merged = call(
        merge_kernel,
        "merge",
        [like(shape, f32)] + [like(shape, bf16)] * (count - 1),
        [keep, got],
        2,
    )
    return [merged[0]] + [send(merged[k], axis, 2 * k) for k in reversed(range(1, count))]


def deal(keep, got, us=2):
    shape = (keep.shape[0] // 2,) + keep.shape[1:]
    return call(deal_kernel, "deal", [like(shape, bf16)] * 2, [keep, got], us)


def body(
    tokens,
    expert_index,
    expert_slot,
    route_kept,
    ln1_gain,
    w_qkv,
    w_out,
    ln2_gain,
    w_router,
    expert_in,
    expert_bias,
    expert_out,
    cotangent,
):
    groups = lax.axis_size("expert")
    owners = lax.axis_size("dp")
    capacity = 8 * (5 * SEQ // (16 * groups) + 1)
    slots = groups * capacity
    wide = expert_in.shape[2]
    rows = w_qkv.shape[0]
    tall = expert_out.shape[1]
    dense_width = 4 * D + LANES
    half = half_width(dense_width)
    me = jnp.stack([lax.axis_index("expert"), lax.axis_index("dp")]).astype(jnp.int32)
    far_args = [w_qkv, w_out, expert_in, expert_out]
    core = lax.axis_index("expert").astype(jnp.int32).reshape(1)
    near_args = [core, w_router.T, ln1_gain[None], ln2_gain[None], expert_bias]
    own_half, own_pack = call(
        pack_kernel,
        "pack",
        [like((rows, half), bf16), like((2 * tall + 16, D), bf16)],
        near_args + far_args,
        2,
        in_specs=[SCALAR]
        + [whole(a.shape) for a in near_args[1:]]
        + [pl.BlockSpec(memory_space=FAR)] * len(far_args),
        scratch=[pltpu.VMEM(a.shape, a.dtype) for a in far_args]
        + [pltpu.SemaphoreType.DMA((len(far_args),))],
        vmem=60 * 1024 * 1024,
    )
    far = sorted(range(2, owners, 2), reverse=True)
    halves = [own_half] + [None] * (owners - 1)
    for k in far:
        halves[k] = send(own_half, "dp", k)
    halves[1] = send(own_half, "dp", 1)
    for k in far:
        halves[k + 1] = send(halves[k], "dp", 1)
    packs = [own_pack] + [None] * (owners - 1)
    packs[1] = send(own_pack, "dp", 1)
    own_late = after(own_pack, *[halves[k] for k in far])
    direct = [k for k in far if k == 2 or k >= 4 and k % 4 == 0]
    for k in direct:
        packs[k] = send(own_late, "dp", k)
    mine = call(
        functools.partial(arrange_kernel, owners),
        "arrange",
        [like((owners, rows, half), bf16)],
        [after(me, packs[1])] + halves,
        2,
    )[0].reshape(D, half)
    other = send(mine, "expert", 1)
    dense, side = call(
        join_kernel, "join", [like((D, 4 * D), bf16), like((LANES, D), f32)], [me, mine, other], 2
    )

    routes = [
        after(jnp.swapaxes(a, 2, 3), halves[far[0]])
        for a in (expert_index, expert_slot, route_kept)
    ]
    state = []
    boxes = []
    for m in range(MB):
        shared = [tokens] + routes + [cotangent]
        ready = after(dense, packs[direct[0]], *boxes[0]) if m == MB - 1 else dense
        ready = after(dense, state[0][4]) if m == 1 else ready
        outs = call(
            functools.partial(forward_kernel, groups, capacity),
            "forward",
            [
                like((SEQ, 3 * D), bf16),
                like((HEADS, SEQ, SEQ), bf16),
                like((SEQ, D), bf16),
                like((SEQ, D), f32),
                like((SEQ, groups), f32),
            ]
            + [like((2 * capacity, D), bf16)] * groups,
            [me] + shared + [ready, side],
            4,
            in_specs=[SCALAR] + [of_batch(a.shape, m) for a in shared] + [whole(dense.shape), whole(side.shape)],
        )
        state.append(outs[:5])
        sends = outs[5:]
        boxes.append(
            [sends[0]] + [send(sends[k], "expert", k) for k in reversed(range(1, groups))][::-1]
        )
    for k in direct:
        late = after(packs[k], state[1][4])
        if k + 2 < owners and k >= 4:
            packs[k + 2] = send(late, "dp", 2)
        packs[k + 1] = send(late, "dp", 1)
    for k in far:
        if k not in direct:
            packs[k + 1] = send(after(packs[k], state[2][4]), "dp", 1)
    first, second, bias = call(
        functools.partial(unpack_kernel, owners),
        "unpack",
        [
            like((owners, rows, wide), bf16),
            like((owners, tall, D), bf16),
            like((1, wide), f32),
        ],
        [after(me, *boxes[1])] + packs,
        4,
        scratch=[pltpu.VMEM((owners, 16, D), bf16)],
    )
    first = first.reshape(D, wide)
    second = second.reshape(wide, D)

    actives, hiddens, returned = [], [], []
    for m in range(MB):
        outs = call(
            functools.partial(expert_kernel, groups, capacity),
            "experts",
            [like((2 * capacity, D), bf16)] * groups + [like((slots, wide), bf16)] * 2,
            list(boxes[m]) + [first, after(bias, hiddens[m - 1]) if m else bias, second],
            5,
        )
        actives.append(outs[groups])
        hiddens.append(outs[groups + 1])
        returned.append(
            [outs[0]] + [send(outs[k], "expert", k) for k in reversed(range(1, groups))][::-1]
        )
    all_boxes = [box for m in range(MB) for box in boxes[m]]
    second_keep, second_send = call(
        functools.partial(second_grad_kernel, groups, capacity, owners),
        "second_grad",
        [like((owners // 2, tall, D), bf16)] * 2,
        [me] + all_boxes + actives,
        5,
    )
    second_got = send(second_send, "dp", 1)
    first_keep, first_send = call(
        functools.partial(first_grad_kernel, groups, capacity, owners),
        "first_grad",
        [like((owners // 2, rows + 8, wide), bf16)] * 2,
        [after(me, second_send, *returned[0])] + all_boxes + hiddens,
        5,
    )

    first_got = send(first_send, "dp", 1)
    output = token_grads = total = None
    gates_to = [[first_send], [], []]
    for m in range(MB):
        last = m == MB - 1
        shared = [tokens] + routes + [cotangent]
        dense_late = after(dense, *gates_to[m]) if gates_to[m] else dense
        rest = [dense_late, side] + list(state[m]) + list(returned[m])
        rest += [] if m == 0 else [total, side_total]
        carried = [] if m == 0 else [output, token_grads]
        at = 1 + len(shared) + len(rest)
        outs = call(
            functools.partial(backward_kernel, groups, capacity, m > 0, last),
            "backward",
            [like(tokens.shape, bf16), like(tokens.shape, f32)]
            + (
                [like((owners, rows, half), bf16)] * 2
                if last
                else [like((D, 4 * D), f32), like((LANES, D), f32)]
            ),
            [me] + shared + rest + carried,
            7,
            in_specs=[SCALAR]
            + [of_batch(a.shape, m) for a in shared]
            + [whole(a.shape) for a in rest]
            + [pl.BlockSpec(memory_space=pl.ANY)] * len(carried),
            out_specs=[of_batch(tokens.shape, m)] * 2
            + [whole((owners, rows, half))] * 2 * last
            + [whole((D, 4 * D)), whole((LANES, D))] * (not last),
            aliases={} if m == 0 else {at: 0, at + 1: 1},
        )
        output, token_grads, total, side_total = outs
        if m == MB - 2:
            second_keep, second_send = deal(second_keep, after(second_got, total))
            gates_to[m + 1] = [second_send]
        dense_send = outs[-1]
    second_got = send(second_send, "dp", 2)
    keep, share = deal(after(total, first_got), send(dense_send, "expert", 1))
    dense_got = send(share, "dp", 1)
    second_stage, first_stage = [second_keep, second_got], [first_keep, after(first_got, share)]
    first_keep, first_send = deal(*first_stage)
    bit = 2
    first_stage = [first_keep, send(first_send, "dp", bit)]
    dense_terms = sum_rest(keep, dense_got, "dp")
    while bit * 2 < owners:
        second_keep, second_send = deal(second_stage[0], after(second_stage[1], first_send), 1)
        second_stage = [second_keep, send(second_send, "dp", 2 * bit)]
        first_keep, first_send = deal(first_stage[0], after(first_stage[1], dense_terms[0]), 1)
        bit *= 2
        first_stage = [first_keep, send(first_send, "dp", bit)]
    dense_terms[0] = after(dense_terms[0], first_send)
    reduced = call(total_kernel, "total", [like((rows, half), bf16)], dense_terms, 1)[0]
    spread = [reduced] + [send(reduced, "expert", k) for k in range(1, groups)]
    d_qkv, d_out, d_router, d_one, d_two = call(
        functools.partial(finish_kernel, groups),
        "finish",
        [
            like((rows, 3 * D), f32),
            like((rows, D), f32),
            like((groups, rows), f32),
            like((1, rows), f32),
            like((1, rows), f32),
        ],
        [me] + spread,
        1,
    )
    d_second = call(
        total_kernel, "total", [like((1, tall, D), f32)], [a[0] for a in second_stage], 1
    )[0]
    d_first, d_biases = call(
        first_total_kernel,
        "total",
        [like((1, rows, wide), f32), like((8, wide), f32)],
        [a[0] for a in first_stage],
        1,
    )
    d_bias = lax.dynamic_slice(d_biases, (0, me[1] * tall), (1, tall))
    return (
        output,
        token_grads,
        d_one[0],
        d_qkv,
        d_out,
        d_two[0],
        d_router.T,
        d_first,
        d_bias,
        d_second,
    )


def solution(mesh):
    images = P(None, ("dp", "expert"), None, None)
    weights = (
        P("dp"),
        P("dp", None),
        P("dp", None),
        P("dp"),
        P("dp", None),
        P("expert", "dp", None),
        P("expert", "dp"),
        P("expert", "dp", None),
    )
    return jax.shard_map(
        body,
        mesh=mesh,
        in_specs=(images,) * 4 + weights + (images,),
        out_specs=(images, images) + weights,
        check_vma=False,
    )
```
